512 devices in a mesh: dom: 128 (over z, x, core), rep: 4 (over y).
Axes of the slice: x: 4, y: 4, z: 16, core: 2. Of those that a mesh axis runs over, the one named last changes fastest.
Arguments:
- start_block: float32 [65536, 512], P(('dom', 'rep')), may hold values from -250 to 250
- restriction_maps: float32 [8, 8, 393216], P(None, None, ('dom', 'rep')), may hold values from -2 to 2
- send_rows: int32 [512, 64], P(('dom', 'rep')), may hold values from 0 to 767, as said below
- partner: int32 [393216], P(('dom', 'rep')), may hold values from 0 to 831, as said below
Outputs:
- basis: float32 [65536, 512], P(('dom', 'rep'))
- triangle: float32 [64, 64], replicated
The draws below stay inside these ranges and needn't reach their ends.
Inputs may be any that keep to these rules, and one draw needn't show every extreme that they name: `send_rows`: row p holds four groups of 16 slots, for ends sent to the partitions at dom index d + 1, d - 1 and rep index r + 1, r - 1 (cyclic in rep). Group k holds distinct local edge-end indices of p in its first c slots, c even and at most 16, and 0 in the rest; c is the same for a link seen from both sides. Partitions at the two ends of dom send nothing outward. In every draw some dom link and some rep link carry exactly 16 ends. `partner`: the pairing is mutual: a value below 768 names a local end whose entry names this end back; the end in slot s of group k of send_rows has the value 128 * 6 + o * 16 + s with o = 1, 0, 3, 2 for k = 0, 1, 2, 3, and the neighbour's end in slot s of its group o has the corresponding value pointing back.
All inputs are finite; a program needn't handle non-finite values.
Results may differ from the reference program's by a relative error of at most 0.0003.
Values sent between devices are 32-bit elements; how exact they have to be, the bound alone decides.
A program may use at most 64 MiB of HBM per device.

```python
import math
import jax
import jax.numpy as jnp
from jax import lax

STALK = 8
COLS = 64
DEG = 6
NODE_DEV = 128
BND = 16
NODES = 65536
N_DOM = 128
N_REP = 4


def draw_start_block(key, part):
    total = NODE_DEV * N_DOM * N_REP
    subkeys = jax.random.split(key, 3)
    node_scale = jnp.exp(jax.random.uniform(subkeys[1], (total, 1), jnp.float32) * jnp.log(10.0))
    column_scale = jnp.exp(jax.random.uniform(subkeys[2], (1, COLS), jnp.float32) * jnp.log(10.0))
    column_scale = jnp.tile(column_scale, (1, STALK))
    owner = (jnp.arange(total, dtype=jnp.int32) // NODE_DEV).astype(jnp.float32)
    rising = jnp.exp(jnp.log(3.0) * owner / max(N_DOM * N_REP - 1, 1))[:, None]
    base_draw = jnp.clip(jax.random.normal(subkeys[0], (total, STALK * COLS), jnp.float32), -6.0, 6.0)
    return jnp.clip(0.1 * base_draw * node_scale * column_scale * rising, -250.0, 250.0)


def build_graph(key):
    end_count = NODE_DEV * DEG
    parts_count = N_DOM * N_REP
    slot_count = BND
    key = jax.random.fold_in(key, 7)
    key_dom, key_rep, key_perm, key_fulld, key_fullr = jax.random.split(key, 5)
    dom_count = 2 * jax.random.randint(key_dom, (N_DOM, N_REP), slot_count // 8, slot_count // 2 + 1)
    rep_count = 2 * jax.random.randint(key_rep, (N_DOM, N_REP), slot_count // 8, slot_count // 2 + 1)
    full_dom = jax.random.randint(key_fulld, (), 0, (N_DOM - 1) * N_REP)
    full_rep = jax.random.randint(key_fullr, (), 0, N_DOM * N_REP)
    link_ids = jnp.arange(N_DOM * N_REP, dtype=jnp.int32).reshape(N_DOM, N_REP)
    dom_count = jnp.where(link_ids == full_dom, slot_count, dom_count)
    rep_count = jnp.where(link_ids == full_rep, slot_count, rep_count)
    dom_rows = jnp.arange(N_DOM, dtype=jnp.int32)[:, None]
    dom_count = jnp.where(dom_rows < N_DOM - 1, dom_count, 0)
    count_up = dom_count
    count_down = jnp.concatenate([jnp.zeros((1, N_REP), jnp.int32), dom_count[:-1]], 0)
    count_next = rep_count
    count_prev = jnp.roll(rep_count, 1, axis=1)
    counts = jnp.stack([count_up, count_down, count_next, count_prev], -1).reshape(parts_count, 4).astype(jnp.int32)
    perms = jax.vmap(lambda index: jax.random.permutation(jax.random.fold_in(key_perm, index), end_count))(jnp.arange(parts_count, dtype=jnp.int32)).astype(jnp.int32)
    positions = jnp.arange(end_count, dtype=jnp.int32)
    region_index = positions // slot_count
    slot_of = positions % slot_count
    opposite_table = jnp.array([1, 0, 3, 2], jnp.int32)

    def per_device(order_perm, counts_row):
        clipped = jnp.minimum(region_index, 3)
        fill_limit = jnp.where(region_index < 4, counts_row[clipped], 0)
        in_use = (region_index < 4) & (slot_of < fill_limit)
        pool_order = jnp.argsort(in_use.astype(jnp.int32), stable=True).astype(jnp.int32)
        pool_rank = jnp.zeros(end_count, jnp.int32).at[pool_order].set(positions)
        pool_mate = pool_order[pool_rank ^ 1]
        remote = end_count + opposite_table[clipped] * slot_count + slot_of
        end_value = jnp.where(in_use, remote, order_perm[pool_mate])
        partner_row = jnp.zeros(end_count, jnp.int32).at[order_perm].set(end_value)
        head = 4 * slot_count
        send_row = jnp.where(slot_of[:head] < counts_row[region_index[:head]], order_perm[:head], 0)
        return (send_row.astype(jnp.int32), partner_row)
    sends, partners = jax.vmap(per_device)(perms, counts)
    return (sends, partners)


def draw_send_rows(key, part):
    return build_graph(key)[0]


def draw_partner(key, part):
    return build_graph(key)[1].reshape(-1)


def level_of(own_key, extent, pieces, smallest, high):
    factor_of = 1.0
    for dim, blocks in pieces:
        draws = jax.random.uniform(jax.random.fold_in(jax.random.fold_in(own_key, 6), dim), (blocks,), jnp.float32, smallest / len(pieces), high / len(pieces))
        factor_of = factor_of * jnp.repeat(jnp.exp(draws), extent[dim] // blocks).reshape((-1,) + (1,) * (len(extent) - 1 - dim))
    return factor_of


def centred(key, shape, width, most, cuts=(), kind=jnp.bfloat16):
    values = width * jax.random.normal(key, shape, jnp.float32)
    if cuts:
        values = values * level_of(key, shape, cuts, -0.22, 0.18)
    return jnp.clip(values, -most, most).astype(kind)


def setup_inputs(seed: int = 0) -> dict:
    arg_keys = jax.random.split(jax.random.key(seed), 5)
    start_block = draw_start_block(jax.random.fold_in(arg_keys[4], 71), 0)
    restriction_maps = centred(arg_keys[1], (STALK, STALK, NODES * DEG), STALK ** -0.5, 2.0, ((2, 512),), jnp.float32)
    send_rows = draw_send_rows(jax.random.fold_in(arg_keys[4], 71), 0)
    partner = draw_partner(jax.random.fold_in(arg_keys[4], 71), 0)
    return {"start_block": start_block, "restriction_maps": restriction_maps, "send_rows": send_rows, "partner": partner}


highest = lax.Precision.HIGHEST
filter_center = 21.0
filter_radius = 15.0

def global_mates(send_rows, partner):
    end_count = NODE_DEV * DEG
    local_ids = partner.reshape(N_DOM * N_REP, end_count)
    device_ids = jnp.arange(N_DOM * N_REP, dtype=jnp.int32)[:, None]
    dom_pos = device_ids // N_REP
    rep_pos = device_ids % N_REP
    excess = jnp.maximum(local_ids - end_count, 0)
    group_index = excess // BND
    slot_index = excess % BND
    dom_step = jnp.where(group_index == 0, -1, jnp.where(group_index == 1, 1, 0))
    rep_step = jnp.where(group_index == 2, -1, jnp.where(group_index == 3, 1, 0))
    source = jnp.clip(dom_pos + dom_step, 0, N_DOM - 1) * N_REP + (rep_pos + rep_step + N_REP) % N_REP
    source = source.astype(jnp.int32)
    remote = send_rows[source, group_index * BND + slot_index]
    joined = jnp.where(local_ids < end_count, device_ids * end_count + local_ids, source * end_count + remote)
    return joined.reshape(-1).astype(jnp.int32)

def laplace(values, restriction_maps, mates):
    end_count = NODE_DEV * DEG
    stalks = values.reshape(-1, STALK, COLS)

    def per_device(device):
        own_stalks = lax.dynamic_slice_in_dim(stalks, device * NODE_DEV, NODE_DEV, 0)
        own_maps = lax.dynamic_slice_in_dim(restriction_maps, device * end_count, end_count, 2)
        own_mates = lax.dynamic_slice_in_dim(mates, device * end_count, end_count, 0)
        maps_four = own_maps.reshape(STALK, STALK, NODE_DEV, DEG)
        own_proj = jnp.einsum('abnk,nbc->nkac', maps_four, own_stalks, precision=highest)
        far_maps = jnp.take(restriction_maps, own_mates, axis=2)
        far_stalks = jnp.take(stalks, own_mates // DEG, axis=0)
        far_proj = jnp.einsum('abj,jbc->jac', far_maps, far_stalks, precision=highest)
        difference = own_proj - far_proj.reshape(NODE_DEV, DEG, STALK, COLS)
        return jnp.einsum('abnk,nkac->nbc', maps_four, difference, precision=highest)
    result = lax.map(per_device, jnp.arange(N_DOM * N_REP, dtype=jnp.int32))
    return result.reshape(-1, STALK * COLS)

def reference(start_block, restriction_maps, send_rows, partner):
    mates = global_mates(send_rows, partner)
    first_term = (laplace(start_block, restriction_maps, mates) - filter_center * start_block) / filter_radius
    filtered = 2.0 * (laplace(first_term, restriction_maps, mates) - filter_center * first_term) / filter_radius - start_block
    flat_rows = filtered.reshape(-1, COLS)
    gram_matrix = jnp.einsum('rc,rd->cd', flat_rows, flat_rows, precision=highest)
    upper_factor = jnp.linalg.cholesky(gram_matrix).T
    solved = lax.linalg.triangular_solve(upper_factor, flat_rows, left_side=False, lower=False)
    scaling = math.sqrt(NODES * STALK)
    return ((solved * scaling).reshape(-1, STALK * COLS), upper_factor / scaling)
```

```python
import functools
import math

import jax
import jax.numpy as jnp
from jax import lax
from jax.experimental import pallas as pl
from jax.experimental.pallas import tpu as pltpu
from jax.sharding import PartitionSpec as P

MESH = pl.DeviceIdType.MESH
F32 = jnp.float32
BF16 = jnp.bfloat16

STALK = 8
COLS = 64
DEG = 6
NODE_DEV = 128
ENDS = NODE_DEV * DEG
BND = 16
SLOTS = 4 * BND
WIDE = STALK * COLS
PLANE_DOM = 8
CENTER = 21.0
RADIUS = 15.0


def split_two(x):
    hi = x.astype(BF16)
    lo = (x - hi.astype(F32)).astype(BF16)
    return hi, lo


def dot_nn(a, b):
    return lax.dot_general(a, b, (((1,), (0,)), ((), ())), preferred_element_type=F32)


def dot_nt(a, b):
    return lax.dot_general(a, b, (((1,), (1,)), ((), ())), preferred_element_type=F32)


def row_bcast(row):
    return jnp.broadcast_to(row, (8, row.shape[1]))


def drain(ref, count, sem):
    pltpu.make_async_copy(ref.at[pl.ds(0, count)], ref.at[pl.ds(0, count)], sem).wait()


def filter_kernel(
    n_dom,
    n_rep,
    send_ref,
    start_ref,
    maps_ref,
    partner_ref,
    f_ref,
    g_ref,
    rt_ref,
    rk_ref,
    coef_ref,
    ss_ref,
    vt_ref,
    vhl_ref,
    vx_ref,
    t_ref,
    rs_ref,
    ms_ref,
    vsend_ref,
    rrecv_ref,
    vrecv_ref,
    cpack_ref,
    gsl_ref,
    rsbuf_ref,
    zsend_ref,
    zbuf_ref,
    agbuf_ref,
    rsem,
    vsem,
    arsem,
):
    d = lax.axis_index("dom")
    r = lax.axis_index("rep")
    z_count = n_dom // PLANE_DOM
    plane = PLANE_DOM * n_rep
    z = d // PLANE_DOM
    base = z * PLANE_DOM
    q = (d - base) * n_rep + r

    def plane_peer(i):
        t = lax.rem(q + 1 + i, plane)
        return t, (base + t // n_rep, lax.rem(t, n_rep))

    def z_peer(i):
        t = lax.rem(z + 1 + i, z_count)
        return (t * PLANE_DOM + (d - base), r)

    up = lax.rem(d + 1, n_dom)
    down = lax.rem(d + n_dom - 1, n_dom)
    nxt = lax.rem(r + 1, n_rep)
    prv = lax.rem(r + n_rep - 1, n_rep)
    neighbours = ((up, r), (down, r), (d, nxt), (d, prv))

    barrier = pltpu.get_barrier_semaphore()
    for peer in neighbours:
        pl.semaphore_signal(barrier, inc=1, device_id=peer, device_id_type=MESH)

    def greet_plane(i, carry):
        pl.semaphore_signal(barrier, inc=1, device_id=plane_peer(i)[1], device_id_type=MESH)
        return carry

    def greet_z(i, carry):
        pl.semaphore_signal(barrier, inc=1, device_id=z_peer(i), device_id_type=MESH)
        return carry

    lax.fori_loop(0, z_count - 1, greet_z, 0)
    lax.fori_loop(0, plane - 1, greet_plane, 0)

    part = jnp.broadcast_to(partner_ref[...].astype(F32), (8, ENDS))
    end_id = lax.broadcasted_iota(jnp.int32, (8, ENDS), 1).astype(F32)
    node_id = jnp.floor((end_id + 0.5) * (1.0 / DEG))
    sub8 = lax.broadcasted_iota(jnp.int32, (8, ENDS), 0)
    extra = jnp.where(sub8 == 0, part, node_id)
    for t in range(DEG):
        cols = slice(t * 128, (t + 1) * 128)
        block = jnp.concatenate(
            [maps_ref[:, cols], extra[:, cols], jnp.zeros((56, 128), F32)], axis=0
        )
        rt_ref[cols, :] = block.T

    for t in range(4):
        vt_ref[t * 128 : (t + 1) * 128, :] = start_ref[:, t * 128 : (t + 1) * 128].T

    for s in range(SLOTS):
        rs_ref[s : s + 1, :] = rt_ref[pl.ds(send_ref[0, s], 1), :]
    rs = rs_ref[...]
    lane = lax.broadcasted_iota(jnp.int32, (SLOTS, 128), 1).astype(F32)
    slot = lax.broadcasted_iota(jnp.int32, (SLOTS, 1), 0)
    expect = (ENDS + jnp.bitwise_xor(slot, BND)).astype(F32)
    used = rs[:, 64:65] == expect
    hot = jnp.where(jnp.logical_and(rs[:, 65:66] == lane, used), 1.0, 0.0).astype(BF16)
    hot_wide = jnp.concatenate([hot, hot], axis=1)
    hot_tall = jnp.concatenate([hot, hot], axis=0)

    sub = lax.broadcasted_iota(jnp.int32, (128, 128), 0).astype(F32)
    rhl = []
    kk_rows = []
    for k in range(DEG):
        rk = rt_ref[pl.ds(k, NODE_DEV, stride=DEG), :].T
        rk_ref[k] = rk[0:64, :]
        p = rk[64:65, :]
        node = jnp.floor((p + 0.5) * (1.0 / DEG))
        kk_rows.append(p - DEG * node)
        one = jnp.where(sub == node, 1.0, 0.0).astype(BF16)
        ss_ref[0:128, k * 128 : (k + 1) * 128] = one
        ss_ref[128:256, k * 128 : (k + 1) * 128] = one
        hi, lo = split_two(rk[0:64, :])
        rhl.append(jnp.concatenate([hi, lo], axis=1))
    rhl = jnp.concatenate(rhl, axis=0)

    sub_b = lax.broadcasted_iota(jnp.int32, (8, 128), 0)
    own = [jnp.zeros((8, 128), F32) for _ in range(STALK)]
    for j in range(3):
        far = dot_nn(rhl, ss_ref[:, j * 256 : (j + 1) * 256])
        for h in range(2):
            k = 2 * j + h
            mate_map = far[0:64, h * 128 : (h + 1) * 128]
            for m in range(1, DEG):
                mate_map = jnp.where(
                    kk_rows[k] == float(m),
                    far[m * 64 : (m + 1) * 64, h * 128 : (h + 1) * 128],
                    mate_map,
                )
            for a2 in range(STALK):
                acc = jnp.zeros((8, 128), F32)
                for a in range(STALK):
                    coef = row_bcast(rk_ref[k, a * 8 + a2 : a * 8 + a2 + 1, :])
                    acc = acc + coef * mate_map[a * 8 : (a + 1) * 8, :]
                    own[a2] = own[a2] + coef * rk_ref[k, a * 8 : (a + 1) * 8, :]
                coef_ref[k, a2 * 8 : (a2 + 1) * 8, :] = acc * (-1.0 / RADIUS)
    for a2 in range(STALK):
        coef_ref[DEG, a2 * 8 : (a2 + 1) * 8, :] = (
            own[a2] - jnp.where(sub_b == a2, CENTER, 0.0)
        ) * (1.0 / RADIUS)

    def spread(values_ref):
        hi, lo = split_two(values_ref[...])
        vhl_ref[:, 0:128] = hi
        vhl_ref[:, 128:256] = lo

    def value_copies(step):
        return [
            pltpu.make_async_remote_copy(
                src_ref=vsend_ref.at[step, pl.ds(k * BND, BND), :],
                dst_ref=vrecv_ref.at[step, pl.ds((k ^ 1) * BND, BND), :],
                send_sem=vsem.at[0, step, k],
                recv_sem=vsem.at[1, step, k ^ 1],
                device_id=neighbours[k],
                device_id_type=MESH,
            )
            for k in range(4)
        ]

    map_copies = [
        pltpu.make_async_remote_copy(
            src_ref=rs_ref.at[pl.ds(k * BND, BND), :],
            dst_ref=rrecv_ref.at[pl.ds((k ^ 1) * BND, BND), :],
            send_sem=rsem.at[0, k],
            recv_sem=rsem.at[1, k ^ 1],
            device_id=neighbours[k],
            device_id_type=MESH,
        )
        for k in range(4)
    ]

    def recv_waits(copies):
        for copy in copies:
            copy.wait_recv()

    def outgoing(step):
        vsend_ref[step] = dot_nt(hot_wide, vhl_ref[...])

    def local_part(own_ref, out_ref, combine):
        for j in range(3):
            vx_ref[:, j * 256 : (j + 1) * 256] = dot_nn(
                vhl_ref[...], ss_ref[:, j * 256 : (j + 1) * 256]
            )

        def columns(i, carry):
            acc = [[jnp.zeros((8, 128), F32) for _ in range(2)] for _ in range(STALK)]
            for k in range(DEG + 1):
                for b in range(STALK):
                    vals = []
                    for h in range(2):
                        at = pl.ds(pl.multiple_of(b * COLS + i * 16 + h * 8, 8), 8)
                        if k == DEG:
                            vals.append(own_ref[at, :])
                        else:
                            vals.append(vx_ref[at, k * 128 : (k + 1) * 128])
                    for a2 in range(STALK):
                        coef = row_bcast(coef_ref[k, a2 * 8 + b : a2 * 8 + b + 1, :])
                        for h in range(2):
                            acc[a2][h] = acc[a2][h] + coef * vals[h]
            for a2 in range(STALK):
                for h in range(2):
                    at = pl.ds(pl.multiple_of(a2 * COLS + i * 16 + h * 8, 8), 8)
                    out_ref[at, :] = combine(acc[a2][h], at)
            return carry

        lax.fori_loop(0, 4, columns, 0)

    def remote_part(step):
        low = lax.broadcasted_iota(jnp.int32, (8, 128), 1) < SLOTS
        turned = []
        for t in range(4):
            block = vrecv_ref[step, :, t * 128 : (t + 1) * 128]
            turned.append(jnp.concatenate([block, block], axis=0).T)
        for cg in range(8):
            acc = [jnp.zeros((8, 128), F32) for _ in range(STALK)]
            for b in range(STALK):
                row = b * COLS + cg * 8
                val = turned[row // 128][row % 128 : row % 128 + 8, :]
                for a2 in range(STALK):
                    coef = row_bcast(ms_ref[a2 * 8 + b : a2 * 8 + b + 1, :])
                    acc[a2] = acc[a2] + coef * val
            for a2 in range(STALK):
                hi = acc[a2].astype(BF16).astype(F32)
                cpack_ref[a2 * COLS + cg * 8 : a2 * COLS + cg * 8 + 8, :] = jnp.where(
                    low, hi, acc[a2] - hi
                )
        return dot_nn(cpack_ref[...].astype(BF16), hot_tall)

    spread(vt_ref)
    outgoing(0)
    pl.semaphore_wait(barrier, 4 + (plane - 1) + (z_count - 1))
    for copy in map_copies:
        copy.start()
    first_copies = value_copies(0)
    for copy in first_copies:
        copy.start()
    local_part(vt_ref, t_ref, lambda acc, at: acc)

    recv_waits(map_copies)
    far_maps = jnp.concatenate([rrecv_ref[...], rrecv_ref[...]], axis=0).T
    own_maps = jnp.concatenate([rs, rs], axis=0).T
    for a2 in range(STALK):
        acc = jnp.zeros((8, 128), F32)
        for a in range(STALK):
            acc = acc + row_bcast(own_maps[a * 8 + a2 : a * 8 + a2 + 1, :]) * (
                far_maps[a * 8 : (a + 1) * 8, :]
            )
        ms_ref[a2 * 8 : (a2 + 1) * 8, :] = acc * (-1.0 / RADIUS)
    recv_waits(first_copies)
    t_ref[...] = t_ref[...] + remote_part(0)

    spread(t_ref)
    outgoing(1)
    second_copies = value_copies(1)
    for copy in second_copies:
        copy.start()
    local_part(t_ref, vt_ref, lambda acc, at: 2.0 * acc - vt_ref[at, :])
    recv_waits(second_copies)
    vt_ref[...] = vt_ref[...] + 2.0 * remote_part(1)

    spread(vt_ref)
    tall = jnp.concatenate(
        [
            jnp.concatenate(
                [vhl_ref[a * COLS : (a + 1) * COLS, h * 128 : (h + 1) * 128] for a in range(STALK)],
                axis=1,
            )
            for h in range(2)
        ],
        axis=0,
    )
    prod = dot_nt(tall, tall)
    half = prod[0:64, :] + prod[64:128, :]
    both = half + pltpu.roll(half, 64, 1)
    lane32 = lax.broadcasted_iota(jnp.int32, (32, 128), 1)
    packed = jnp.where(lane32 < 64, both[0:32, :], both[32:64, :])
    for i in range(plane):
        gsl_ref[i] = packed[i : i + 1, :]

    def reduce_start(i, carry):
        t, peer = plane_peer(i)
        pltpu.make_async_remote_copy(
            src_ref=gsl_ref.at[t],
            dst_ref=rsbuf_ref.at[q],
            send_sem=arsem.at[0],
            recv_sem=arsem.at[1],
            device_id=peer,
            device_id_type=MESH,
        ).start()
        return carry

    lax.fori_loop(0, plane - 1, reduce_start, 0)
    rsbuf_ref[q] = gsl_ref[q]
    for t in range(4):
        f_ref[:, t * 128 : (t + 1) * 128] = vt_ref[t * 128 : (t + 1) * 128, :].T
    drain(rsbuf_ref, plane - 1, arsem.at[1])

    def total(ref, count):
        rows = [ref[i] for i in range(count)]
        while len(rows) > 1:
            rows = [rows[i] + rows[i + 1] for i in range(0, len(rows) - 1, 2)] + (
                [rows[-1]] if len(rows) % 2 else []
            )
        return rows[0]

    part_sum = total(rsbuf_ref, plane)
    zsend_ref[0] = part_sum

    def z_start(i, carry):
        pltpu.make_async_remote_copy(
            src_ref=zsend_ref.at[0],
            dst_ref=zbuf_ref.at[z],
            send_sem=arsem.at[2],
            recv_sem=arsem.at[3],
            device_id=z_peer(i),
            device_id_type=MESH,
        ).start()
        return carry

    lax.fori_loop(0, z_count - 1, z_start, 0)
    zbuf_ref[z] = part_sum
    drain(zbuf_ref, z_count - 1, arsem.at[3])
    slice_sum = total(zbuf_ref, z_count)
    zsend_ref[1] = slice_sum

    def gather_start(i, carry):
        pltpu.make_async_remote_copy(
            src_ref=zsend_ref.at[1],
            dst_ref=agbuf_ref.at[q],
            send_sem=arsem.at[4],
            recv_sem=arsem.at[5],
            device_id=plane_peer(i)[1],
            device_id_type=MESH,
        ).start()
        return carry

    lax.fori_loop(0, plane - 1, gather_start, 0)
    agbuf_ref[q] = slice_sum
    drain(agbuf_ref, plane - 1, arsem.at[5])
    for i in range(plane):
        g_ref[i : i + 1, :] = agbuf_ref[i]

    for copies in (map_copies, first_copies, second_copies):
        for copy in copies:
            copy.wait_send()
    drain(rsbuf_ref, plane - 1, arsem.at[0])
    drain(zbuf_ref, z_count - 1, arsem.at[2])
    drain(agbuf_ref, plane - 1, arsem.at[4])


def solve_kernel(scaling, f_ref, g_ref, basis_ref, triangle_ref):
    g = g_ref[...]
    turned = pltpu.roll(g, 64, 1)
    lane32 = lax.broadcasted_iota(jnp.int32, (32, 128), 1)
    row32 = lax.broadcasted_iota(jnp.int32, (32, 128), 0)
    top = jnp.where(lane32 < 64, g, jnp.where(lane32 - 64 == row32, 1.0, 0.0))
    bottom = jnp.where(lane32 < 64, turned, jnp.where(lane32 - 96 == row32, 1.0, 0.0))
    work = [top[i * 8 : (i + 1) * 8, :] for i in range(4)] + [
        bottom[i * 8 : (i + 1) * 8, :] for i in range(4)
    ]
    sub = lax.broadcasted_iota(jnp.int32, (8, 128), 0)
    for k in range(COLS):
        group, row = k // 8, k % 8
        pivot_row = work[group][row : row + 1, :]
        scaled = pivot_row / pivot_row[:, k : k + 1]
        for i in range(group, 8):
            col = work[i][:, k : k + 1]
            update = col * scaled
            if i == group:
                update = jnp.where(sub > row, update, 0.0)
            work[i] = work[i] - update
    lane = lax.broadcasted_iota(jnp.int32, (8, 128), 1)
    rows_out = []
    for i in range(8):
        diag = jnp.sum(jnp.where(lane == sub + 8 * i, work[i], 0.0), axis=1, keepdims=True)
        rows_out.append(work[i] / jnp.sqrt(diag))
    full = jnp.concatenate(rows_out, axis=0)
    lane64 = lax.broadcasted_iota(jnp.int32, (COLS, 128), 1)
    row64 = lax.broadcasted_iota(jnp.int32, (COLS, 128), 0)
    triangle_ref[...] = jnp.where(lane64 >= row64, full * (1.0 / scaling), 0.0)[:, 0:COLS]
    full = full * scaling
    block = jnp.concatenate(
        [
            jnp.where(lane64 < 64, pltpu.roll(full, 64, 1), 0.0),
            jnp.where(lane64 < 64, 0.0, full),
        ],
        axis=0,
    )
    bhi, blo = split_two(block)
    right = jnp.concatenate([bhi, bhi, blo], axis=1)
    for t in range(4):
        fhi, flo = split_two(f_ref[:, t * 128 : (t + 1) * 128])
        left = jnp.concatenate([fhi, flo, fhi], axis=1)
        basis_ref[:, t * 128 : (t + 1) * 128] = dot_nt(left, right)


def local(n_dom, n_rep, start_block, restriction_maps, send_rows, partner):
    z_count = n_dom // PLANE_DOM
    plane = PLANE_DOM * n_rep
    vmem = pl.BlockSpec(memory_space=pltpu.VMEM)
    smem = pl.BlockSpec(memory_space=pltpu.SMEM)
    maps = restriction_maps.reshape(STALK * STALK, ENDS)
    partner = partner.reshape(1, ENDS)
    f_rows, gram = pl.pallas_call(
        functools.partial(filter_kernel, n_dom, n_rep),
        out_shape=[
            jax.ShapeDtypeStruct((NODE_DEV, WIDE), F32),
            jax.ShapeDtypeStruct((32, 128), F32),
        ],
        in_specs=[smem, vmem, vmem, vmem],
        out_specs=[vmem, vmem],
        scratch_shapes=[
            pltpu.VMEM((ENDS, 128), F32),
            pltpu.VMEM((DEG, 64, 128), F32),
            pltpu.VMEM((DEG + 1, 64, 128), F32),
            pltpu.VMEM((256, ENDS), BF16),
            pltpu.VMEM((WIDE, 128), F32),
            pltpu.VMEM((WIDE, 256), BF16),
            pltpu.VMEM((WIDE, ENDS), F32),
            pltpu.VMEM((WIDE, 128), F32),
            pltpu.VMEM((SLOTS, 128), F32),
            pltpu.VMEM((64, 128), F32),
            pltpu.VMEM((2, SLOTS, WIDE), F32),
            pltpu.VMEM((SLOTS, 128), F32),
            pltpu.VMEM((2, SLOTS, WIDE), F32),
            pltpu.VMEM((WIDE, 128), F32),
            pltpu.VMEM((plane, 1, 128), F32),
            pltpu.VMEM((plane, 1, 128), F32),
            pltpu.VMEM((2, 1, 128), F32),
            pltpu.VMEM((z_count, 1, 128), F32),
            pltpu.VMEM((plane, 1, 128), F32),
            pltpu.SemaphoreType.DMA((2, 4)),
            pltpu.SemaphoreType.DMA((2, 2, 4)),
            pltpu.SemaphoreType.DMA((6,)),
        ],
        compiler_params=pltpu.CompilerParams(
            collective_id=0, has_side_effects=True, vmem_limit_bytes=40 * 1024 * 1024
        ),
        name="filter_and_gram",
    )(send_rows, start_block, maps, partner)
    scaling = math.sqrt(NODE_DEV * STALK * n_dom * n_rep)
    return pl.pallas_call(
        functools.partial(solve_kernel, scaling),
        out_shape=[
            jax.ShapeDtypeStruct((NODE_DEV, WIDE), F32),
            jax.ShapeDtypeStruct((COLS, COLS), F32),
        ],
        in_specs=[vmem, vmem],
        out_specs=[vmem, vmem],
        compiler_params=pltpu.CompilerParams(vmem_limit_bytes=16 * 1024 * 1024),
        name="factor_and_solve",
    )(f_rows, gram)


def solution(mesh):
    n_dom, n_rep = mesh.shape["dom"], mesh.shape["rep"]
    in_specs = (
        P(("dom", "rep"), None),
        P(None, None, ("dom", "rep")),
        P(("dom", "rep"), None),
        P(("dom", "rep")),
    )
    out_specs = (P(("dom", "rep"), None), P())
    return jax.shard_map(
        functools.partial(local, n_dom, n_rep),
        mesh=mesh,
        in_specs=in_specs,
        out_specs=out_specs,
        check_vma=False,
    )
```

```python
import functools
import math

import jax
import jax.numpy as jnp
from jax import lax
from jax.experimental import pallas as pl
from jax.experimental.pallas import tpu as pltpu
from jax.sharding import PartitionSpec as P

MESH = pl.DeviceIdType.MESH
F32 = jnp.float32
BF16 = jnp.bfloat16

STALK = 8
COLS = 64
DEG = 6
NODE_DEV = 128
ENDS = NODE_DEV * DEG
BND = 16
SLOTS = 4 * BND
WIDE = STALK * COLS
PLANE_DOM = 8
CENTER = 21.0
RADIUS = 15.0


def split_two(x):
    hi = x.astype(BF16)
    lo = (x - hi.astype(F32)).astype(BF16)
    return hi, lo


def dot_nn(a, b):
    return lax.dot_general(a, b, (((1,), (0,)), ((), ())), preferred_element_type=F32)


def dot_nt(a, b):
    return lax.dot_general(a, b, (((1,), (1,)), ((), ())), preferred_element_type=F32)


def row_bcast(row):
    return jnp.broadcast_to(row, (8, row.shape[1]))


def drain(ref, count, sem):
    pltpu.make_async_copy(ref.at[pl.ds(0, count)], ref.at[pl.ds(0, count)], sem).wait()


def filter_kernel(
    n_dom,
    n_rep,
    start_hbm,
    maps_hbm,
    send_hbm,
    partner_hbm,
    f_ref,
    g_ref,
    start_ref,
    maps_ref,
    send_ref,
    partner_ref,
    rt_ref,
    rk_ref,
    coef_ref,
    ss_ref,
    vt_ref,
    vhl_ref,
    vx_ref,
    t_ref,
    rs_ref,
    ms_ref,
    vsend_ref,
    rrecv_ref,
    vrecv_ref,
    cpack_ref,
    gsl_ref,
    rsbuf_ref,
    zsend_ref,
    zbuf_ref,
    agbuf_ref,
    rsem,
    vsem,
    arsem,
    insem,
    xsem,
    zsem,
):
    d = lax.axis_index("dom")
    r = lax.axis_index("rep")
    z_count = n_dom // PLANE_DOM
    plane = PLANE_DOM * n_rep
    z = d // PLANE_DOM
    base = z * PLANE_DOM
    q = (d - base) * n_rep + r

    def plane_peer(i):
        t = lax.rem(q + 1 + i, plane)
        return t, (base + t // n_rep, lax.rem(t, n_rep))

    def z_peer(i):
        t = lax.rem(z + 1 + i, z_count)
        return (t * PLANE_DOM + (d - base), r)

    up = lax.rem(d + 1, n_dom)
    down = lax.rem(d + n_dom - 1, n_dom)
    nxt = lax.rem(r + 1, n_rep)
    prv = lax.rem(r + n_rep - 1, n_rep)
    neighbours = ((up, r), (down, r), (d, nxt), (d, prv))

    loads = [
        pltpu.make_async_copy(src, dst, insem.at[i])
        for i, (src, dst) in enumerate(
            (
                (send_hbm, send_ref),
                (start_hbm, start_ref),
                (maps_hbm, maps_ref),
                (partner_hbm, partner_ref),
            )
        )
    ]
    for load in loads:
        load.start()

    mine = d - base
    other_core = d + 1 - 2 * lax.rem(d, 2)
    x_peers = [(base + lax.rem(mine + 2 * i, PLANE_DOM), r) for i in range(1, PLANE_DOM // 2)]
    near = [(up, r), (down, r)]
    near += [(base + lax.rem(mine + i, PLANE_DOM), r) for i in range(1, PLANE_DOM)]
    for i in range(1, n_rep):
        turn = lax.rem(r + i, n_rep)
        near += [(d, turn), (other_core, turn)]

    def z_shift(by):
        return (lax.rem(z + z_count + by, z_count) * PLANE_DOM + mine, r)

    near += [z_shift(by) for by in (1, -1, 2, -2)]
    barrier = pltpu.get_barrier_semaphore()
    for peer in near:
        pl.semaphore_signal(barrier, inc=1, device_id=peer, device_id_type=MESH)

    loads[0].wait()
    loads[1].wait()
    for s in range(SLOTS):
        node = lax.div(send_ref[0, s], DEG)
        vsend_ref[0, s : s + 1, :] = start_ref[pl.ds(node, 1), :]
    loads[2].wait()
    loads[3].wait()

    part = jnp.broadcast_to(partner_ref[...].reshape(1, ENDS).astype(F32), (8, ENDS))
    end_id = lax.broadcasted_iota(jnp.int32, (8, ENDS), 1).astype(F32)
    node_id = jnp.floor((end_id + 0.5) * (1.0 / DEG))
    sub8 = lax.broadcasted_iota(jnp.int32, (8, ENDS), 0)
    extra = jnp.where(sub8 == 0, part, node_id)
    for t in range(DEG):
        cols = slice(t * 128, (t + 1) * 128)
        block = jnp.concatenate(
            [maps_ref[:, :, cols].reshape(64, 128), extra[:, cols], jnp.zeros((56, 128), F32)], axis=0
        )
        rt_ref[cols, :] = block.T

    for t in range(4):
        vt_ref[t * 128 : (t + 1) * 128, :] = start_ref[:, t * 128 : (t + 1) * 128].T

    for s in range(SLOTS):
        rs_ref[s : s + 1, :] = rt_ref[pl.ds(send_ref[0, s], 1), :]
    rs = rs_ref[...]
    lane = lax.broadcasted_iota(jnp.int32, (SLOTS, 128), 1).astype(F32)
    slot = lax.broadcasted_iota(jnp.int32, (SLOTS, 1), 0)
    expect = (ENDS + jnp.bitwise_xor(slot, BND)).astype(F32)
    used = rs[:, 64:65] == expect
    hot = jnp.where(jnp.logical_and(rs[:, 65:66] == lane, used), 1.0, 0.0).astype(BF16)
    hot_wide = jnp.concatenate([hot, hot], axis=1)
    hot_tall = jnp.concatenate([hot, hot], axis=0)

    sub = lax.broadcasted_iota(jnp.int32, (128, 128), 0).astype(F32)
    rhl = []
    kk_rows = []
    for k in range(DEG):
        rk = rt_ref[pl.ds(k, NODE_DEV, stride=DEG), :].T
        rk_ref[k] = rk[0:64, :]
        p = rk[64:65, :]
        node = jnp.floor((p + 0.5) * (1.0 / DEG))
        kk_rows.append(p - DEG * node)
        one = jnp.where(sub == node, 1.0, 0.0).astype(BF16)
        ss_ref[0:128, k * 128 : (k + 1) * 128] = one
        ss_ref[128:256, k * 128 : (k + 1) * 128] = one
        hi, lo = split_two(rk[0:64, :])
        rhl.append(jnp.concatenate([hi, lo], axis=1))
    rhl = jnp.concatenate(rhl, axis=0)

    def value_copies(step):
        return [
            pltpu.make_async_remote_copy(
                src_ref=vsend_ref.at[step, pl.ds(k * BND, BND), :],
                dst_ref=vrecv_ref.at[step, pl.ds((k ^ 1) * BND, BND), :],
                send_sem=vsem.at[0, step, k],
                recv_sem=vsem.at[1, step, k ^ 1],
                device_id=neighbours[k],
                device_id_type=MESH,
            )
            for k in range(4)
        ]

    map_copies = [
        pltpu.make_async_remote_copy(
            src_ref=rs_ref.at[pl.ds(k * BND, BND), :],
            dst_ref=rrecv_ref.at[pl.ds((k ^ 1) * BND, BND), :],
            send_sem=rsem.at[0, k],
            recv_sem=rsem.at[1, k ^ 1],
            device_id=neighbours[k],
            device_id_type=MESH,
        )
        for k in range(4)
    ]

    pl.semaphore_wait(barrier, len(near))
    first_copies = value_copies(0)
    for copy in first_copies + map_copies:
        copy.start()
    for peer in x_peers:
        pl.semaphore_signal(xsem, inc=1, device_id=peer, device_id_type=MESH)
    for by in (2, -2):
        pl.semaphore_signal(zsem.at[0], inc=1, device_id=z_shift(by), device_id_type=MESH)

    sub_b = lax.broadcasted_iota(jnp.int32, (8, 128), 0)
    own = [jnp.zeros((8, 128), F32) for _ in range(STALK)]
    for j in range(3):
        far = dot_nn(rhl, ss_ref[:, j * 256 : (j + 1) * 256])
        for h in range(2):
            k = 2 * j + h
            mate_map = far[0:64, h * 128 : (h + 1) * 128]
            for m in range(1, DEG):
                mate_map = jnp.where(
                    kk_rows[k] == float(m),
                    far[m * 64 : (m + 1) * 64, h * 128 : (h + 1) * 128],
                    mate_map,
                )
            for a2 in range(STALK):
                acc = jnp.zeros((8, 128), F32)
                for a in range(STALK):
                    coef = row_bcast(rk_ref[k, a * 8 + a2 : a * 8 + a2 + 1, :])
                    acc = acc + coef * mate_map[a * 8 : (a + 1) * 8, :]
                    own[a2] = own[a2] + coef * rk_ref[k, a * 8 : (a + 1) * 8, :]
                coef_ref[k, a2 * 8 : (a2 + 1) * 8, :] = acc * (-1.0 / RADIUS)
    for a2 in range(STALK):
        coef_ref[DEG, a2 * 8 : (a2 + 1) * 8, :] = (
            own[a2] - jnp.where(sub_b == a2, CENTER, 0.0)
        ) * (1.0 / RADIUS)

    def spread(values_ref):
        hi, lo = split_two(values_ref[...])
        vhl_ref[:, 0:128] = hi
        vhl_ref[:, 128:256] = lo

    def recv_waits(copies):
        for copy in copies:
            copy.wait_recv()

    def outgoing(step):
        vsend_ref[step] = dot_nt(hot_wide, vhl_ref[...])

    def local_part(own_ref, out_ref, combine):
        for j in range(3):
            vx_ref[:, j * 256 : (j + 1) * 256] = dot_nn(
                vhl_ref[...], ss_ref[:, j * 256 : (j + 1) * 256]
            )

        def columns(i, carry):
            acc = [[jnp.zeros((8, 128), F32) for _ in range(2)] for _ in range(STALK)]
            for k in range(DEG + 1):
                for b in range(STALK):
                    vals = []
                    for h in range(2):
                        at = pl.ds(pl.multiple_of(b * COLS + i * 16 + h * 8, 8), 8)
                        if k == DEG:
                            vals.append(own_ref[at, :])
                        else:
                            vals.append(vx_ref[at, k * 128 : (k + 1) * 128])
                    for a2 in range(STALK):
                        coef = row_bcast(coef_ref[k, a2 * 8 + b : a2 * 8 + b + 1, :])
                        for h in range(2):
                            acc[a2][h] = acc[a2][h] + coef * vals[h]
            for a2 in range(STALK):
                for h in range(2):
                    at = pl.ds(pl.multiple_of(a2 * COLS + i * 16 + h * 8, 8), 8)
                    out_ref[at, :] = combine(acc[a2][h], at)
            return carry

        lax.fori_loop(0, 4, columns, 0)

    def remote_part(step):
        low = lax.broadcasted_iota(jnp.int32, (8, 128), 1) < SLOTS
        turned = []
        for t in range(4):
            block = vrecv_ref[step, :, t * 128 : (t + 1) * 128]
            turned.append(jnp.concatenate([block, block], axis=0).T)
        for cg in range(8):
            acc = [jnp.zeros((8, 128), F32) for _ in range(STALK)]
            for b in range(STALK):
                row = b * COLS + cg * 8
                val = turned[row // 128][row % 128 : row % 128 + 8, :]
                for a2 in range(STALK):
                    coef = row_bcast(ms_ref[a2 * 8 + b : a2 * 8 + b + 1, :])
                    acc[a2] = acc[a2] + coef * val
            for a2 in range(STALK):
                hi = acc[a2].astype(BF16).astype(F32)
                cpack_ref[a2 * COLS + cg * 8 : a2 * COLS + cg * 8 + 8, :] = jnp.where(
                    low, hi, acc[a2] - hi
                )
        return dot_nn(cpack_ref[...].astype(BF16), hot_tall)

    spread(vt_ref)
    local_part(vt_ref, t_ref, lambda acc, at: acc)

    recv_waits(map_copies)
    far_maps = jnp.concatenate([rrecv_ref[...], rrecv_ref[...]], axis=0).T
    own_maps = jnp.concatenate([rs, rs], axis=0).T
    for a2 in range(STALK):
        acc = jnp.zeros((8, 128), F32)
        for a in range(STALK):
            acc = acc + row_bcast(own_maps[a * 8 + a2 : a * 8 + a2 + 1, :]) * (
                far_maps[a * 8 : (a + 1) * 8, :]
            )
        ms_ref[a2 * 8 : (a2 + 1) * 8, :] = acc * (-1.0 / RADIUS)
    recv_waits(first_copies)
    t_ref[...] = t_ref[...] + remote_part(0)

    spread(t_ref)
    outgoing(1)
    second_copies = value_copies(1)
    for copy in second_copies:
        copy.start()
    pl.semaphore_wait(zsem.at[0], 2)
    for by in (4, -4):
        pl.semaphore_signal(zsem.at[1], inc=1, device_id=z_shift(by), device_id_type=MESH)
    local_part(t_ref, vt_ref, lambda acc, at: 2.0 * acc - vt_ref[at, :])
    recv_waits(second_copies)
    vt_ref[...] = vt_ref[...] + 2.0 * remote_part(1)

    spread(vt_ref)
    tall = jnp.concatenate(
        [
            jnp.concatenate(
                [vhl_ref[a * COLS : (a + 1) * COLS, h * 128 : (h + 1) * 128] for a in range(STALK)],
                axis=1,
            )
            for h in range(2)
        ],
        axis=0,
    )
    prod = dot_nt(tall, tall)
    half = prod[0:64, :] + prod[64:128, :]
    both = half + pltpu.roll(half, 64, 1)
    lane32 = lax.broadcasted_iota(jnp.int32, (32, 128), 1)
    packed = jnp.where(lane32 < 64, both[0:32, :], both[32:64, :])
    for i in range(plane):
        gsl_ref[i] = packed[i : i + 1, :]

    pl.semaphore_wait(xsem, len(x_peers))

    def reduce_start(i, carry):
        t, peer = plane_peer(i)
        pltpu.make_async_remote_copy(
            src_ref=gsl_ref.at[t],
            dst_ref=rsbuf_ref.at[q],
            send_sem=arsem.at[0],
            recv_sem=arsem.at[1],
            device_id=peer,
            device_id_type=MESH,
        ).start()
        return carry

    lax.fori_loop(0, plane - 1, reduce_start, 0)
    rsbuf_ref[q] = gsl_ref[q]
    for t in range(4):
        f_ref[:, t * 128 : (t + 1) * 128] = vt_ref[t * 128 : (t + 1) * 128, :].T
    drain(rsbuf_ref, plane - 1, arsem.at[1])

    def total(ref, count):
        rows = [ref[i] for i in range(count)]
        while len(rows) > 1:
            rows = [rows[i] + rows[i + 1] for i in range(0, len(rows) - 1, 2)] + (
                [rows[-1]] if len(rows) % 2 else []
            )
        return rows[0]

    part_sum = total(rsbuf_ref, plane)
    zsend_ref[0] = part_sum
    pl.semaphore_wait(zsem.at[1], 2)

    def z_start(i, carry):
        pltpu.make_async_remote_copy(
            src_ref=zsend_ref.at[0],
            dst_ref=zbuf_ref.at[z],
            send_sem=arsem.at[2],
            recv_sem=arsem.at[3],
            device_id=z_peer(i),
            device_id_type=MESH,
        ).start()
        return carry

    lax.fori_loop(0, z_count - 1, z_start, 0)
    zbuf_ref[z] = part_sum
    drain(zbuf_ref, z_count - 1, arsem.at[3])
    slice_sum = total(zbuf_ref, z_count)
    zsend_ref[1] = slice_sum

    def gather_start(i, carry):
        pltpu.make_async_remote_copy(
            src_ref=zsend_ref.at[1],
            dst_ref=agbuf_ref.at[q],
            send_sem=arsem.at[4],
            recv_sem=arsem.at[5],
            device_id=plane_peer(i)[1],
            device_id_type=MESH,
        ).start()
        return carry

    lax.fori_loop(0, plane - 1, gather_start, 0)
    agbuf_ref[q] = slice_sum
    drain(agbuf_ref, plane - 1, arsem.at[5])
    for i in range(plane):
        g_ref[i : i + 1, :] = agbuf_ref[i]

    for copies in (map_copies, first_copies, second_copies):
        for copy in copies:
            copy.wait_send()
    drain(rsbuf_ref, plane - 1, arsem.at[0])
    drain(zbuf_ref, z_count - 1, arsem.at[2])
    drain(agbuf_ref, plane - 1, arsem.at[4])


def solve_kernel(scaling, f_ref, g_ref, basis_ref, triangle_ref):
    g = g_ref[...]
    turned = pltpu.roll(g, 64, 1)
    lane32 = lax.broadcasted_iota(jnp.int32, (32, 128), 1)
    row32 = lax.broadcasted_iota(jnp.int32, (32, 128), 0)
    top = jnp.where(lane32 < 64, g, jnp.where(lane32 - 64 == row32, 1.0, 0.0))
    bottom = jnp.where(lane32 < 64, turned, jnp.where(lane32 - 96 == row32, 1.0, 0.0))
    work = [top[i * 8 : (i + 1) * 8, :] for i in range(4)] + [
        bottom[i * 8 : (i + 1) * 8, :] for i in range(4)
    ]
    sub = lax.broadcasted_iota(jnp.int32, (8, 128), 0)
    for k in range(COLS):
        group, row = k // 8, k % 8
        pivot_row = work[group][row : row + 1, :]
        scaled = pivot_row / pivot_row[:, k : k + 1]
        for i in range(group, 8):
            col = work[i][:, k : k + 1]
            update = col * scaled
            if i == group:
                update = jnp.where(sub > row, update, 0.0)
            work[i] = work[i] - update
    lane = lax.broadcasted_iota(jnp.int32, (8, 128), 1)
    rows_out = []
    for i in range(8):
        diag = jnp.sum(jnp.where(lane == sub + 8 * i, work[i], 0.0), axis=1, keepdims=True)
        rows_out.append(work[i] / jnp.sqrt(diag))
    full = jnp.concatenate(rows_out, axis=0)
    lane64 = lax.broadcasted_iota(jnp.int32, (COLS, 128), 1)
    row64 = lax.broadcasted_iota(jnp.int32, (COLS, 128), 0)
    triangle_ref[...] = jnp.where(lane64 >= row64, full * (1.0 / scaling), 0.0)[:, 0:COLS]
    full = full * scaling
    block = jnp.concatenate(
        [
            jnp.where(lane64 < 64, pltpu.roll(full, 64, 1), 0.0),
            jnp.where(lane64 < 64, 0.0, full),
        ],
        axis=0,
    )
    bhi, blo = split_two(block)
    right = jnp.concatenate([bhi, bhi, blo], axis=1)
    for t in range(4):
        fhi, flo = split_two(f_ref[:, t * 128 : (t + 1) * 128])
        left = jnp.concatenate([fhi, flo, fhi], axis=1)
        basis_ref[:, t * 128 : (t + 1) * 128] = dot_nt(left, right)


def local(n_dom, n_rep, start_block, restriction_maps, send_rows, partner):
    z_count = n_dom // PLANE_DOM
    plane = PLANE_DOM * n_rep
    vmem = pl.BlockSpec(memory_space=pltpu.VMEM)
    hbm = pl.BlockSpec(memory_space=pltpu.HBM)
    inputs = [
        pltpu.with_memory_space_constraint(value, pltpu.HBM)
        for value in (start_block, restriction_maps, send_rows, partner)
    ]
    f_rows, gram = pl.pallas_call(
        functools.partial(filter_kernel, n_dom, n_rep),
        out_shape=[
            pltpu.VMEM((NODE_DEV, WIDE), F32),
            pltpu.VMEM((32, 128), F32),
        ],
        in_specs=[hbm, hbm, hbm, hbm],
        out_specs=[vmem, vmem],
        scratch_shapes=[
            pltpu.VMEM((NODE_DEV, WIDE), F32),
            pltpu.VMEM((STALK, STALK, ENDS), F32),
            pltpu.SMEM((1, SLOTS), jnp.int32),
            pltpu.VMEM((ENDS,), jnp.int32),
            pltpu.VMEM((ENDS, 128), F32),
            pltpu.VMEM((DEG, 64, 128), F32),
            pltpu.VMEM((DEG + 1, 64, 128), F32),
            pltpu.VMEM((256, ENDS), BF16),
            pltpu.VMEM((WIDE, 128), F32),
            pltpu.VMEM((WIDE, 256), BF16),
            pltpu.VMEM((WIDE, ENDS), F32),
            pltpu.VMEM((WIDE, 128), F32),
            pltpu.VMEM((SLOTS, 128), F32),
            pltpu.VMEM((64, 128), F32),
            pltpu.VMEM((2, SLOTS, WIDE), F32),
            pltpu.VMEM((SLOTS, 128), F32),
            pltpu.VMEM((2, SLOTS, WIDE), F32),
            pltpu.VMEM((WIDE, 128), F32),
            pltpu.VMEM((plane, 1, 128), F32),
            pltpu.VMEM((plane, 1, 128), F32),
            pltpu.VMEM((2, 1, 128), F32),
            pltpu.VMEM((z_count, 1, 128), F32),
            pltpu.VMEM((plane, 1, 128), F32),
            pltpu.SemaphoreType.DMA((2, 4)),
            pltpu.SemaphoreType.DMA((2, 2, 4)),
            pltpu.SemaphoreType.DMA((6,)),
            pltpu.SemaphoreType.DMA((4,)),
            pltpu.SemaphoreType.REGULAR,
            pltpu.SemaphoreType.REGULAR((2,)),
        ],
        compiler_params=pltpu.CompilerParams(
            collective_id=0, has_side_effects=True, vmem_limit_bytes=40 * 1024 * 1024
        ),
        name="filter_and_gram",
    )(*inputs)
    scaling = math.sqrt(NODE_DEV * STALK * n_dom * n_rep)
    return pl.pallas_call(
        functools.partial(solve_kernel, scaling),
        out_shape=[
            jax.ShapeDtypeStruct((NODE_DEV, WIDE), F32),
            jax.ShapeDtypeStruct((COLS, COLS), F32),
        ],
        in_specs=[vmem, vmem],
        out_specs=[vmem, vmem],
        compiler_params=pltpu.CompilerParams(vmem_limit_bytes=16 * 1024 * 1024),
        name="factor_and_solve",
    )(f_rows, gram)


def solution(mesh):
    n_dom, n_rep = mesh.shape["dom"], mesh.shape["rep"]
    in_specs = (
        P(("dom", "rep"), None),
        P(None, None, ("dom", "rep")),
        P(("dom", "rep"), None),
        P(("dom", "rep")),
    )
    out_specs = (P(("dom", "rep"), None), P())
    return jax.shard_map(
        functools.partial(local, n_dom, n_rep),
        mesh=mesh,
        in_specs=in_specs,
        out_specs=out_specs,
        check_vma=False,
    )
```

```python
import functools
import math

import jax
import jax.numpy as jnp
from jax import lax
from jax.experimental import pallas as pl
from jax.experimental.pallas import tpu as pltpu
from jax.sharding import PartitionSpec as P

MESH = pl.DeviceIdType.MESH
F32 = jnp.float32
BF16 = jnp.bfloat16

STALK = 8
COLS = 64
DEG = 6
NODE_DEV = 128
ENDS = NODE_DEV * DEG
BND = 16
SLOTS = 4 * BND
WIDE = STALK * COLS
PLANE_DOM = 8
CENTER = 21.0
RADIUS = 15.0


def split_two(x):
    hi = x.astype(BF16)
    lo = (x - hi.astype(F32)).astype(BF16)
    return hi, lo


def dot_nn(a, b):
    return lax.dot_general(a, b, (((1,), (0,)), ((), ())), preferred_element_type=F32)


def dot_nt(a, b):
    return lax.dot_general(a, b, (((1,), (1,)), ((), ())), preferred_element_type=F32)


def row_bcast(row):
    return jnp.broadcast_to(row, (8, row.shape[1]))


def drain(ref, count, sem):
    pltpu.make_async_copy(ref.at[pl.ds(0, count)], ref.at[pl.ds(0, count)], sem).wait()


def filter_kernel(
    n_dom,
    n_rep,
    start_hbm,
    maps_hbm,
    send_hbm,
    partner_hbm,
    f_ref,
    g_ref,
    start_ref,
    maps_ref,
    send_ref,
    partner_ref,
    rt_ref,
    rk_ref,
    coef_ref,
    ss_ref,
    vt_ref,
    vhl_ref,
    vx_ref,
    t_ref,
    rs_ref,
    ms_ref,
    vsend_ref,
    rrecv_ref,
    vrecv_ref,
    cpack_ref,
    gsl_ref,
    rsbuf_ref,
    zsend_ref,
    zbuf_ref,
    agbuf_ref,
    rsem,
    vsem,
    arsem,
    insem,
    xsem,
    zsem,
):
    d = lax.axis_index("dom")
    r = lax.axis_index("rep")
    z_count = n_dom // PLANE_DOM
    plane = PLANE_DOM * n_rep
    z = d // PLANE_DOM
    base = z * PLANE_DOM
    q = (d - base) * n_rep + r

    up = lax.rem(d + 1, n_dom)
    down = lax.rem(d + n_dom - 1, n_dom)
    nxt = lax.rem(r + 1, n_rep)
    prv = lax.rem(r + n_rep - 1, n_rep)
    neighbours = ((up, r), (down, r), (d, nxt), (d, prv))

    loads = [
        pltpu.make_async_copy(src, dst, insem.at[i])
        for i, (src, dst) in enumerate(
            (
                (send_hbm, send_ref),
                (start_hbm, start_ref),
                (maps_hbm, maps_ref),
                (partner_hbm, partner_ref),
            )
        )
    ]
    for load in loads:
        load.start()

    mine = d - base
    other_core = d + 1 - 2 * lax.rem(d, 2)
    x_peers = [(base + lax.rem(mine + 2 * i, PLANE_DOM), r) for i in range(1, PLANE_DOM // 2)]
    near = [(up, r), (down, r)]
    near += [(base + lax.rem(mine + i, PLANE_DOM), r) for i in range(1, PLANE_DOM)]
    for i in range(1, n_rep):
        turn = lax.rem(r + i, n_rep)
        near += [(d, turn), (other_core, turn)]

    def z_shift(by):
        return (lax.rem(z + z_count + by, z_count) * PLANE_DOM + mine, r)

    near += [z_shift(by) for by in (1, -1, 2, -2)]
    barrier = pltpu.get_barrier_semaphore()
    for peer in near:
        pl.semaphore_signal(barrier, inc=1, device_id=peer, device_id_type=MESH)

    loads[0].wait()
    loads[1].wait()
    for s in range(SLOTS):
        node = lax.div(send_ref[0, s], DEG)
        vsend_ref[0, s : s + 1, :] = start_ref[pl.ds(node, 1), :]
    loads[2].wait()
    loads[3].wait()

    part = jnp.broadcast_to(partner_ref[...].reshape(1, ENDS).astype(F32), (8, ENDS))
    end_id = lax.broadcasted_iota(jnp.int32, (8, ENDS), 1).astype(F32)
    node_id = jnp.floor((end_id + 0.5) * (1.0 / DEG))
    sub8 = lax.broadcasted_iota(jnp.int32, (8, ENDS), 0)
    extra = jnp.where(sub8 == 0, part, node_id)
    for t in range(DEG):
        cols = slice(t * 128, (t + 1) * 128)
        block = jnp.concatenate(
            [maps_ref[:, :, cols].reshape(64, 128), extra[:, cols], jnp.zeros((56, 128), F32)], axis=0
        )
        rt_ref[cols, :] = block.T

    for t in range(4):
        vt_ref[t * 128 : (t + 1) * 128, :] = start_ref[:, t * 128 : (t + 1) * 128].T

    for s in range(SLOTS):
        rs_ref[s : s + 1, :] = rt_ref[pl.ds(send_ref[0, s], 1), :]
    rs = rs_ref[...]
    lane = lax.broadcasted_iota(jnp.int32, (SLOTS, 128), 1).astype(F32)
    slot = lax.broadcasted_iota(jnp.int32, (SLOTS, 1), 0)
    expect = (ENDS + jnp.bitwise_xor(slot, BND)).astype(F32)
    used = rs[:, 64:65] == expect
    hot = jnp.where(jnp.logical_and(rs[:, 65:66] == lane, used), 1.0, 0.0).astype(BF16)
    hot_wide = jnp.concatenate([hot, hot], axis=1)
    hot_tall = jnp.concatenate([hot, hot], axis=0)

    sub = lax.broadcasted_iota(jnp.int32, (128, 128), 0).astype(F32)
    rhl = []
    kk_rows = []
    for k in range(DEG):
        rk = rt_ref[pl.ds(k, NODE_DEV, stride=DEG), :].T
        rk_ref[k] = rk[0:64, :]
        p = rk[64:65, :]
        node = jnp.floor((p + 0.5) * (1.0 / DEG))
        kk_rows.append(p - DEG * node)
        one = jnp.where(sub == node, 1.0, 0.0).astype(BF16)
        ss_ref[0:128, k * 128 : (k + 1) * 128] = one
        ss_ref[128:256, k * 128 : (k + 1) * 128] = one
        hi, lo = split_two(rk[0:64, :])
        rhl.append(jnp.concatenate([hi, lo], axis=1))
    rhl = jnp.concatenate(rhl, axis=0)

    def value_copies(step):
        return [
            pltpu.make_async_remote_copy(
                src_ref=vsend_ref.at[step, pl.ds(k * BND, BND), :],
                dst_ref=vrecv_ref.at[step, pl.ds((k ^ 1) * BND, BND), :],
                send_sem=vsem.at[0, step, k],
                recv_sem=vsem.at[1, step, k ^ 1],
                device_id=neighbours[k],
                device_id_type=MESH,
            )
            for k in range(4)
        ]

    map_copies = [
        pltpu.make_async_remote_copy(
            src_ref=rs_ref.at[pl.ds(k * BND, BND), :],
            dst_ref=rrecv_ref.at[pl.ds((k ^ 1) * BND, BND), :],
            send_sem=rsem.at[0, k],
            recv_sem=rsem.at[1, k ^ 1],
            device_id=neighbours[k],
            device_id_type=MESH,
        )
        for k in range(4)
    ]

    pl.semaphore_wait(barrier, len(near))
    first_copies = value_copies(0)
    for copy in first_copies + map_copies:
        copy.start()
    for peer in x_peers:
        pl.semaphore_signal(xsem, inc=1, device_id=peer, device_id_type=MESH)
    for by in (2, -2):
        pl.semaphore_signal(zsem.at[0], inc=1, device_id=z_shift(by), device_id_type=MESH)

    sub_b = lax.broadcasted_iota(jnp.int32, (8, 128), 0)
    own = [jnp.zeros((8, 128), F32) for _ in range(STALK)]
    for j in range(3):
        far = dot_nn(rhl, ss_ref[:, j * 256 : (j + 1) * 256])
        for h in range(2):
            k = 2 * j + h
            mate_map = far[0:64, h * 128 : (h + 1) * 128]
            for m in range(1, DEG):
                mate_map = jnp.where(
                    kk_rows[k] == float(m),
                    far[m * 64 : (m + 1) * 64, h * 128 : (h + 1) * 128],
                    mate_map,
                )
            for a2 in range(STALK):
                acc = jnp.zeros((8, 128), F32)
                for a in range(STALK):
                    coef = row_bcast(rk_ref[k, a * 8 + a2 : a * 8 + a2 + 1, :])
                    acc = acc + coef * mate_map[a * 8 : (a + 1) * 8, :]
                    own[a2] = own[a2] + coef * rk_ref[k, a * 8 : (a + 1) * 8, :]
                coef_ref[k, a2 * 8 : (a2 + 1) * 8, :] = acc * (-1.0 / RADIUS)
    for a2 in range(STALK):
        coef_ref[DEG, a2 * 8 : (a2 + 1) * 8, :] = (
            own[a2] - jnp.where(sub_b == a2, CENTER, 0.0)
        ) * (1.0 / RADIUS)

    def spread(values_ref):
        hi, lo = split_two(values_ref[...])
        vhl_ref[:, 0:128] = hi
        vhl_ref[:, 128:256] = lo

    def recv_waits(copies):
        for copy in copies:
            copy.wait_recv()

    def outgoing(step):
        vsend_ref[step] = dot_nt(hot_wide, vhl_ref[...])

    def local_part(own_ref, out_ref, combine):
        for j in range(3):
            vx_ref[:, j * 256 : (j + 1) * 256] = dot_nn(
                vhl_ref[...], ss_ref[:, j * 256 : (j + 1) * 256]
            )

        def columns(i, carry):
            acc = [[jnp.zeros((8, 128), F32) for _ in range(2)] for _ in range(STALK)]
            for k in range(DEG + 1):
                for b in range(STALK):
                    vals = []
                    for h in range(2):
                        at = pl.ds(pl.multiple_of(b * COLS + i * 16 + h * 8, 8), 8)
                        if k == DEG:
                            vals.append(own_ref[at, :])
                        else:
                            vals.append(vx_ref[at, k * 128 : (k + 1) * 128])
                    for a2 in range(STALK):
                        coef = row_bcast(coef_ref[k, a2 * 8 + b : a2 * 8 + b + 1, :])
                        for h in range(2):
                            acc[a2][h] = acc[a2][h] + coef * vals[h]
            for a2 in range(STALK):
                for h in range(2):
                    at = pl.ds(pl.multiple_of(a2 * COLS + i * 16 + h * 8, 8), 8)
                    out_ref[at, :] = combine(acc[a2][h], at)
            return carry

        lax.fori_loop(0, 4, columns, 0)

    def remote_part(step):
        low = lax.broadcasted_iota(jnp.int32, (8, 128), 1) < SLOTS
        turned = []
        for t in range(4):
            block = vrecv_ref[step, :, t * 128 : (t + 1) * 128]
            turned.append(jnp.concatenate([block, block], axis=0).T)
        for cg in range(8):
            acc = [jnp.zeros((8, 128), F32) for _ in range(STALK)]
            for b in range(STALK):
                row = b * COLS + cg * 8
                val = turned[row // 128][row % 128 : row % 128 + 8, :]
                for a2 in range(STALK):
                    coef = row_bcast(ms_ref[a2 * 8 + b : a2 * 8 + b + 1, :])
                    acc[a2] = acc[a2] + coef * val
            for a2 in range(STALK):
                hi = acc[a2].astype(BF16).astype(F32)
                cpack_ref[a2 * COLS + cg * 8 : a2 * COLS + cg * 8 + 8, :] = jnp.where(
                    low, hi, acc[a2] - hi
                )
        return dot_nn(cpack_ref[...].astype(BF16), hot_tall)

    spread(vt_ref)
    local_part(vt_ref, t_ref, lambda acc, at: acc)

    recv_waits(map_copies)
    far_maps = jnp.concatenate([rrecv_ref[...], rrecv_ref[...]], axis=0).T
    own_maps = jnp.concatenate([rs, rs], axis=0).T
    for a2 in range(STALK):
        acc = jnp.zeros((8, 128), F32)
        for a in range(STALK):
            acc = acc + row_bcast(own_maps[a * 8 + a2 : a * 8 + a2 + 1, :]) * (
                far_maps[a * 8 : (a + 1) * 8, :]
            )
        ms_ref[a2 * 8 : (a2 + 1) * 8, :] = acc * (-1.0 / RADIUS)
    recv_waits(first_copies)
    t_ref[...] = t_ref[...] + remote_part(0)

    spread(t_ref)
    outgoing(1)
    second_copies = value_copies(1)
    for copy in second_copies:
        copy.start()
    pl.semaphore_wait(zsem.at[0], 2)
    for by in (4, -4):
        pl.semaphore_signal(zsem.at[1], inc=1, device_id=z_shift(by), device_id_type=MESH)
    local_part(t_ref, vt_ref, lambda acc, at: 2.0 * acc - vt_ref[at, :])
    recv_waits(second_copies)
    vt_ref[...] = vt_ref[...] + 2.0 * remote_part(1)

    spread(vt_ref)
    tall = jnp.concatenate(
        [
            jnp.concatenate(
                [vhl_ref[a * COLS : (a + 1) * COLS, h * 128 : (h + 1) * 128] for a in range(STALK)],
                axis=1,
            )
            for h in range(2)
        ],
        axis=0,
    )
    prod = dot_nt(tall, tall)
    half = prod[0:64, :] + prod[64:128, :]
    both = half + pltpu.roll(half, 64, 1)
    lane32 = lax.broadcasted_iota(jnp.int32, (32, 128), 1)
    packed = jnp.where(lane32 < 64, both[0:32, :], both[32:64, :])
    share = 32 // PLANE_DOM
    for i in range(PLANE_DOM):
        gsl_ref[i] = packed[i * share : (i + 1) * share, :]

    pl.semaphore_wait(xsem, len(x_peers))
    chips_x = PLANE_DOM // 2
    x, c = mine // 2, lax.rem(mine, 2)

    def ring(step, count):
        return min(step, count - step)

    offsets = [
        (dx, dy, dc) for dx in range(chips_x) for dy in range(n_rep) for dc in range(2)
    ][1:]
    offsets.sort(key=lambda o: -(ring(o[0], chips_x) + ring(o[1], n_rep)))

    def plane_peer(dx, dy, dc):
        to = lax.rem(x + dx, chips_x) * 2 + lax.rem(c + dc, 2)
        return to, (base + to, lax.rem(r + dy, n_rep))

    for offset in offsets:
        to, peer = plane_peer(*offset)
        pltpu.make_async_remote_copy(
            src_ref=gsl_ref.at[to],
            dst_ref=rsbuf_ref.at[q],
            send_sem=arsem.at[0],
            recv_sem=arsem.at[1],
            device_id=peer,
            device_id_type=MESH,
        ).start()
    rsbuf_ref[q] = gsl_ref[mine]
    for t in range(4):
        f_ref[:, t * 128 : (t + 1) * 128] = vt_ref[t * 128 : (t + 1) * 128, :].T
    pl.semaphore_wait(zsem.at[1], 2)
    drain(rsbuf_ref, plane - 1, arsem.at[1])

    def total(ref, count):
        rows = [ref[i] for i in range(count)]
        while len(rows) > 1:
            rows = [rows[i] + rows[i + 1] for i in range(0, len(rows) - 1, 2)] + (
                [rows[-1]] if len(rows) % 2 else []
            )
        return rows[0]

    part_sum = total(rsbuf_ref, plane)
    zsend_ref[0] = part_sum
    for by in sorted(range(1, z_count), key=lambda step: -ring(step, z_count)):
        pltpu.make_async_remote_copy(
            src_ref=zsend_ref.at[0],
            dst_ref=zbuf_ref.at[z],
            send_sem=arsem.at[2],
            recv_sem=arsem.at[3],
            device_id=z_shift(by),
            device_id_type=MESH,
        ).start()
    zbuf_ref[z] = part_sum
    drain(zbuf_ref, z_count - 1, arsem.at[3])
    slice_sum = total(zbuf_ref, z_count)
    zsend_ref[1] = slice_sum
    for offset in offsets:
        if offset[1] == 0:
            pltpu.make_async_remote_copy(
                src_ref=zsend_ref.at[1],
                dst_ref=agbuf_ref.at[mine],
                send_sem=arsem.at[4],
                recv_sem=arsem.at[5],
                device_id=plane_peer(*offset)[1],
                device_id_type=MESH,
            ).start()
    agbuf_ref[mine] = slice_sum
    drain(agbuf_ref, PLANE_DOM - 1, arsem.at[5])
    for i in range(PLANE_DOM):
        g_ref[i * share : (i + 1) * share, :] = agbuf_ref[i]

    for copies in (map_copies, first_copies, second_copies):
        for copy in copies:
            copy.wait_send()
    drain(rsbuf_ref, plane - 1, arsem.at[0])
    drain(zbuf_ref, z_count - 1, arsem.at[2])
    drain(agbuf_ref, PLANE_DOM - 1, arsem.at[4])


def full8(value):
    return jnp.broadcast_to(value, (8, 128))


def eliminate(work):
    sub = lax.broadcasted_iota(jnp.int32, (8, 128), 0)
    for g in range(8):
        cols = [[full8(work[i][:, g * 8 + j : g * 8 + j + 1]) for i in range(g, 8)] for j in range(8)]
        rows = [full8(work[g][j : j + 1, :]) for j in range(8)]
        block = [[full8(cols[b][0][a : a + 1, :]) for b in range(a + 1)] for a in range(8)]
        mult = [[None] * 8 for _ in range(8)]
        inverse = []
        for j in range(8):
            inverse.append(1.0 / block[j][j])
            for a in range(j + 1, 8):
                mult[a][j] = block[a][j] * inverse[j]
            for a in range(j + 1, 8):
                for b in range(j + 1, a + 1):
                    block[a][b] = block[a][b] - mult[a][j] * block[b][j]
                rows[a] = rows[a] - mult[a][j] * rows[j]
        scaled = [rows[j] * inverse[j] for j in range(8)]
        done = rows[0]
        for j in range(1, 8):
            done = jnp.where(sub == j, rows[j], done)
        work[g] = done
        for i in range(g + 1, 8):
            col = [cols[j][i - g] for j in range(8)]
            for j in range(8):
                for t in range(j):
                    col[j] = col[j] - col[t] * mult[j][t]
            terms = [col[j] * scaled[j] for j in range(8)]
            while len(terms) > 1:
                terms = [terms[t] + terms[t + 1] for t in range(0, len(terms), 2)]
            work[i] = work[i] - terms[0]


def solve_kernel(scaling, f_ref, g_ref, basis_hbm, triangle_ref, basis_ref, sem):
    g = g_ref[...]
    turned = pltpu.roll(g, 64, 1)
    lane32 = lax.broadcasted_iota(jnp.int32, (32, 128), 1)
    row32 = lax.broadcasted_iota(jnp.int32, (32, 128), 0)
    top = jnp.where(lane32 < 64, g, jnp.where(lane32 - 64 == row32, 1.0, 0.0))
    bottom = jnp.where(lane32 < 64, turned, jnp.where(lane32 - 96 == row32, 1.0, 0.0))
    work = [top[i * 8 : (i + 1) * 8, :] for i in range(4)] + [
        bottom[i * 8 : (i + 1) * 8, :] for i in range(4)
    ]
    eliminate(work)
    sub = lax.broadcasted_iota(jnp.int32, (8, 128), 0)
    lane = lax.broadcasted_iota(jnp.int32, (8, 128), 1)
    rows_out = []
    for i in range(8):
        diag = jnp.sum(jnp.where(lane == sub + 8 * i, work[i], 0.0), axis=1, keepdims=True)
        rows_out.append(work[i] * lax.rsqrt(diag))
    full = jnp.concatenate(rows_out, axis=0)
    lane64 = lax.broadcasted_iota(jnp.int32, (COLS, 128), 1)
    row64 = lax.broadcasted_iota(jnp.int32, (COLS, 128), 0)
    triangle_ref[...] = jnp.where(lane64 >= row64, full * (1.0 / scaling), 0.0)[:, 0:COLS]
    full = full * scaling
    block = jnp.concatenate(
        [
            jnp.where(lane64 < 64, pltpu.roll(full, 64, 1), 0.0),
            jnp.where(lane64 < 64, 0.0, full),
        ],
        axis=0,
    )
    bhi, blo = split_two(block)
    right = jnp.concatenate([bhi, bhi, blo], axis=1)
    for t in range(4):
        fhi, flo = split_two(f_ref[:, t * 128 : (t + 1) * 128])
        left = jnp.concatenate([fhi, flo, fhi], axis=1)
        basis_ref[t] = dot_nt(left, right)
        pltpu.make_async_copy(
            basis_ref.at[t], basis_hbm.at[:, pl.ds(t * 128, 128)], sem.at[t]
        ).start()
    for t in range(4):
        pltpu.make_async_copy(
            basis_ref.at[t], basis_hbm.at[:, pl.ds(t * 128, 128)], sem.at[t]
        ).wait()


def local(n_dom, n_rep, start_block, restriction_maps, send_rows, partner):
    z_count = n_dom // PLANE_DOM
    plane = PLANE_DOM * n_rep
    share = 32 // PLANE_DOM
    vmem = pl.BlockSpec(memory_space=pltpu.VMEM)
    hbm = pl.BlockSpec(memory_space=pltpu.HBM)
    inputs = [
        pltpu.with_memory_space_constraint(value, pltpu.HBM)
        for value in (start_block, restriction_maps, send_rows, partner)
    ]
    f_rows, gram = pl.pallas_call(
        functools.partial(filter_kernel, n_dom, n_rep),
        out_shape=[
            pltpu.VMEM((NODE_DEV, WIDE), F32),
            pltpu.VMEM((32, 128), F32),
        ],
        in_specs=[hbm, hbm, hbm, hbm],
        out_specs=[vmem, vmem],
        scratch_shapes=[
            pltpu.VMEM((NODE_DEV, WIDE), F32),
            pltpu.VMEM((STALK, STALK, ENDS), F32),
            pltpu.SMEM((1, SLOTS), jnp.int32),
            pltpu.VMEM((ENDS,), jnp.int32),
            pltpu.VMEM((ENDS, 128), F32),
            pltpu.VMEM((DEG, 64, 128), F32),
            pltpu.VMEM((DEG + 1, 64, 128), F32),
            pltpu.VMEM((256, ENDS), BF16),
            pltpu.VMEM((WIDE, 128), F32),
            pltpu.VMEM((WIDE, 256), BF16),
            pltpu.VMEM((WIDE, ENDS), F32),
            pltpu.VMEM((WIDE, 128), F32),
            pltpu.VMEM((SLOTS, 128), F32),
            pltpu.VMEM((64, 128), F32),
            pltpu.VMEM((2, SLOTS, WIDE), F32),
            pltpu.VMEM((SLOTS, 128), F32),
            pltpu.VMEM((2, SLOTS, WIDE), F32),
            pltpu.VMEM((WIDE, 128), F32),
            pltpu.VMEM((PLANE_DOM, share, 128), F32),
            pltpu.VMEM((plane, share, 128), F32),
            pltpu.VMEM((2, share, 128), F32),
            pltpu.VMEM((z_count, share, 128), F32),
            pltpu.VMEM((PLANE_DOM, share, 128), F32),
            pltpu.SemaphoreType.DMA((2, 4)),
            pltpu.SemaphoreType.DMA((2, 2, 4)),
            pltpu.SemaphoreType.DMA((6,)),
            pltpu.SemaphoreType.DMA((4,)),
            pltpu.SemaphoreType.REGULAR,
            pltpu.SemaphoreType.REGULAR((2,)),
        ],
        compiler_params=pltpu.CompilerParams(
            collective_id=0, has_side_effects=True, vmem_limit_bytes=40 * 1024 * 1024
        ),
        name="filter_and_gram",
    )(*inputs)
    scaling = math.sqrt(NODE_DEV * STALK * n_dom * n_rep)
    return pl.pallas_call(
        functools.partial(solve_kernel, scaling),
        out_shape=[
            jax.ShapeDtypeStruct((NODE_DEV, WIDE), F32),
            jax.ShapeDtypeStruct((COLS, COLS), F32),
        ],
        in_specs=[vmem, vmem],
        out_specs=[hbm, vmem],
        scratch_shapes=[pltpu.VMEM((4, NODE_DEV, 128), F32), pltpu.SemaphoreType.DMA((4,))],
        compiler_params=pltpu.CompilerParams(vmem_limit_bytes=16 * 1024 * 1024),
        name="factor_and_solve",
    )(f_rows, gram)


def solution(mesh):
    n_dom, n_rep = mesh.shape["dom"], mesh.shape["rep"]
    in_specs = (
        P(("dom", "rep"), None),
        P(None, None, ("dom", "rep")),
        P(("dom", "rep"), None),
        P(("dom", "rep")),
    )
    out_specs = (P(("dom", "rep"), None), P())
    return jax.shard_map(
        functools.partial(local, n_dom, n_rep),
        mesh=mesh,
        in_specs=in_specs,
        out_specs=out_specs,
        check_vma=False,
    )
```

```python
import functools
import math

import jax
import jax.numpy as jnp
from jax import lax
from jax.experimental import pallas as pl
from jax.experimental.pallas import tpu as pltpu
from jax.sharding import PartitionSpec as P

MESH = pl.DeviceIdType.MESH
F32 = jnp.float32
BF16 = jnp.bfloat16

STALK = 8
COLS = 64
DEG = 6
NODE_DEV = 128
ENDS = NODE_DEV * DEG
BND = 16
SLOTS = 4 * BND
WIDE = STALK * COLS
PLANE_DOM = 8
CENTER = 21.0
RADIUS = 15.0


def split_two(x):
    hi = x.astype(BF16)
    lo = (x - hi.astype(F32)).astype(BF16)
    return hi, lo


def dot_nn(a, b):
    return lax.dot_general(a, b, (((1,), (0,)), ((), ())), preferred_element_type=F32)


def dot_nt(a, b):
    return lax.dot_general(a, b, (((1,), (1,)), ((), ())), preferred_element_type=F32)


def row_bcast(row):
    return jnp.broadcast_to(row, (8, row.shape[1]))


def drain(ref, count, sem):
    pltpu.make_async_copy(ref.at[pl.ds(0, count)], ref.at[pl.ds(0, count)], sem).wait()


def filter_kernel(
    n_dom,
    n_rep,
    start_hbm,
    maps_hbm,
    send_hbm,
    partner_hbm,
    f_ref,
    g_ref,
    start_ref,
    maps_ref,
    send_ref,
    partner_ref,
    rt_ref,
    rk_ref,
    coef_ref,
    ss_ref,
    vt_ref,
    vhl_ref,
    vx_ref,
    t_ref,
    rs_ref,
    ms_ref,
    vsend_ref,
    rrecv_ref,
    vrecv_ref,
    cpack_ref,
    gsl_ref,
    rsbuf_ref,
    zsend_ref,
    zbuf_ref,
    agbuf_ref,
    rsem,
    vsem,
    arsem,
    insem,
    xsem,
    zsem,
):
    d = lax.axis_index("dom")
    r = lax.axis_index("rep")
    z_count = n_dom // PLANE_DOM
    plane = PLANE_DOM * n_rep
    z = d // PLANE_DOM
    base = z * PLANE_DOM
    q = (d - base) * n_rep + r

    up = lax.rem(d + 1, n_dom)
    down = lax.rem(d + n_dom - 1, n_dom)
    nxt = lax.rem(r + 1, n_rep)
    prv = lax.rem(r + n_rep - 1, n_rep)
    neighbours = ((up, r), (down, r), (d, nxt), (d, prv))

    loads = [
        pltpu.make_async_copy(src, dst, insem.at[i])
        for i, (src, dst) in enumerate(
            (
                (send_hbm, send_ref),
                (start_hbm, start_ref),
                (maps_hbm, maps_ref),
                (partner_hbm, partner_ref),
            )
        )
    ]
    mine = d - base
    other_core = d + 1 - 2 * lax.rem(d, 2)
    x_peers = [(base + lax.rem(mine + 2 * i, PLANE_DOM), r) for i in range(1, PLANE_DOM // 2)]
    near = [(up, r), (down, r)]

    def z_shift(by):
        return (lax.rem(z + z_count + by, z_count) * PLANE_DOM + mine, r)

    near += [z_shift(by) for by in (2, -2)]
    for i in sorted(range(1, n_rep), key=lambda i: -min(i, n_rep - i)):
        turn = lax.rem(r + i, n_rep)
        near += [(d, turn), (other_core, turn)]
    near += [
        (base + lax.rem(mine + i, PLANE_DOM), r)
        for i in sorted(range(1, PLANE_DOM), key=lambda i: -min(i, PLANE_DOM - i))
    ]
    near += [z_shift(by) for by in (1, -1)]
    barrier = pltpu.get_barrier_semaphore()
    for peer in near:
        pl.semaphore_signal(barrier, inc=1, device_id=peer, device_id_type=MESH)

    for load in loads:
        load.start()

    loads[0].wait()
    loads[1].wait()
    for s in range(SLOTS):
        node = lax.div(send_ref[0, s], DEG)
        vsend_ref[0, s : s + 1, :] = start_ref[pl.ds(node, 1), :]
    loads[2].wait()
    loads[3].wait()

    part = jnp.broadcast_to(partner_ref[...].reshape(1, ENDS).astype(F32), (8, ENDS))
    end_id = lax.broadcasted_iota(jnp.int32, (8, ENDS), 1).astype(F32)
    node_id = jnp.floor((end_id + 0.5) * (1.0 / DEG))
    sub8 = lax.broadcasted_iota(jnp.int32, (8, ENDS), 0)
    extra = jnp.where(sub8 == 0, part, node_id)
    for t in range(DEG):
        cols = slice(t * 128, (t + 1) * 128)
        block = jnp.concatenate(
            [maps_ref[:, :, cols].reshape(64, 128), extra[:, cols], jnp.zeros((56, 128), F32)], axis=0
        )
        rt_ref[cols, :] = block.T

    for t in range(4):
        vt_ref[t * 128 : (t + 1) * 128, :] = start_ref[:, t * 128 : (t + 1) * 128].T

    for s in range(SLOTS):
        rs_ref[s : s + 1, :] = rt_ref[pl.ds(send_ref[0, s], 1), :]
    rs = rs_ref[...]
    lane = lax.broadcasted_iota(jnp.int32, (SLOTS, 128), 1).astype(F32)
    slot = lax.broadcasted_iota(jnp.int32, (SLOTS, 1), 0)
    expect = (ENDS + jnp.bitwise_xor(slot, BND)).astype(F32)
    used = rs[:, 64:65] == expect
    hot = jnp.where(jnp.logical_and(rs[:, 65:66] == lane, used), 1.0, 0.0).astype(BF16)
    hot_wide = jnp.concatenate([hot, hot], axis=1)
    hot_tall = jnp.concatenate([hot, hot], axis=0)
    same = dot_nt(hot, hot).astype(BF16)
    same_wide = jnp.concatenate([same, same], axis=1)

    sub = lax.broadcasted_iota(jnp.int32, (128, 128), 0).astype(F32)
    rhl = []
    kk_rows = []
    for k in range(DEG):
        rk = rt_ref[pl.ds(k, NODE_DEV, stride=DEG), :].T
        rk_ref[k] = rk[0:64, :]
        p = rk[64:65, :]
        node = jnp.floor((p + 0.5) * (1.0 / DEG))
        kk_rows.append(p - DEG * node)
        one = jnp.where(sub == node, 1.0, 0.0).astype(BF16)
        ss_ref[0:128, k * 128 : (k + 1) * 128] = one
        ss_ref[128:256, k * 128 : (k + 1) * 128] = one
        hi, lo = split_two(rk[0:64, :])
        rhl.append(jnp.concatenate([hi, lo], axis=1))
    rhl = jnp.concatenate(rhl, axis=0)

    def value_copies(step):
        return [
            pltpu.make_async_remote_copy(
                src_ref=vsend_ref.at[step, pl.ds(k * BND, BND), :],
                dst_ref=vrecv_ref.at[step, pl.ds((k ^ 1) * BND, BND), :],
                send_sem=vsem.at[0, step, k],
                recv_sem=vsem.at[1, step, k ^ 1],
                device_id=neighbours[k],
                device_id_type=MESH,
            )
            for k in range(4)
        ]

    map_copies = [
        pltpu.make_async_remote_copy(
            src_ref=rs_ref.at[pl.ds(k * BND, BND), :],
            dst_ref=rrecv_ref.at[pl.ds((k ^ 1) * BND, BND), :],
            send_sem=rsem.at[0, k],
            recv_sem=rsem.at[1, k ^ 1],
            device_id=neighbours[k],
            device_id_type=MESH,
        )
        for k in range(4)
    ]

    pl.semaphore_wait(barrier, len(near))
    first_copies = value_copies(0)
    for copy in map_copies + first_copies:
        copy.start()
    for peer in x_peers:
        pl.semaphore_signal(xsem, inc=1, device_id=peer, device_id_type=MESH)
    for by in (2, -2):
        pl.semaphore_signal(zsem.at[0], inc=1, device_id=z_shift(by), device_id_type=MESH)

    sub_b = lax.broadcasted_iota(jnp.int32, (8, 128), 0)
    own = [jnp.zeros((8, 128), F32) for _ in range(STALK)]
    for j in range(3):
        far = dot_nn(rhl, ss_ref[:, j * 256 : (j + 1) * 256])
        for h in range(2):
            k = 2 * j + h
            mate_map = far[0:64, h * 128 : (h + 1) * 128]
            for m in range(1, DEG):
                mate_map = jnp.where(
                    kk_rows[k] == float(m),
                    far[m * 64 : (m + 1) * 64, h * 128 : (h + 1) * 128],
                    mate_map,
                )
            for a2 in range(STALK):
                acc = jnp.zeros((8, 128), F32)
                for a in range(STALK):
                    coef = row_bcast(rk_ref[k, a * 8 + a2 : a * 8 + a2 + 1, :])
                    acc = acc + coef * mate_map[a * 8 : (a + 1) * 8, :]
                    own[a2] = own[a2] + coef * rk_ref[k, a * 8 : (a + 1) * 8, :]
                coef_ref[k, a2 * 8 : (a2 + 1) * 8, :] = acc * (-1.0 / RADIUS)
    for a2 in range(STALK):
        coef_ref[DEG, a2 * 8 : (a2 + 1) * 8, :] = (
            own[a2] - jnp.where(sub_b == a2, CENTER, 0.0)
        ) * (1.0 / RADIUS)

    def spread(values_ref):
        hi, lo = split_two(values_ref[...])
        vhl_ref[:, 0:128] = hi
        vhl_ref[:, 128:256] = lo

    def recv_waits(copies):
        for copy in copies:
            copy.wait_recv()

    def local_part(own_ref, out_ref, combine):
        for j in range(3):
            vx_ref[:, j * 256 : (j + 1) * 256] = dot_nn(
                vhl_ref[...], ss_ref[:, j * 256 : (j + 1) * 256]
            )

        def columns(i, carry):
            acc = [[jnp.zeros((8, 128), F32) for _ in range(2)] for _ in range(STALK)]
            for k in range(DEG + 1):
                for b in range(STALK):
                    vals = []
                    for h in range(2):
                        at = pl.ds(pl.multiple_of(b * COLS + i * 16 + h * 8, 8), 8)
                        if k == DEG:
                            vals.append(own_ref[at, :])
                        else:
                            vals.append(vx_ref[at, k * 128 : (k + 1) * 128])
                    for a2 in range(STALK):
                        coef = row_bcast(coef_ref[k, a2 * 8 + b : a2 * 8 + b + 1, :])
                        for h in range(2):
                            acc[a2][h] = acc[a2][h] + coef * vals[h]
            for a2 in range(STALK):
                for h in range(2):
                    at = pl.ds(pl.multiple_of(a2 * COLS + i * 16 + h * 8, 8), 8)
                    out_ref[at, :] = combine(acc[a2][h], at)
            return carry

        lax.fori_loop(0, 4, columns, 0)

    def remote_part(step):
        low = lax.broadcasted_iota(jnp.int32, (8, 128), 1) < SLOTS
        turned = []
        for t in range(4):
            block = vrecv_ref[step, :, t * 128 : (t + 1) * 128]
            turned.append(jnp.concatenate([block, block], axis=0).T)
        for cg in range(8):
            acc = [jnp.zeros((8, 128), F32) for _ in range(STALK)]
            for b in range(STALK):
                row = b * COLS + cg * 8
                val = turned[row // 128][row % 128 : row % 128 + 8, :]
                for a2 in range(STALK):
                    coef = row_bcast(ms_ref[a2 * 8 + b : a2 * 8 + b + 1, :])
                    acc[a2] = acc[a2] + coef * val
            for a2 in range(STALK):
                hi = acc[a2].astype(BF16).astype(F32)
                cpack_ref[a2 * COLS + cg * 8 : a2 * COLS + cg * 8 + 8, :] = jnp.where(
                    low, hi, acc[a2] - hi
                )
        return cpack_ref[...].astype(BF16)

    spread(vt_ref)
    local_part(vt_ref, t_ref, lambda acc, at: acc)
    hi, lo = split_two(t_ref[...])
    vsend_ref[1] = dot_nt(hot_wide, jnp.concatenate([hi, lo], axis=1))

    recv_waits(map_copies)
    far_maps = jnp.concatenate([rrecv_ref[...], rrecv_ref[...]], axis=0).T
    own_maps = jnp.concatenate([rs, rs], axis=0).T
    for a2 in range(STALK):
        acc = jnp.zeros((8, 128), F32)
        for a in range(STALK):
            acc = acc + row_bcast(own_maps[a * 8 + a2 : a * 8 + a2 + 1, :]) * (
                far_maps[a * 8 : (a + 1) * 8, :]
            )
        ms_ref[a2 * 8 : (a2 + 1) * 8, :] = acc * (-1.0 / RADIUS)
    recv_waits(first_copies)
    packed_far = remote_part(0)
    vsend_ref[1] = vsend_ref[1] + dot_nt(same_wide, packed_far)
    second_copies = value_copies(1)
    for copy in second_copies:
        copy.start()

    t_ref[...] = t_ref[...] + dot_nn(packed_far, hot_tall)
    spread(t_ref)
    pl.semaphore_wait(zsem.at[0], 2)
    for by in (4, -4):
        pl.semaphore_signal(zsem.at[1], inc=1, device_id=z_shift(by), device_id_type=MESH)
    local_part(t_ref, vt_ref, lambda acc, at: 2.0 * acc - vt_ref[at, :])
    recv_waits(second_copies)
    vt_ref[...] = vt_ref[...] + 2.0 * dot_nn(remote_part(1), hot_tall)

    spread(vt_ref)
    tall = jnp.concatenate(
        [
            jnp.concatenate(
                [vhl_ref[a * COLS : (a + 1) * COLS, h * 128 : (h + 1) * 128] for a in range(STALK)],
                axis=1,
            )
            for h in range(2)
        ],
        axis=0,
    )
    prod = dot_nt(tall, tall)
    half = prod[0:64, :] + prod[64:128, :]
    both = half + pltpu.roll(half, 64, 1)
    lane32 = lax.broadcasted_iota(jnp.int32, (32, 128), 1)
    packed = jnp.where(lane32 < 64, both[0:32, :], both[32:64, :])
    share = 32 // PLANE_DOM
    for i in range(PLANE_DOM):
        gsl_ref[i] = packed[i * share : (i + 1) * share, :]

    pl.semaphore_wait(xsem, len(x_peers))
    chips_x = PLANE_DOM // 2
    x, c = mine // 2, lax.rem(mine, 2)

    def ring(step, count):
        return min(step, count - step)

    offsets = [
        (dx, dy, dc) for dx in range(chips_x) for dy in range(n_rep) for dc in range(2)
    ][1:]
    offsets.sort(key=lambda o: -(ring(o[0], chips_x) + ring(o[1], n_rep)))

    def plane_peer(dx, dy, dc):
        to = lax.rem(x + dx, chips_x) * 2 + lax.rem(c + dc, 2)
        return to, (base + to, lax.rem(r + dy, n_rep))

    for offset in offsets:
        to, peer = plane_peer(*offset)
        pltpu.make_async_remote_copy(
            src_ref=gsl_ref.at[to],
            dst_ref=rsbuf_ref.at[q],
            send_sem=arsem.at[0],
            recv_sem=arsem.at[1],
            device_id=peer,
            device_id_type=MESH,
        ).start()
    rsbuf_ref[q] = gsl_ref[mine]
    for t in range(4):
        f_ref[:, t * 128 : (t + 1) * 128] = vt_ref[t * 128 : (t + 1) * 128, :].T
    pl.semaphore_wait(zsem.at[1], 2)
    drain(rsbuf_ref, plane - 1, arsem.at[1])

    def total(ref, count):
        rows = [ref[i] for i in range(count)]
        while len(rows) > 1:
            rows = [rows[i] + rows[i + 1] for i in range(0, len(rows) - 1, 2)] + (
                [rows[-1]] if len(rows) % 2 else []
            )
        return rows[0]

    part_sum = total(rsbuf_ref, plane)
    zsend_ref[0] = part_sum
    for by in sorted(range(1, z_count), key=lambda step: -ring(step, z_count)):
        pltpu.make_async_remote_copy(
            src_ref=zsend_ref.at[0],
            dst_ref=zbuf_ref.at[z],
            send_sem=arsem.at[2],
            recv_sem=arsem.at[3],
            device_id=z_shift(by),
            device_id_type=MESH,
        ).start()
    zbuf_ref[z] = part_sum
    drain(zbuf_ref, z_count - 1, arsem.at[3])
    slice_sum = total(zbuf_ref, z_count)
    zsend_ref[1] = slice_sum
    for offset in offsets:
        if offset[1] == 0:
            pltpu.make_async_remote_copy(
                src_ref=zsend_ref.at[1],
                dst_ref=agbuf_ref.at[mine],
                send_sem=arsem.at[4],
                recv_sem=arsem.at[5],
                device_id=plane_peer(*offset)[1],
                device_id_type=MESH,
            ).start()
    agbuf_ref[mine] = slice_sum
    drain(agbuf_ref, PLANE_DOM - 1, arsem.at[5])
    for i in range(PLANE_DOM):
        g_ref[i * share : (i + 1) * share, :] = agbuf_ref[i]

    for copies in (map_copies, first_copies, second_copies):
        for copy in copies:
            copy.wait_send()
    drain(rsbuf_ref, plane - 1, arsem.at[0])
    drain(zbuf_ref, z_count - 1, arsem.at[2])
    drain(agbuf_ref, PLANE_DOM - 1, arsem.at[4])


def full8(value):
    return jnp.broadcast_to(value, (8, 128))


def eliminate(work):
    sub = lax.broadcasted_iota(jnp.int32, (8, 128), 0)
    for g in range(8):
        cols = [[full8(work[i][:, g * 8 + j : g * 8 + j + 1]) for i in range(g, 8)] for j in range(8)]
        rows = [full8(work[g][j : j + 1, :]) for j in range(8)]
        block = [[full8(cols[b][0][a : a + 1, :]) for b in range(a + 1)] for a in range(8)]
        mult = [[None] * 8 for _ in range(8)]
        inverse = []
        for j in range(8):
            inverse.append(1.0 / block[j][j])
            for a in range(j + 1, 8):
                mult[a][j] = block[a][j] * inverse[j]
            for a in range(j + 1, 8):
                for b in range(j + 1, a + 1):
                    block[a][b] = block[a][b] - mult[a][j] * block[b][j]
                rows[a] = rows[a] - mult[a][j] * rows[j]
        scaled = [rows[j] * inverse[j] for j in range(8)]
        done = rows[0]
        for j in range(1, 8):
            done = jnp.where(sub == j, rows[j], done)
        work[g] = done
        for i in range(g + 1, 8):
            col = [cols[j][i - g] for j in range(8)]
            for j in range(8):
                for t in range(j):
                    col[j] = col[j] - col[t] * mult[j][t]
            terms = [col[j] * scaled[j] for j in range(8)]
            while len(terms) > 1:
                terms = [terms[t] + terms[t + 1] for t in range(0, len(terms), 2)]
            work[i] = work[i] - terms[0]


def solve_kernel(scaling, f_ref, g_ref, basis_hbm, triangle_ref, basis_ref, sem):
    g = g_ref[...]
    turned = pltpu.roll(g, 64, 1)
    lane32 = lax.broadcasted_iota(jnp.int32, (32, 128), 1)
    row32 = lax.broadcasted_iota(jnp.int32, (32, 128), 0)
    top = jnp.where(lane32 < 64, g, jnp.where(lane32 - 64 == row32, 1.0, 0.0))
    bottom = jnp.where(lane32 < 64, turned, jnp.where(lane32 - 96 == row32, 1.0, 0.0))
    work = [top[i * 8 : (i + 1) * 8, :] for i in range(4)] + [
        bottom[i * 8 : (i + 1) * 8, :] for i in range(4)
    ]
    eliminate(work)
    sub = lax.broadcasted_iota(jnp.int32, (8, 128), 0)
    lane = lax.broadcasted_iota(jnp.int32, (8, 128), 1)
    rows_out = []
    for i in range(8):
        diag = jnp.sum(jnp.where(lane == sub + 8 * i, work[i], 0.0), axis=1, keepdims=True)
        rows_out.append(work[i] * lax.rsqrt(diag))
    full = jnp.concatenate(rows_out, axis=0)
    lane64 = lax.broadcasted_iota(jnp.int32, (COLS, 128), 1)
    row64 = lax.broadcasted_iota(jnp.int32, (COLS, 128), 0)
    triangle_ref[...] = jnp.where(lane64 >= row64, full * (1.0 / scaling), 0.0)[:, 0:COLS]
    full = full * scaling
    block = jnp.concatenate(
        [
            jnp.where(lane64 < 64, pltpu.roll(full, 64, 1), 0.0),
            jnp.where(lane64 < 64, 0.0, full),
        ],
        axis=0,
    )
    bhi, blo = split_two(block)
    right = jnp.concatenate([bhi, bhi, blo], axis=1)
    for t in range(4):
        fhi, flo = split_two(f_ref[:, t * 128 : (t + 1) * 128])
        left = jnp.concatenate([fhi, flo, fhi], axis=1)
        basis_ref[t] = dot_nt(left, right)
        pltpu.make_async_copy(
            basis_ref.at[t], basis_hbm.at[:, pl.ds(t * 128, 128)], sem.at[t]
        ).start()
    for t in range(4):
        pltpu.make_async_copy(
            basis_ref.at[t], basis_hbm.at[:, pl.ds(t * 128, 128)], sem.at[t]
        ).wait()


def local(n_dom, n_rep, start_block, restriction_maps, send_rows, partner):
    z_count = n_dom // PLANE_DOM
    plane = PLANE_DOM * n_rep
    share = 32 // PLANE_DOM
    vmem = pl.BlockSpec(memory_space=pltpu.VMEM)
    hbm = pl.BlockSpec(memory_space=pltpu.HBM)
    inputs = [
        pltpu.with_memory_space_constraint(value, pltpu.HBM)
        for value in (start_block, restriction_maps, send_rows, partner)
    ]
    f_rows, gram = pl.pallas_call(
        functools.partial(filter_kernel, n_dom, n_rep),
        out_shape=[
            pltpu.VMEM((NODE_DEV, WIDE), F32),
            pltpu.VMEM((32, 128), F32),
        ],
        in_specs=[hbm, hbm, hbm, hbm],
        out_specs=[vmem, vmem],
        scratch_shapes=[
            pltpu.VMEM((NODE_DEV, WIDE), F32),
            pltpu.VMEM((STALK, STALK, ENDS), F32),
            pltpu.SMEM((1, SLOTS), jnp.int32),
            pltpu.VMEM((ENDS,), jnp.int32),
            pltpu.VMEM((ENDS, 128), F32),
            pltpu.VMEM((DEG, 64, 128), F32),
            pltpu.VMEM((DEG + 1, 64, 128), F32),
            pltpu.VMEM((256, ENDS), BF16),
            pltpu.VMEM((WIDE, 128), F32),
            pltpu.VMEM((WIDE, 256), BF16),
            pltpu.VMEM((WIDE, ENDS), F32),
            pltpu.VMEM((WIDE, 128), F32),
            pltpu.VMEM((SLOTS, 128), F32),
            pltpu.VMEM((64, 128), F32),
            pltpu.VMEM((2, SLOTS, WIDE), F32),
            pltpu.VMEM((SLOTS, 128), F32),
            pltpu.VMEM((2, SLOTS, WIDE), F32),
            pltpu.VMEM((WIDE, 128), F32),
            pltpu.VMEM((PLANE_DOM, share, 128), F32),
            pltpu.VMEM((plane, share, 128), F32),
            pltpu.VMEM((2, share, 128), F32),
            pltpu.VMEM((z_count, share, 128), F32),
            pltpu.VMEM((PLANE_DOM, share, 128), F32),
            pltpu.SemaphoreType.DMA((2, 4)),
            pltpu.SemaphoreType.DMA((2, 2, 4)),
            pltpu.SemaphoreType.DMA((6,)),
            pltpu.SemaphoreType.DMA((4,)),
            pltpu.SemaphoreType.REGULAR,
            pltpu.SemaphoreType.REGULAR((2,)),
        ],
        compiler_params=pltpu.CompilerParams(
            collective_id=0, has_side_effects=True, vmem_limit_bytes=40 * 1024 * 1024
        ),
        name="filter_and_gram",
    )(*inputs)
    scaling = math.sqrt(NODE_DEV * STALK * n_dom * n_rep)
    return pl.pallas_call(
        functools.partial(solve_kernel, scaling),
        out_shape=[
            jax.ShapeDtypeStruct((NODE_DEV, WIDE), F32),
            jax.ShapeDtypeStruct((COLS, COLS), F32),
        ],
        in_specs=[vmem, vmem],
        out_specs=[hbm, vmem],
        scratch_shapes=[pltpu.VMEM((4, NODE_DEV, 128), F32), pltpu.SemaphoreType.DMA((4,))],
        compiler_params=pltpu.CompilerParams(vmem_limit_bytes=16 * 1024 * 1024),
        name="factor_and_solve",
    )(f_rows, gram)


def solution(mesh):
    n_dom, n_rep = mesh.shape["dom"], mesh.shape["rep"]
    in_specs = (
        P(("dom", "rep"), None),
        P(None, None, ("dom", "rep")),
        P(("dom", "rep"), None),
        P(("dom", "rep")),
    )
    out_specs = (P(("dom", "rep"), None), P())
    return jax.shard_map(
        functools.partial(local, n_dom, n_rep),
        mesh=mesh,
        in_specs=in_specs,
        out_specs=out_specs,
        check_vma=False,
    )
```

```python
import functools
import math

import jax
import jax.numpy as jnp
from jax import lax
from jax.experimental import pallas as pl
from jax.experimental.pallas import tpu as pltpu
from jax.sharding import PartitionSpec as P

MESH = pl.DeviceIdType.MESH
F32 = jnp.float32
BF16 = jnp.bfloat16

STALK = 8
COLS = 64
DEG = 6
NODE_DEV = 128
ENDS = NODE_DEV * DEG
BND = 16
SLOTS = 4 * BND
WIDE = STALK * COLS
PLANE_DOM = 8
CENTER = 21.0
RADIUS = 15.0


def split_two(x):
    hi = x.astype(BF16)
    lo = (x - hi.astype(F32)).astype(BF16)
    return hi, lo


def dot_nn(a, b):
    return lax.dot_general(a, b, (((1,), (0,)), ((), ())), preferred_element_type=F32)


def dot_nt(a, b):
    return lax.dot_general(a, b, (((1,), (1,)), ((), ())), preferred_element_type=F32)


def row_bcast(row):
    return jnp.broadcast_to(row, (8, row.shape[1]))


def drain(ref, count, sem):
    pltpu.make_async_copy(ref.at[pl.ds(0, count)], ref.at[pl.ds(0, count)], sem).wait()


def filter_kernel(
    n_dom,
    n_rep,
    start_hbm,
    maps_hbm,
    send_hbm,
    partner_hbm,
    f_ref,
    g_ref,
    start_ref,
    maps_ref,
    send_ref,
    partner_ref,
    rt_ref,
    rk_ref,
    coef_ref,
    ss_ref,
    vt_ref,
    vhl_ref,
    vx_ref,
    t_ref,
    rs_ref,
    ms_ref,
    vsend_ref,
    rrecv_ref,
    vrecv_ref,
    cpack_ref,
    gsl_ref,
    rsbuf_ref,
    zsend_ref,
    zbuf_ref,
    agbuf_ref,
    rsem,
    vsem,
    arsem,
    insem,
    xsem,
    zsem,
):
    d = lax.axis_index("dom")
    r = lax.axis_index("rep")
    z_count = n_dom // PLANE_DOM
    plane = PLANE_DOM * n_rep
    z = d // PLANE_DOM
    base = z * PLANE_DOM
    q = (d - base) * n_rep + r

    up = lax.rem(d + 1, n_dom)
    down = lax.rem(d + n_dom - 1, n_dom)
    nxt = lax.rem(r + 1, n_rep)
    prv = lax.rem(r + n_rep - 1, n_rep)
    neighbours = ((up, r), (down, r), (d, nxt), (d, prv))

    loads = [
        pltpu.make_async_copy(src, dst, insem.at[i])
        for i, (src, dst) in enumerate(
            (
                (send_hbm, send_ref),
                (start_hbm, start_ref),
                (maps_hbm, maps_ref),
                (partner_hbm, partner_ref),
            )
        )
    ]
    mine = d - base
    other_core = d + 1 - 2 * lax.rem(d, 2)
    x_peers = [(base + lax.rem(mine + 2 * i, PLANE_DOM), r) for i in range(1, PLANE_DOM // 2)]
    near = [(up, r), (down, r)]

    def z_shift(by):
        return (lax.rem(z + z_count + by, z_count) * PLANE_DOM + mine, r)

    near += [z_shift(by) for by in (2, -2)]
    for i in sorted(range(1, n_rep), key=lambda i: -min(i, n_rep - i)):
        turn = lax.rem(r + i, n_rep)
        near += [(d, turn), (other_core, turn)]
    near += [
        (base + lax.rem(mine + i, PLANE_DOM), r)
        for i in sorted(range(1, PLANE_DOM), key=lambda i: -min(i, PLANE_DOM - i))
    ]
    near += [z_shift(by) for by in (1, -1)]
    barrier = pltpu.get_barrier_semaphore()
    for peer in near:
        pl.semaphore_signal(barrier, inc=1, device_id=peer, device_id_type=MESH)

    for load in loads:
        load.start()

    loads[0].wait()
    loads[1].wait()
    for s in range(SLOTS):
        node = lax.div(send_ref[0, s], DEG)
        vsend_ref[0, s : s + 1, :] = start_ref[pl.ds(node, 1), :]
    loads[2].wait()
    loads[3].wait()

    part = jnp.broadcast_to(partner_ref[...].reshape(1, ENDS).astype(F32), (8, ENDS))
    end_id = lax.broadcasted_iota(jnp.int32, (8, ENDS), 1).astype(F32)
    node_id = jnp.floor((end_id + 0.5) * (1.0 / DEG))
    sub8 = lax.broadcasted_iota(jnp.int32, (8, ENDS), 0)
    extra = jnp.where(sub8 == 0, part, node_id)
    for t in range(DEG):
        cols = slice(t * 128, (t + 1) * 128)
        block = jnp.concatenate(
            [maps_ref[:, :, cols].reshape(64, 128), extra[:, cols], jnp.zeros((56, 128), F32)], axis=0
        )
        rt_ref[cols, :] = block.T

    for t in range(4):
        vt_ref[t * 128 : (t + 1) * 128, :] = start_ref[:, t * 128 : (t + 1) * 128].T

    for s in range(SLOTS):
        rs_ref[s : s + 1, :] = rt_ref[pl.ds(send_ref[0, s], 1), :]
    rs = rs_ref[...]
    lane = lax.broadcasted_iota(jnp.int32, (SLOTS, 128), 1).astype(F32)
    slot = lax.broadcasted_iota(jnp.int32, (SLOTS, 1), 0)
    expect = (ENDS + jnp.bitwise_xor(slot, BND)).astype(F32)
    used = rs[:, 64:65] == expect
    hot = jnp.where(jnp.logical_and(rs[:, 65:66] == lane, used), 1.0, 0.0).astype(BF16)
    hot_wide = jnp.concatenate([hot, hot], axis=1)
    hot_tall = jnp.concatenate([hot, hot], axis=0)
    same = dot_nt(hot, hot).astype(BF16)
    same_wide = jnp.concatenate([same, same], axis=1)

    sub = lax.broadcasted_iota(jnp.int32, (128, 128), 0).astype(F32)
    rhl = []
    kk_rows = []
    for k in range(DEG):
        rk = rt_ref[pl.ds(k, NODE_DEV, stride=DEG), :].T
        rk_ref[k] = rk[0:64, :]
        p = rk[64:65, :]
        node = jnp.floor((p + 0.5) * (1.0 / DEG))
        kk_rows.append(p - DEG * node)
        one = jnp.where(sub == node, 1.0, 0.0).astype(BF16)
        ss_ref[0:128, k * 128 : (k + 1) * 128] = one
        ss_ref[128:256, k * 128 : (k + 1) * 128] = one
        hi, lo = split_two(rk[0:64, :])
        rhl.append(jnp.concatenate([hi, lo], axis=1))
    rhl = jnp.concatenate(rhl, axis=0)

    def value_copies(step):
        return [
            pltpu.make_async_remote_copy(
                src_ref=vsend_ref.at[step, pl.ds(k * BND, BND), :],
                dst_ref=vrecv_ref.at[step, pl.ds((k ^ 1) * BND, BND), :],
                send_sem=vsem.at[0, step, k],
                recv_sem=vsem.at[1, step, k ^ 1],
                device_id=neighbours[k],
                device_id_type=MESH,
            )
            for k in range(4)
        ]

    map_copies = [
        pltpu.make_async_remote_copy(
            src_ref=rs_ref.at[pl.ds(k * BND, BND), :],
            dst_ref=rrecv_ref.at[pl.ds((k ^ 1) * BND, BND), :],
            send_sem=rsem.at[0, k],
            recv_sem=rsem.at[1, k ^ 1],
            device_id=neighbours[k],
            device_id_type=MESH,
        )
        for k in range(4)
    ]

    pl.semaphore_wait(barrier, len(near))
    first_copies = value_copies(0)
    for copy in map_copies + first_copies:
        copy.start()
    for peer in x_peers:
        pl.semaphore_signal(xsem, inc=1, device_id=peer, device_id_type=MESH)
    for by in (2, -2):
        pl.semaphore_signal(zsem.at[0], inc=1, device_id=z_shift(by), device_id_type=MESH)

    sub_b = lax.broadcasted_iota(jnp.int32, (8, 128), 0)
    own = [jnp.zeros((8, 128), F32) for _ in range(STALK)]
    for j in range(3):
        far = dot_nn(rhl, ss_ref[:, j * 256 : (j + 1) * 256])
        for h in range(2):
            k = 2 * j + h
            mate_map = far[0:64, h * 128 : (h + 1) * 128]
            for m in range(1, DEG):
                mate_map = jnp.where(
                    kk_rows[k] == float(m),
                    far[m * 64 : (m + 1) * 64, h * 128 : (h + 1) * 128],
                    mate_map,
                )
            for a2 in range(STALK):
                acc = jnp.zeros((8, 128), F32)
                for a in range(STALK):
                    coef = row_bcast(rk_ref[k, a * 8 + a2 : a * 8 + a2 + 1, :])
                    acc = acc + coef * mate_map[a * 8 : (a + 1) * 8, :]
                    own[a2] = own[a2] + coef * rk_ref[k, a * 8 : (a + 1) * 8, :]
                coef_ref[k, a2 * 8 : (a2 + 1) * 8, :] = acc * (-1.0 / RADIUS)
    for a2 in range(STALK):
        coef_ref[DEG, a2 * 8 : (a2 + 1) * 8, :] = (
            own[a2] - jnp.where(sub_b == a2, CENTER, 0.0)
        ) * (1.0 / RADIUS)

    def spread(values_ref):
        hi, lo = split_two(values_ref[...])
        vhl_ref[:, 0:128] = hi
        vhl_ref[:, 128:256] = lo

    def recv_waits(copies):
        for copy in copies:
            copy.wait_recv()

    def local_part(own_ref, out_ref, combine):
        for j in range(3):
            vx_ref[:, j * 256 : (j + 1) * 256] = dot_nn(
                vhl_ref[...], ss_ref[:, j * 256 : (j + 1) * 256]
            )

        def columns(i, carry):
            acc = [[jnp.zeros((8, 128), F32) for _ in range(2)] for _ in range(STALK)]
            for k in range(DEG + 1):
                for b in range(STALK):
                    vals = []
                    for h in range(2):
                        at = pl.ds(pl.multiple_of(b * COLS + i * 16 + h * 8, 8), 8)
                        if k == DEG:
                            vals.append(own_ref[at, :])
                        else:
                            vals.append(vx_ref[at, k * 128 : (k + 1) * 128])
                    for a2 in range(STALK):
                        coef = row_bcast(coef_ref[k, a2 * 8 + b : a2 * 8 + b + 1, :])
                        for h in range(2):
                            acc[a2][h] = acc[a2][h] + coef * vals[h]
            for a2 in range(STALK):
                for h in range(2):
                    at = pl.ds(pl.multiple_of(a2 * COLS + i * 16 + h * 8, 8), 8)
                    out_ref[at, :] = combine(acc[a2][h], at)
            return carry

        lax.fori_loop(0, 4, columns, 0)

    def remote_part(step):
        low = lax.broadcasted_iota(jnp.int32, (8, 128), 1) < SLOTS
        turned = []
        for t in range(4):
            block = vrecv_ref[step, :, t * 128 : (t + 1) * 128]
            turned.append(jnp.concatenate([block, block], axis=0).T)
        for cg in range(8):
            acc = [jnp.zeros((8, 128), F32) for _ in range(STALK)]
            for b in range(STALK):
                row = b * COLS + cg * 8
                val = turned[row // 128][row % 128 : row % 128 + 8, :]
                for a2 in range(STALK):
                    coef = row_bcast(ms_ref[a2 * 8 + b : a2 * 8 + b + 1, :])
                    acc[a2] = acc[a2] + coef * val
            for a2 in range(STALK):
                hi = acc[a2].astype(BF16).astype(F32)
                cpack_ref[a2 * COLS + cg * 8 : a2 * COLS + cg * 8 + 8, :] = jnp.where(
                    low, hi, acc[a2] - hi
                )
        return cpack_ref[...].astype(BF16)

    spread(vt_ref)
    local_part(vt_ref, t_ref, lambda acc, at: acc)
    hi, lo = split_two(t_ref[...])
    vsend_ref[1] = dot_nt(hot_wide, jnp.concatenate([hi, lo], axis=1))

    recv_waits(map_copies)
    far_maps = jnp.concatenate([rrecv_ref[...], rrecv_ref[...]], axis=0).T
    own_maps = jnp.concatenate([rs, rs], axis=0).T
    for a2 in range(STALK):
        acc = jnp.zeros((8, 128), F32)
        for a in range(STALK):
            acc = acc + row_bcast(own_maps[a * 8 + a2 : a * 8 + a2 + 1, :]) * (
                far_maps[a * 8 : (a + 1) * 8, :]
            )
        ms_ref[a2 * 8 : (a2 + 1) * 8, :] = acc * (-1.0 / RADIUS)
    recv_waits(first_copies)
    packed_far = remote_part(0)
    vsend_ref[1] = vsend_ref[1] + dot_nt(same_wide, packed_far)
    second_copies = value_copies(1)
    for copy in second_copies:
        copy.start()

    t_ref[...] = t_ref[...] + dot_nn(packed_far, hot_tall)
    spread(t_ref)
    pl.semaphore_wait(zsem.at[0], 2)
    for by in (4, -4):
        pl.semaphore_signal(zsem.at[1], inc=1, device_id=z_shift(by), device_id_type=MESH)
    local_part(t_ref, vt_ref, lambda acc, at: 2.0 * acc - vt_ref[at, :])
    recv_waits(second_copies)
    vt_ref[...] = vt_ref[...] + 2.0 * dot_nn(remote_part(1), hot_tall)

    spread(vt_ref)
    tall = jnp.concatenate(
        [
            jnp.concatenate(
                [vhl_ref[a * COLS : (a + 1) * COLS, h * 128 : (h + 1) * 128] for a in range(STALK)],
                axis=1,
            )
            for h in range(2)
        ],
        axis=0,
    )
    prod = dot_nt(tall, tall)
    half = prod[0:64, :] + prod[64:128, :]
    both = half + pltpu.roll(half, 64, 1)
    lane32 = lax.broadcasted_iota(jnp.int32, (32, 128), 1)
    packed = jnp.where(lane32 < 64, both[0:32, :], both[32:64, :])
    share = 32 // PLANE_DOM
    for i in range(PLANE_DOM):
        gsl_ref[i] = packed[i * share : (i + 1) * share, :]

    pl.semaphore_wait(xsem, len(x_peers))
    chips_x = PLANE_DOM // 2
    x, c = mine // 2, lax.rem(mine, 2)

    def ring(step, count):
        return min(step, count - step)

    offsets = [
        (dx, dy, dc) for dx in range(chips_x) for dy in range(n_rep) for dc in range(2)
    ][1:]
    offsets.sort(key=lambda o: -(ring(o[0], chips_x) + ring(o[1], n_rep)))

    def plane_peer(dx, dy, dc):
        to = lax.rem(x + dx, chips_x) * 2 + lax.rem(c + dc, 2)
        return to, (base + to, lax.rem(r + dy, n_rep))

    for offset in offsets:
        to, peer = plane_peer(*offset)
        pltpu.make_async_remote_copy(
            src_ref=gsl_ref.at[to],
            dst_ref=rsbuf_ref.at[q],
            send_sem=arsem.at[0],
            recv_sem=arsem.at[1],
            device_id=peer,
            device_id_type=MESH,
        ).start()
    rsbuf_ref[q] = gsl_ref[mine]
    for t in range(4):
        f_ref[:, t * 128 : (t + 1) * 128] = vt_ref[t * 128 : (t + 1) * 128, :].T
    pl.semaphore_wait(zsem.at[1], 2)
    drain(rsbuf_ref, plane - 1, arsem.at[1])

    def total(ref, count):
        rows = [ref[i] for i in range(count)]
        while len(rows) > 1:
            rows = [rows[i] + rows[i + 1] for i in range(0, len(rows) - 1, 2)] + (
                [rows[-1]] if len(rows) % 2 else []
            )
        return rows[0]

    part_sum = total(rsbuf_ref, plane)
    zsend_ref[0] = part_sum
    for by in sorted(range(1, z_count), key=lambda step: -ring(step, z_count)):
        pltpu.make_async_remote_copy(
            src_ref=zsend_ref.at[0],
            dst_ref=zbuf_ref.at[z],
            send_sem=arsem.at[2],
            recv_sem=arsem.at[3],
            device_id=z_shift(by),
            device_id_type=MESH,
        ).start()
    zbuf_ref[z] = part_sum
    drain(zbuf_ref, z_count - 1, arsem.at[3])
    slice_sum = total(zbuf_ref, z_count)
    zsend_ref[1] = slice_sum
    for offset in offsets:
        if offset[1] == 0:
            pltpu.make_async_remote_copy(
                src_ref=zsend_ref.at[1],
                dst_ref=agbuf_ref.at[mine],
                send_sem=arsem.at[4],
                recv_sem=arsem.at[5],
                device_id=plane_peer(*offset)[1],
                device_id_type=MESH,
            ).start()
    agbuf_ref[mine] = slice_sum
    drain(agbuf_ref, PLANE_DOM - 1, arsem.at[5])
    for i in range(PLANE_DOM):
        g_ref[i * share : (i + 1) * share, :] = agbuf_ref[i]

    for copies in (map_copies, first_copies, second_copies):
        for copy in copies:
            copy.wait_send()
    drain(rsbuf_ref, plane - 1, arsem.at[0])
    drain(zbuf_ref, z_count - 1, arsem.at[2])
    drain(agbuf_ref, PLANE_DOM - 1, arsem.at[4])


def full8(value):
    return jnp.broadcast_to(value, (8, 128))


def eliminate(work):
    sub = lax.broadcasted_iota(jnp.int32, (8, 128), 0)
    for g in range(8):
        cols = [[full8(work[i][:, g * 8 + j : g * 8 + j + 1]) for i in range(g, 8)] for j in range(8)]
        rows = [full8(work[g][j : j + 1, :]) for j in range(8)]
        block = [[full8(cols[b][0][a : a + 1, :]) for b in range(a + 1)] for a in range(8)]
        mult = [[None] * 8 for _ in range(8)]
        inverse = []
        for j in range(8):
            inverse.append(1.0 / block[j][j])
            for a in range(j + 1, 8):
                mult[a][j] = block[a][j] * inverse[j]
            for a in range(j + 1, 8):
                for b in range(j + 1, a + 1):
                    block[a][b] = block[a][b] - mult[a][j] * block[b][j]
                rows[a] = rows[a] - mult[a][j] * rows[j]
        scaled = [rows[j] * inverse[j] for j in range(8)]
        done = rows[0]
        for j in range(1, 8):
            done = jnp.where(sub == j, rows[j], done)
        work[g] = done
        for i in range(g + 1, 8):
            col = [cols[j][i - g] for j in range(8)]
            for j in range(8):
                for t in range(j):
                    col[j] = col[j] - col[t] * mult[j][t]
            terms = [col[j] * scaled[j] for j in range(8)]
            while len(terms) > 1:
                terms = [terms[t] + terms[t + 1] for t in range(0, len(terms), 2)]
            work[i] = work[i] - terms[0]


def solve_kernel(
    scaling, f_ref, g_ref, basis_hbm, triangle_hbm, basis_ref, triangle_ref, left_ref, sem
):
    g = g_ref[...]
    turned = pltpu.roll(g, 64, 1)
    lane32 = lax.broadcasted_iota(jnp.int32, (32, 128), 1)
    row32 = lax.broadcasted_iota(jnp.int32, (32, 128), 0)
    top = jnp.where(lane32 < 64, g, jnp.where(lane32 - 64 == row32, 1.0, 0.0))
    bottom = jnp.where(lane32 < 64, turned, jnp.where(lane32 - 96 == row32, 1.0, 0.0))
    work = [top[i * 8 : (i + 1) * 8, :] for i in range(4)] + [
        bottom[i * 8 : (i + 1) * 8, :] for i in range(4)
    ]
    for t in range(4):
        fhi, flo = split_two(f_ref[:, t * 128 : (t + 1) * 128])
        left_ref[t * 128 : (t + 1) * 128, 0:128] = fhi
        left_ref[t * 128 : (t + 1) * 128, 128:256] = flo
    eliminate(work)
    sub = lax.broadcasted_iota(jnp.int32, (8, 128), 0)
    lane = lax.broadcasted_iota(jnp.int32, (8, 128), 1)
    rows_out = []
    for i in range(8):
        diag = jnp.sum(jnp.where(lane == sub + 8 * i, work[i], 0.0), axis=1, keepdims=True)
        rows_out.append(work[i] * lax.rsqrt(diag))
    full = jnp.concatenate(rows_out, axis=0)
    lane64 = lax.broadcasted_iota(jnp.int32, (COLS, 128), 1)
    row64 = lax.broadcasted_iota(jnp.int32, (COLS, 128), 0)
    triangle_ref[...] = jnp.where(lane64 >= row64, full * (1.0 / scaling), 0.0)[:, 0:COLS]
    copies = [pltpu.make_async_copy(triangle_ref, triangle_hbm, sem.at[4])]
    copies[0].start()
    full = full * scaling
    block = jnp.concatenate(
        [
            jnp.where(lane64 < 64, pltpu.roll(full, 64, 1), 0.0),
            jnp.where(lane64 < 64, 0.0, full),
        ],
        axis=0,
    )
    bhi, blo = split_two(block)
    right = jnp.concatenate(
        [
            jnp.concatenate([bhi, bhi], axis=1),
            jnp.concatenate([blo, jnp.zeros_like(blo)], axis=1),
        ],
        axis=0,
    )
    for t in range(4):
        both = dot_nt(left_ref[t * 128 : (t + 1) * 128, :], right)
        basis_ref[t] = both[:, 0:128] + both[:, 128:256]
        copy = pltpu.make_async_copy(
            basis_ref.at[t], basis_hbm.at[:, pl.ds(t * 128, 128)], sem.at[t]
        )
        copy.start()
        copies.append(copy)
    for copy in copies:
        copy.wait()


def local(n_dom, n_rep, start_block, restriction_maps, send_rows, partner):
    z_count = n_dom // PLANE_DOM
    plane = PLANE_DOM * n_rep
    share = 32 // PLANE_DOM
    vmem = pl.BlockSpec(memory_space=pltpu.VMEM)
    hbm = pl.BlockSpec(memory_space=pltpu.HBM)
    inputs = [
        pltpu.with_memory_space_constraint(value, pltpu.HBM)
        for value in (start_block, restriction_maps, send_rows, partner)
    ]
    f_rows, gram = pl.pallas_call(
        functools.partial(filter_kernel, n_dom, n_rep),
        out_shape=[
            pltpu.VMEM((NODE_DEV, WIDE), F32),
            pltpu.VMEM((32, 128), F32),
        ],
        in_specs=[hbm, hbm, hbm, hbm],
        out_specs=[vmem, vmem],
        scratch_shapes=[
            pltpu.VMEM((NODE_DEV, WIDE), F32),
            pltpu.VMEM((STALK, STALK, ENDS), F32),
            pltpu.SMEM((1, SLOTS), jnp.int32),
            pltpu.VMEM((ENDS,), jnp.int32),
            pltpu.VMEM((ENDS, 128), F32),
            pltpu.VMEM((DEG, 64, 128), F32),
            pltpu.VMEM((DEG + 1, 64, 128), F32),
            pltpu.VMEM((256, ENDS), BF16),
            pltpu.VMEM((WIDE, 128), F32),
            pltpu.VMEM((WIDE, 256), BF16),
            pltpu.VMEM((WIDE, ENDS), F32),
            pltpu.VMEM((WIDE, 128), F32),
            pltpu.VMEM((SLOTS, 128), F32),
            pltpu.VMEM((64, 128), F32),
            pltpu.VMEM((2, SLOTS, WIDE), F32),
            pltpu.VMEM((SLOTS, 128), F32),
            pltpu.VMEM((2, SLOTS, WIDE), F32),
            pltpu.VMEM((WIDE, 128), F32),
            pltpu.VMEM((PLANE_DOM, share, 128), F32),
            pltpu.VMEM((plane, share, 128), F32),
            pltpu.VMEM((2, share, 128), F32),
            pltpu.VMEM((z_count, share, 128), F32),
            pltpu.VMEM((PLANE_DOM, share, 128), F32),
            pltpu.SemaphoreType.DMA((2, 4)),
            pltpu.SemaphoreType.DMA((2, 2, 4)),
            pltpu.SemaphoreType.DMA((6,)),
            pltpu.SemaphoreType.DMA((4,)),
            pltpu.SemaphoreType.REGULAR,
            pltpu.SemaphoreType.REGULAR((2,)),
        ],
        compiler_params=pltpu.CompilerParams(
            collective_id=0, has_side_effects=True, vmem_limit_bytes=40 * 1024 * 1024
        ),
        name="filter_and_gram",
    )(*inputs)
    scaling = math.sqrt(NODE_DEV * STALK * n_dom * n_rep)
    return pl.pallas_call(
        functools.partial(solve_kernel, scaling),
        out_shape=[
            jax.ShapeDtypeStruct((NODE_DEV, WIDE), F32),
            jax.ShapeDtypeStruct((COLS, COLS), F32),
        ],
        in_specs=[vmem, vmem],
        out_specs=[hbm, hbm],
        scratch_shapes=[
            pltpu.VMEM((4, NODE_DEV, 128), F32),
            pltpu.VMEM((COLS, COLS), F32),
            pltpu.VMEM((4 * NODE_DEV, 256), BF16),
            pltpu.SemaphoreType.DMA((5,)),
        ],
        compiler_params=pltpu.CompilerParams(vmem_limit_bytes=16 * 1024 * 1024),
        name="factor_and_solve",
    )(f_rows, gram)


def solution(mesh):
    n_dom, n_rep = mesh.shape["dom"], mesh.shape["rep"]
    in_specs = (
        P(("dom", "rep"), None),
        P(None, None, ("dom", "rep")),
        P(("dom", "rep"), None),
        P(("dom", "rep")),
    )
    out_specs = (P(("dom", "rep"), None), P())
    return jax.shard_map(
        functools.partial(local, n_dom, n_rep),
        mesh=mesh,
        in_specs=in_specs,
        out_specs=out_specs,
        check_vma=False,
    )
```

```python
import functools
import math

import jax
import jax.numpy as jnp
from jax import lax
from jax.experimental import pallas as pl
from jax.experimental.pallas import tpu as pltpu
from jax.sharding import PartitionSpec as P

MESH = pl.DeviceIdType.MESH
F32 = jnp.float32
BF16 = jnp.bfloat16

STALK = 8
COLS = 64
DEG = 6
NODE_DEV = 128
ENDS = NODE_DEV * DEG
BND = 16
SLOTS = 4 * BND
WIDE = STALK * COLS
PLANE_DOM = 8
CENTER = 21.0
RADIUS = 15.0


def split_two(x):
    hi = x.astype(BF16)
    lo = (x - hi.astype(F32)).astype(BF16)
    return hi, lo


def dot_nn(a, b):
    return lax.dot_general(a, b, (((1,), (0,)), ((), ())), preferred_element_type=F32)


def dot_nt(a, b):
    return lax.dot_general(a, b, (((1,), (1,)), ((), ())), preferred_element_type=F32)


def row_bcast(row):
    return jnp.broadcast_to(row, (8, row.shape[1]))


def drain(ref, count, sem):
    pltpu.make_async_copy(ref.at[pl.ds(0, count)], ref.at[pl.ds(0, count)], sem).wait()


def filter_kernel(
    n_dom,
    n_rep,
    start_hbm,
    maps_hbm,
    send_hbm,
    partner_hbm,
    f_ref,
    g_ref,
    start_ref,
    maps_ref,
    send_ref,
    partner_ref,
    rt_ref,
    rk_ref,
    coef_ref,
    ss_ref,
    vt_ref,
    vhl_ref,
    vx_ref,
    t_ref,
    rs_ref,
    ms_ref,
    vsend_ref,
    rrecv_ref,
    vrecv_ref,
    cpack_ref,
    gsl_ref,
    rsbuf_ref,
    zsend_ref,
    zbuf_ref,
    agbuf_ref,
    rsem,
    vsem,
    arsem,
    insem,
    xsem,
    zsem,
):
    d = lax.axis_index("dom")
    r = lax.axis_index("rep")
    z_count = n_dom // PLANE_DOM
    plane = PLANE_DOM * n_rep
    z = d // PLANE_DOM
    base = z * PLANE_DOM
    q = (d - base) * n_rep + r

    up = lax.rem(d + 1, n_dom)
    down = lax.rem(d + n_dom - 1, n_dom)
    nxt = lax.rem(r + 1, n_rep)
    prv = lax.rem(r + n_rep - 1, n_rep)
    neighbours = ((up, r), (down, r), (d, nxt), (d, prv))

    loads = [
        pltpu.make_async_copy(src, dst, insem.at[i])
        for i, (src, dst) in enumerate(
            (
                (send_hbm, send_ref),
                (start_hbm, start_ref),
                (maps_hbm, maps_ref),
                (partner_hbm, partner_ref),
            )
        )
    ]
    mine = d - base
    other_core = d + 1 - 2 * lax.rem(d, 2)
    x_peers = [(base + lax.rem(mine + 2 * i, PLANE_DOM), r) for i in range(1, PLANE_DOM // 2)]
    near = [(up, r), (down, r)]

    def z_shift(by):
        return (lax.rem(z + z_count + by, z_count) * PLANE_DOM + mine, r)

    near += [z_shift(by) for by in (2, -2)]
    for i in sorted(range(1, n_rep), key=lambda i: -min(i, n_rep - i)):
        turn = lax.rem(r + i, n_rep)
        near += [(d, turn), (other_core, turn)]
    near += [
        (base + lax.rem(mine + i, PLANE_DOM), r)
        for i in sorted(range(1, PLANE_DOM), key=lambda i: -min(i, PLANE_DOM - i))
    ]
    near += [z_shift(by) for by in (1, -1)]
    barrier = pltpu.get_barrier_semaphore()
    for peer in near:
        pl.semaphore_signal(barrier, inc=1, device_id=peer, device_id_type=MESH)

    for load in loads:
        load.start()

    loads[0].wait()
    loads[1].wait()
    for s in range(SLOTS):
        node = lax.div(send_ref[0, s], DEG)
        vsend_ref[0, s : s + 1, :] = start_ref[pl.ds(node, 1), :]
    loads[2].wait()
    loads[3].wait()

    part = jnp.broadcast_to(partner_ref[...].reshape(1, ENDS).astype(F32), (8, ENDS))
    end_id = lax.broadcasted_iota(jnp.int32, (8, ENDS), 1).astype(F32)
    node_id = jnp.floor((end_id + 0.5) * (1.0 / DEG))
    sub8 = lax.broadcasted_iota(jnp.int32, (8, ENDS), 0)
    extra = jnp.where(sub8 == 0, part, node_id)
    for t in range(DEG):
        cols = slice(t * 128, (t + 1) * 128)
        block = jnp.concatenate(
            [maps_ref[:, :, cols].reshape(64, 128), extra[:, cols], jnp.zeros((56, 128), F32)], axis=0
        )
        rt_ref[cols, :] = block.T

    for t in range(4):
        vt_ref[t * 128 : (t + 1) * 128, :] = start_ref[:, t * 128 : (t + 1) * 128].T

    for s in range(SLOTS):
        rs_ref[s : s + 1, :] = rt_ref[pl.ds(send_ref[0, s], 1), :]
    rs = rs_ref[...]
    lane = lax.broadcasted_iota(jnp.int32, (SLOTS, 128), 1).astype(F32)
    slot = lax.broadcasted_iota(jnp.int32, (SLOTS, 1), 0)
    expect = (ENDS + jnp.bitwise_xor(slot, BND)).astype(F32)
    used = rs[:, 64:65] == expect
    hot = jnp.where(jnp.logical_and(rs[:, 65:66] == lane, used), 1.0, 0.0).astype(BF16)
    hot_wide = jnp.concatenate([hot, hot], axis=1)
    none = jnp.zeros_like(hot)
    hot_pair = jnp.concatenate(
        [jnp.concatenate([hot, none], axis=1), jnp.concatenate([none, hot], axis=1)], axis=0
    )
    hot_tall = jnp.concatenate([hot_pair, hot_pair], axis=0)
    same = dot_nt(hot_pair, hot_pair).astype(BF16)
    same_wide = jnp.concatenate([same, same], axis=1)

    sub = lax.broadcasted_iota(jnp.int32, (128, 128), 0).astype(F32)
    rhl = []
    kk_rows = []
    for k in range(DEG):
        rk = rt_ref[pl.ds(k, NODE_DEV, stride=DEG), :].T
        rk_ref[k] = rk[0:64, :]
        p = rk[64:65, :]
        node = jnp.floor((p + 0.5) * (1.0 / DEG))
        kk_rows.append(p - DEG * node)
        one = jnp.where(sub == node, 1.0, 0.0).astype(BF16)
        ss_ref[0:128, k * 128 : (k + 1) * 128] = one
        ss_ref[128:256, k * 128 : (k + 1) * 128] = one
        hi, lo = split_two(rk[0:64, :])
        rhl.append(jnp.concatenate([hi, lo], axis=1))
    rhl = jnp.concatenate(rhl, axis=0)

    def value_copies(step):
        return [
            pltpu.make_async_remote_copy(
                src_ref=vsend_ref.at[step, pl.ds(k * BND, BND), :],
                dst_ref=vrecv_ref.at[step, pl.ds((k ^ 1) * BND, BND), :],
                send_sem=vsem.at[0, step, k],
                recv_sem=vsem.at[1, step, k ^ 1],
                device_id=neighbours[k],
                device_id_type=MESH,
            )
            for k in range(4)
        ]

    map_copies = [
        pltpu.make_async_remote_copy(
            src_ref=rs_ref.at[pl.ds(k * BND, BND), :],
            dst_ref=rrecv_ref.at[pl.ds((k ^ 1) * BND, BND), :],
            send_sem=rsem.at[0, k],
            recv_sem=rsem.at[1, k ^ 1],
            device_id=neighbours[k],
            device_id_type=MESH,
        )
        for k in range(4)
    ]

    pl.semaphore_wait(barrier, len(near))
    first_copies = value_copies(0)
    for copy in map_copies + first_copies:
        copy.start()
    for peer in x_peers:
        pl.semaphore_signal(xsem, inc=1, device_id=peer, device_id_type=MESH)
    for by in (2, -2):
        pl.semaphore_signal(zsem.at[0], inc=1, device_id=z_shift(by), device_id_type=MESH)

    sub_b = lax.broadcasted_iota(jnp.int32, (8, 128), 0)
    own = [jnp.zeros((8, 128), F32) for _ in range(STALK)]
    for j in range(3):
        far = dot_nn(rhl, ss_ref[:, j * 256 : (j + 1) * 256])
        for h in range(2):
            k = 2 * j + h
            mate_map = far[0:64, h * 128 : (h + 1) * 128]
            for m in range(1, DEG):
                mate_map = jnp.where(
                    kk_rows[k] == float(m),
                    far[m * 64 : (m + 1) * 64, h * 128 : (h + 1) * 128],
                    mate_map,
                )
            for a2 in range(STALK):
                acc = jnp.zeros((8, 128), F32)
                for a in range(STALK):
                    coef = row_bcast(rk_ref[k, a * 8 + a2 : a * 8 + a2 + 1, :])
                    acc = acc + coef * mate_map[a * 8 : (a + 1) * 8, :]
                    own[a2] = own[a2] + coef * rk_ref[k, a * 8 : (a + 1) * 8, :]
                coef_ref[k, a2 * 8 : (a2 + 1) * 8, :] = acc * (-1.0 / RADIUS)
    for a2 in range(STALK):
        coef_ref[DEG, a2 * 8 : (a2 + 1) * 8, :] = (
            own[a2] - jnp.where(sub_b == a2, CENTER, 0.0)
        ) * (1.0 / RADIUS)

    def spread(values_ref):
        hi, lo = split_two(values_ref[...])
        vhl_ref[:, 0:128] = hi
        vhl_ref[:, 128:256] = lo

    def recv_waits(copies):
        for copy in copies:
            copy.wait_recv()

    def local_part(own_ref, out_ref, combine):
        for j in range(3):
            vx_ref[:, j * 256 : (j + 1) * 256] = dot_nn(
                vhl_ref[...], ss_ref[:, j * 256 : (j + 1) * 256]
            )

        def columns(i, carry):
            acc = [[jnp.zeros((8, 128), F32) for _ in range(2)] for _ in range(STALK)]
            for k in range(DEG + 1):
                for b in range(STALK):
                    vals = []
                    for h in range(2):
                        at = pl.ds(pl.multiple_of(b * COLS + i * 16 + h * 8, 8), 8)
                        if k == DEG:
                            vals.append(own_ref[at, :])
                        else:
                            vals.append(vx_ref[at, k * 128 : (k + 1) * 128])
                    for a2 in range(STALK):
                        coef = row_bcast(coef_ref[k, a2 * 8 + b : a2 * 8 + b + 1, :])
                        for h in range(2):
                            acc[a2][h] = acc[a2][h] + coef * vals[h]
            for a2 in range(STALK):
                for h in range(2):
                    at = pl.ds(pl.multiple_of(a2 * COLS + i * 16 + h * 8, 8), 8)
                    out_ref[at, :] = combine(acc[a2][h], at)
            return carry

        lax.fori_loop(0, 4, columns, 0)

    half = COLS // 2

    def remote_part(step):
        if step == 0:
            per_tile, stride = 2, COLS
            pairs = [vrecv_ref[0, :, t * 128 : (t + 1) * 128] for t in range(4)]
            pairs = [(block, pltpu.roll(block, 128 - half, 1)) for block in pairs]
        else:
            per_tile, stride = 4, half
            pairs = [
                (
                    vrecv_ref[1, :, t * 128 : (t + 1) * 128],
                    vrecv_ref[1, :, 256 + t * 128 : 256 + (t + 1) * 128],
                )
                for t in range(2)
            ]
        turned = [jnp.concatenate(pair, axis=0).T for pair in pairs]
        for cg in range(half // 8):
            acc = [jnp.zeros((8, 128), F32) for _ in range(STALK)]
            for b in range(STALK):
                row = (b % per_tile) * stride + cg * 8
                val = turned[b // per_tile][row : row + 8, :]
                for a2 in range(STALK):
                    coef = row_bcast(ms_ref[a2 * 8 + b : a2 * 8 + b + 1, :])
                    acc[a2] = acc[a2] + coef * val
            for a2 in range(STALK):
                at = slice(a2 * half + cg * 8, a2 * half + cg * 8 + 8)
                hi = acc[a2].astype(BF16).astype(F32)
                cpack_ref[at, 0:128] = hi
                cpack_ref[at, 128:256] = acc[a2] - hi
        return cpack_ref[...].astype(BF16)

    def add_remote(out_ref, packed_slots, scale):
        sums = dot_nn(packed_slots, hot_tall)
        for a2 in range(STALK):
            for h in range(2):
                at = slice(a2 * COLS + h * half, a2 * COLS + (h + 1) * half)
                part = sums[a2 * half : (a2 + 1) * half, h * 128 : (h + 1) * 128]
                out_ref[at, :] = out_ref[at, :] + scale * part

    spread(vt_ref)
    local_part(vt_ref, t_ref, lambda acc, at: acc)
    hi, lo = split_two(t_ref[...])
    both = jnp.concatenate([hi, lo], axis=1)
    by_half = jnp.concatenate(
        [
            both[a * COLS + h * half : a * COLS + (h + 1) * half, :]
            for h in range(2)
            for a in range(STALK)
        ],
        axis=0,
    )
    vsend_ref[1] = dot_nt(hot_wide, by_half)

    recv_waits(map_copies)
    far_maps = jnp.concatenate([rrecv_ref[...], rrecv_ref[...]], axis=0).T
    own_maps = jnp.concatenate([rs, rs], axis=0).T
    for a2 in range(STALK):
        acc = jnp.zeros((8, 128), F32)
        for a in range(STALK):
            acc = acc + row_bcast(own_maps[a * 8 + a2 : a * 8 + a2 + 1, :]) * (
                far_maps[a * 8 : (a + 1) * 8, :]
            )
        ms_ref[a2 * 8 : (a2 + 1) * 8, :] = acc * (-1.0 / RADIUS)
    recv_waits(first_copies)
    packed_far = remote_part(0)
    far_rows = dot_nt(same_wide, packed_far)
    vsend_ref[1, :, 0:256] = vsend_ref[1, :, 0:256] + far_rows[0:64, :]
    vsend_ref[1, :, 256:512] = vsend_ref[1, :, 256:512] + far_rows[64:128, :]
    second_copies = value_copies(1)
    for copy in second_copies:
        copy.start()

    add_remote(t_ref, packed_far, 1.0)
    spread(t_ref)
    pl.semaphore_wait(zsem.at[0], 2)
    for by in (4, -4):
        pl.semaphore_signal(zsem.at[1], inc=1, device_id=z_shift(by), device_id_type=MESH)
    local_part(t_ref, vt_ref, lambda acc, at: 2.0 * acc - vt_ref[at, :])
    recv_waits(second_copies)
    add_remote(vt_ref, remote_part(1), 2.0)

    spread(vt_ref)
    tall = jnp.concatenate(
        [
            jnp.concatenate(
                [vhl_ref[a * COLS : (a + 1) * COLS, h * 128 : (h + 1) * 128] for a in range(STALK)],
                axis=1,
            )
            for h in range(2)
        ],
        axis=0,
    )
    prod = dot_nt(tall, tall)
    halves = prod[0:64, :] + prod[64:128, :]
    both = halves + pltpu.roll(halves, 64, 1)
    lane32 = lax.broadcasted_iota(jnp.int32, (32, 128), 1)
    packed = jnp.where(lane32 < 64, both[0:32, :], both[32:64, :])
    share = 32 // PLANE_DOM
    for i in range(PLANE_DOM):
        gsl_ref[i] = packed[i * share : (i + 1) * share, :]

    pl.semaphore_wait(xsem, len(x_peers))
    chips_x = PLANE_DOM // 2
    x, c = mine // 2, lax.rem(mine, 2)

    def ring(step, count):
        return min(step, count - step)

    offsets = [
        (dx, dy, dc) for dx in range(chips_x) for dy in range(n_rep) for dc in range(2)
    ][1:]
    offsets.sort(key=lambda o: -(ring(o[0], chips_x) + ring(o[1], n_rep)))

    def plane_peer(dx, dy, dc):
        to = lax.rem(x + dx, chips_x) * 2 + lax.rem(c + dc, 2)
        return to, (base + to, lax.rem(r + dy, n_rep))

    for offset in offsets:
        to, peer = plane_peer(*offset)
        pltpu.make_async_remote_copy(
            src_ref=gsl_ref.at[to],
            dst_ref=rsbuf_ref.at[q],
            send_sem=arsem.at[0],
            recv_sem=arsem.at[1],
            device_id=peer,
            device_id_type=MESH,
        ).start()
    rsbuf_ref[q] = gsl_ref[mine]
    for t in range(4):
        f_ref[:, t * 128 : (t + 1) * 128] = vt_ref[t * 128 : (t + 1) * 128, :].T
    pl.semaphore_wait(zsem.at[1], 2)
    drain(rsbuf_ref, plane - 1, arsem.at[1])

    def total(ref, count):
        rows = [ref[i] for i in range(count)]
        while len(rows) > 1:
            rows = [rows[i] + rows[i + 1] for i in range(0, len(rows) - 1, 2)] + (
                [rows[-1]] if len(rows) % 2 else []
            )
        return rows[0]

    part_sum = total(rsbuf_ref, plane)
    zsend_ref[0] = part_sum
    for by in sorted(range(1, z_count), key=lambda step: -ring(step, z_count)):
        pltpu.make_async_remote_copy(
            src_ref=zsend_ref.at[0],
            dst_ref=zbuf_ref.at[z],
            send_sem=arsem.at[2],
            recv_sem=arsem.at[3],
            device_id=z_shift(by),
            device_id_type=MESH,
        ).start()
    zbuf_ref[z] = part_sum
    drain(zbuf_ref, z_count - 1, arsem.at[3])
    slice_sum = total(zbuf_ref, z_count)
    zsend_ref[1] = slice_sum
    for offset in offsets:
        if offset[1] == 0:
            pltpu.make_async_remote_copy(
                src_ref=zsend_ref.at[1],
                dst_ref=agbuf_ref.at[mine],
                send_sem=arsem.at[4],
                recv_sem=arsem.at[5],
                device_id=plane_peer(*offset)[1],
                device_id_type=MESH,
            ).start()
    agbuf_ref[mine] = slice_sum
    drain(agbuf_ref, PLANE_DOM - 1, arsem.at[5])
    for i in range(PLANE_DOM):
        g_ref[i * share : (i + 1) * share, :] = agbuf_ref[i]

    for copies in (map_copies, first_copies, second_copies):
        for copy in copies:
            copy.wait_send()
    drain(rsbuf_ref, plane - 1, arsem.at[0])
    drain(zbuf_ref, z_count - 1, arsem.at[2])
    drain(agbuf_ref, PLANE_DOM - 1, arsem.at[4])


def full8(value):
    return jnp.broadcast_to(value, (8, 128))


def eliminate(work):
    sub = lax.broadcasted_iota(jnp.int32, (8, 128), 0)
    for g in range(8):
        cols = [[full8(work[i][:, g * 8 + j : g * 8 + j + 1]) for i in range(g, 8)] for j in range(8)]
        rows = [full8(work[g][j : j + 1, :]) for j in range(8)]
        block = [[full8(cols[b][0][a : a + 1, :]) for b in range(a + 1)] for a in range(8)]
        mult = [[None] * 8 for _ in range(8)]
        inverse = []
        for j in range(8):
            inverse.append(1.0 / block[j][j])
            for a in range(j + 1, 8):
                mult[a][j] = block[a][j] * inverse[j]
            for a in range(j + 1, 8):
                for b in range(j + 1, a + 1):
                    block[a][b] = block[a][b] - mult[a][j] * block[b][j]
                rows[a] = rows[a] - mult[a][j] * rows[j]
        scaled = [rows[j] * inverse[j] for j in range(8)]
        done = rows[0]
        for j in range(1, 8):
            done = jnp.where(sub == j, rows[j], done)
        work[g] = done
        for i in range(g + 1, 8):
            col = [cols[j][i - g] for j in range(8)]
            for j in range(8):
                for t in range(j):
                    col[j] = col[j] - col[t] * mult[j][t]
            terms = [col[j] * scaled[j] for j in range(8)]
            while len(terms) > 1:
                terms = [terms[t] + terms[t + 1] for t in range(0, len(terms), 2)]
            work[i] = work[i] - terms[0]


def solve_kernel(
    scaling, f_ref, g_ref, basis_hbm, triangle_hbm, basis_ref, triangle_ref, left_ref, sem
):
    g = g_ref[...]
    turned = pltpu.roll(g, 64, 1)
    lane32 = lax.broadcasted_iota(jnp.int32, (32, 128), 1)
    row32 = lax.broadcasted_iota(jnp.int32, (32, 128), 0)
    top = jnp.where(lane32 < 64, g, jnp.where(lane32 - 64 == row32, 1.0, 0.0))
    bottom = jnp.where(lane32 < 64, turned, jnp.where(lane32 - 96 == row32, 1.0, 0.0))
    work = [top[i * 8 : (i + 1) * 8, :] for i in range(4)] + [
        bottom[i * 8 : (i + 1) * 8, :] for i in range(4)
    ]
    for t in range(4):
        fhi, flo = split_two(f_ref[:, t * 128 : (t + 1) * 128])
        left_ref[t * 128 : (t + 1) * 128, 0:128] = fhi
        left_ref[t * 128 : (t + 1) * 128, 128:256] = flo
    eliminate(work)
    sub = lax.broadcasted_iota(jnp.int32, (8, 128), 0)
    lane = lax.broadcasted_iota(jnp.int32, (8, 128), 1)
    rows_out = []
    for i in range(8):
        diag = jnp.sum(jnp.where(lane == sub + 8 * i, work[i], 0.0), axis=1, keepdims=True)
        rows_out.append(work[i] * lax.rsqrt(diag))
    full = jnp.concatenate(rows_out, axis=0)
    lane64 = lax.broadcasted_iota(jnp.int32, (COLS, 128), 1)
    row64 = lax.broadcasted_iota(jnp.int32, (COLS, 128), 0)
    triangle_ref[...] = jnp.where(lane64 >= row64, full * (1.0 / scaling), 0.0)[:, 0:COLS]
    copies = [pltpu.make_async_copy(triangle_ref, triangle_hbm, sem.at[4])]
    copies[0].start()
    full = full * scaling
    block = jnp.concatenate(
        [
            jnp.where(lane64 < 64, pltpu.roll(full, 64, 1), 0.0),
            jnp.where(lane64 < 64, 0.0, full),
        ],
        axis=0,
    )
    bhi, blo = split_two(block)
    right = jnp.concatenate(
        [
            jnp.concatenate([bhi, bhi], axis=1),
            jnp.concatenate([blo, jnp.zeros_like(blo)], axis=1),
        ],
        axis=0,
    )
    for t in range(4):
        both = dot_nt(left_ref[t * 128 : (t + 1) * 128, :], right)
        basis_ref[t] = both[:, 0:128] + both[:, 128:256]
        copy = pltpu.make_async_copy(
            basis_ref.at[t], basis_hbm.at[:, pl.ds(t * 128, 128)], sem.at[t]
        )
        copy.start()
        copies.append(copy)
    for copy in copies:
        copy.wait()


def local(n_dom, n_rep, start_block, restriction_maps, send_rows, partner):
    z_count = n_dom // PLANE_DOM
    plane = PLANE_DOM * n_rep
    share = 32 // PLANE_DOM
    vmem = pl.BlockSpec(memory_space=pltpu.VMEM)
    hbm = pl.BlockSpec(memory_space=pltpu.HBM)
    inputs = [
        pltpu.with_memory_space_constraint(value, pltpu.HBM)
        for value in (start_block, restriction_maps, send_rows, partner)
    ]
    f_rows, gram = pl.pallas_call(
        functools.partial(filter_kernel, n_dom, n_rep),
        out_shape=[
            pltpu.VMEM((NODE_DEV, WIDE), F32),
            pltpu.VMEM((32, 128), F32),
        ],
        in_specs=[hbm, hbm, hbm, hbm],
        out_specs=[vmem, vmem],
        scratch_shapes=[
            pltpu.VMEM((NODE_DEV, WIDE), F32),
            pltpu.VMEM((STALK, STALK, ENDS), F32),
            pltpu.SMEM((1, SLOTS), jnp.int32),
            pltpu.VMEM((ENDS,), jnp.int32),
            pltpu.VMEM((ENDS, 128), F32),
            pltpu.VMEM((DEG, 64, 128), F32),
            pltpu.VMEM((DEG + 1, 64, 128), F32),
            pltpu.VMEM((256, ENDS), BF16),
            pltpu.VMEM((WIDE, 128), F32),
            pltpu.VMEM((WIDE, 256), BF16),
            pltpu.VMEM((WIDE, ENDS), F32),
            pltpu.VMEM((WIDE, 128), F32),
            pltpu.VMEM((SLOTS, 128), F32),
            pltpu.VMEM((64, 128), F32),
            pltpu.VMEM((2, SLOTS, WIDE), F32),
            pltpu.VMEM((SLOTS, 128), F32),
            pltpu.VMEM((2, SLOTS, WIDE), F32),
            pltpu.VMEM((WIDE // 2, 256), F32),
            pltpu.VMEM((PLANE_DOM, share, 128), F32),
            pltpu.VMEM((plane, share, 128), F32),
            pltpu.VMEM((2, share, 128), F32),
            pltpu.VMEM((z_count, share, 128), F32),
            pltpu.VMEM((PLANE_DOM, share, 128), F32),
            pltpu.SemaphoreType.DMA((2, 4)),
            pltpu.SemaphoreType.DMA((2, 2, 4)),
            pltpu.SemaphoreType.DMA((6,)),
            pltpu.SemaphoreType.DMA((4,)),
            pltpu.SemaphoreType.REGULAR,
            pltpu.SemaphoreType.REGULAR((2,)),
        ],
        compiler_params=pltpu.CompilerParams(
            collective_id=0, has_side_effects=True, vmem_limit_bytes=40 * 1024 * 1024
        ),
        name="filter_and_gram",
    )(*inputs)
    scaling = math.sqrt(NODE_DEV * STALK * n_dom * n_rep)
    return pl.pallas_call(
        functools.partial(solve_kernel, scaling),
        out_shape=[
            jax.ShapeDtypeStruct((NODE_DEV, WIDE), F32),
            jax.ShapeDtypeStruct((COLS, COLS), F32),
        ],
        in_specs=[vmem, vmem],
        out_specs=[hbm, hbm],
        scratch_shapes=[
            pltpu.VMEM((4, NODE_DEV, 128), F32),
            pltpu.VMEM((COLS, COLS), F32),
            pltpu.VMEM((4 * NODE_DEV, 256), BF16),
            pltpu.SemaphoreType.DMA((5,)),
        ],
        compiler_params=pltpu.CompilerParams(vmem_limit_bytes=16 * 1024 * 1024),
        name="factor_and_solve",
    )(f_rows, gram)


def solution(mesh):
    n_dom, n_rep = mesh.shape["dom"], mesh.shape["rep"]
    in_specs = (
        P(("dom", "rep"), None),
        P(None, None, ("dom", "rep")),
        P(("dom", "rep"), None),
        P(("dom", "rep")),
    )
    out_specs = (P(("dom", "rep"), None), P())
    return jax.shard_map(
        functools.partial(local, n_dom, n_rep),
        mesh=mesh,
        in_specs=in_specs,
        out_specs=out_specs,
        check_vma=False,
    )
```

```python
import functools
import math

import jax
import jax.numpy as jnp
from jax import lax
from jax.experimental import pallas as pl
from jax.experimental.pallas import tpu as pltpu
from jax.sharding import PartitionSpec as P

MESH = pl.DeviceIdType.MESH
F32 = jnp.float32
BF16 = jnp.bfloat16

STALK = 8
COLS = 64
DEG = 6
NODE_DEV = 128
ENDS = NODE_DEV * DEG
BND = 16
SLOTS = 4 * BND
WIDE = STALK * COLS
PLANE_DOM = 8
CENTER = 21.0
RADIUS = 15.0


def split_two(x):
    hi = x.astype(BF16)
    lo = (x - hi.astype(F32)).astype(BF16)
    return hi, lo


def dot_nn(a, b):
    return lax.dot_general(a, b, (((1,), (0,)), ((), ())), preferred_element_type=F32)


def dot_nt(a, b):
    return lax.dot_general(a, b, (((1,), (1,)), ((), ())), preferred_element_type=F32)


def row_bcast(row):
    return jnp.broadcast_to(row, (8, row.shape[1]))


def drain(ref, count, sem):
    pltpu.make_async_copy(ref.at[pl.ds(0, count)], ref.at[pl.ds(0, count)], sem).wait()


def filter_kernel(
    n_dom,
    n_rep,
    start_hbm,
    maps_hbm,
    send_hbm,
    partner_hbm,
    f_ref,
    g_ref,
    start_ref,
    maps_ref,
    send_ref,
    partner_ref,
    rt_ref,
    rk_ref,
    coef_ref,
    ss_ref,
    vt_ref,
    vhl_ref,
    vx_ref,
    t_ref,
    rs_ref,
    ms_ref,
    vsend_ref,
    rrecv_ref,
    vrecv_ref,
    cpack_ref,
    gsl_ref,
    rsbuf_ref,
    zsend_ref,
    zbuf_ref,
    agbuf_ref,
    rsem,
    vsem,
    arsem,
    insem,
    xsem,
    zsem,
):
    d = lax.axis_index("dom")
    r = lax.axis_index("rep")
    z_count = n_dom // PLANE_DOM
    plane = PLANE_DOM * n_rep
    z = d // PLANE_DOM
    base = z * PLANE_DOM
    q = (d - base) * n_rep + r

    up = lax.rem(d + 1, n_dom)
    down = lax.rem(d + n_dom - 1, n_dom)
    nxt = lax.rem(r + 1, n_rep)
    prv = lax.rem(r + n_rep - 1, n_rep)
    neighbours = ((up, r), (down, r), (d, nxt), (d, prv))

    loads = [
        pltpu.make_async_copy(src, dst, insem.at[i])
        for i, (src, dst) in enumerate(
            (
                (send_hbm, send_ref),
                (start_hbm, start_ref),
                (maps_hbm, maps_ref),
                (partner_hbm, partner_ref),
            )
        )
    ]
    mine = d - base
    other_core = d + 1 - 2 * lax.rem(d, 2)
    x_peers = [(base + lax.rem(mine + 2 * i, PLANE_DOM), r) for i in range(1, PLANE_DOM // 2)]
    near = [(up, r), (down, r)]

    def z_shift(by):
        return (lax.rem(z + z_count + by, z_count) * PLANE_DOM + mine, r)

    near += [z_shift(by) for by in (2, -2)]
    for i in sorted(range(1, n_rep), key=lambda i: -min(i, n_rep - i)):
        turn = lax.rem(r + i, n_rep)
        near += [(d, turn), (other_core, turn)]
    near += [
        (base + lax.rem(mine + i, PLANE_DOM), r)
        for i in sorted(range(1, PLANE_DOM), key=lambda i: -min(i, PLANE_DOM - i))
    ]
    near += [z_shift(by) for by in (1, -1)]
    barrier = pltpu.get_barrier_semaphore()
    for peer in near:
        pl.semaphore_signal(barrier, inc=1, device_id=peer, device_id_type=MESH)

    for load in loads:
        load.start()

    loads[0].wait()
    loads[1].wait()
    for s in range(SLOTS):
        node = lax.div(send_ref[0, s], DEG)
        vsend_ref[0, s : s + 1, :] = start_ref[pl.ds(node, 1), :]
    loads[2].wait()
    loads[3].wait()

    part = jnp.broadcast_to(partner_ref[...].reshape(1, ENDS).astype(F32), (8, ENDS))
    end_id = lax.broadcasted_iota(jnp.int32, (8, ENDS), 1).astype(F32)
    node_id = jnp.floor((end_id + 0.5) * (1.0 / DEG))
    sub8 = lax.broadcasted_iota(jnp.int32, (8, ENDS), 0)
    extra = jnp.where(sub8 == 0, part, node_id)
    for t in range(DEG):
        cols = slice(t * 128, (t + 1) * 128)
        block = jnp.concatenate(
            [maps_ref[:, :, cols].reshape(64, 128), extra[:, cols], jnp.zeros((56, 128), F32)], axis=0
        )
        rt_ref[cols, :] = block.T

    for t in range(4):
        vt_ref[t * 128 : (t + 1) * 128, :] = start_ref[:, t * 128 : (t + 1) * 128].T

    for s in range(SLOTS):
        rs_ref[s : s + 1, :] = rt_ref[pl.ds(send_ref[0, s], 1), :]
    rs = rs_ref[...]
    lane = lax.broadcasted_iota(jnp.int32, (SLOTS, 128), 1).astype(F32)
    slot = lax.broadcasted_iota(jnp.int32, (SLOTS, 1), 0)
    expect = (ENDS + jnp.bitwise_xor(slot, BND)).astype(F32)
    used = rs[:, 64:65] == expect
    hot = jnp.where(jnp.logical_and(rs[:, 65:66] == lane, used), 1.0, 0.0).astype(BF16)
    hot_wide = jnp.concatenate([hot, hot], axis=1)
    none = jnp.zeros_like(hot)
    hot_pair = jnp.concatenate(
        [jnp.concatenate([hot, none], axis=1), jnp.concatenate([none, hot], axis=1)], axis=0
    )
    hot_tall = jnp.concatenate([hot_pair, hot_pair], axis=0)
    same = dot_nt(hot_pair, hot_pair).astype(BF16)
    same_wide = jnp.concatenate([same, same], axis=1)

    sub = lax.broadcasted_iota(jnp.int32, (128, 128), 0).astype(F32)
    rhl = []
    kk_rows = []
    for k in range(DEG):
        rk = rt_ref[pl.ds(k, NODE_DEV, stride=DEG), :].T
        rk_ref[k] = rk[0:64, :]
        p = rk[64:65, :]
        node = jnp.floor((p + 0.5) * (1.0 / DEG))
        kk_rows.append(p - DEG * node)
        one = jnp.where(sub == node, 1.0, 0.0).astype(BF16)
        ss_ref[0:128, k * 128 : (k + 1) * 128] = one
        ss_ref[128:256, k * 128 : (k + 1) * 128] = one
        hi, lo = split_two(rk[0:64, :])
        rhl.append(jnp.concatenate([hi, lo], axis=1))
    rhl = jnp.concatenate(rhl, axis=0)

    def value_copies(step):
        return [
            pltpu.make_async_remote_copy(
                src_ref=vsend_ref.at[step, pl.ds(k * BND, BND), :],
                dst_ref=vrecv_ref.at[step, pl.ds((k ^ 1) * BND, BND), :],
                send_sem=vsem.at[0, step, k],
                recv_sem=vsem.at[1, step, k ^ 1],
                device_id=neighbours[k],
                device_id_type=MESH,
            )
            for k in range(4)
        ]

    map_copies = [
        pltpu.make_async_remote_copy(
            src_ref=rs_ref.at[pl.ds(k * BND, BND), :],
            dst_ref=rrecv_ref.at[pl.ds((k ^ 1) * BND, BND), :],
            send_sem=rsem.at[0, k],
            recv_sem=rsem.at[1, k ^ 1],
            device_id=neighbours[k],
            device_id_type=MESH,
        )
        for k in range(4)
    ]

    pl.semaphore_wait(barrier, len(near))
    first_copies = value_copies(0)
    for copy in map_copies + first_copies:
        copy.start()
    for peer in x_peers:
        pl.semaphore_signal(xsem, inc=1, device_id=peer, device_id_type=MESH)
    for by in (2, -2):
        pl.semaphore_signal(zsem.at[0], inc=1, device_id=z_shift(by), device_id_type=MESH)

    sub_b = lax.broadcasted_iota(jnp.int32, (8, 128), 0)
    own = [jnp.zeros((8, 128), F32) for _ in range(STALK)]
    for j in range(3):
        far = dot_nn(rhl, ss_ref[:, j * 256 : (j + 1) * 256])
        for h in range(2):
            k = 2 * j + h
            mate_map = far[0:64, h * 128 : (h + 1) * 128]
            for m in range(1, DEG):
                mate_map = jnp.where(
                    kk_rows[k] == float(m),
                    far[m * 64 : (m + 1) * 64, h * 128 : (h + 1) * 128],
                    mate_map,
                )
            for a2 in range(STALK):
                acc = jnp.zeros((8, 128), F32)
                for a in range(STALK):
                    coef = row_bcast(rk_ref[k, a * 8 + a2 : a * 8 + a2 + 1, :])
                    acc = acc + coef * mate_map[a * 8 : (a + 1) * 8, :]
                    own[a2] = own[a2] + coef * rk_ref[k, a * 8 : (a + 1) * 8, :]
                coef_ref[k, a2 * 8 : (a2 + 1) * 8, :] = acc * (-1.0 / RADIUS)
    for a2 in range(STALK):
        coef_ref[DEG, a2 * 8 : (a2 + 1) * 8, :] = (
            own[a2] - jnp.where(sub_b == a2, CENTER, 0.0)
        ) * (1.0 / RADIUS)

    def spread(values_ref):
        hi, lo = split_two(values_ref[...])
        vhl_ref[:, 0:128] = hi
        vhl_ref[:, 128:256] = lo

    def recv_waits(copies):
        for copy in copies:
            copy.wait_recv()

    def local_part(own_ref, out_ref, combine):
        for j in range(3):
            vx_ref[:, j * 256 : (j + 1) * 256] = dot_nn(
                vhl_ref[...], ss_ref[:, j * 256 : (j + 1) * 256]
            )

        def columns(i, carry):
            acc = [[jnp.zeros((8, 128), F32) for _ in range(2)] for _ in range(STALK)]
            for k in range(DEG + 1):
                for b in range(STALK):
                    vals = []
                    for h in range(2):
                        at = pl.ds(pl.multiple_of(b * COLS + i * 16 + h * 8, 8), 8)
                        if k == DEG:
                            vals.append(own_ref[at, :])
                        else:
                            vals.append(vx_ref[at, k * 128 : (k + 1) * 128])
                    for a2 in range(STALK):
                        coef = row_bcast(coef_ref[k, a2 * 8 + b : a2 * 8 + b + 1, :])
                        for h in range(2):
                            acc[a2][h] = acc[a2][h] + coef * vals[h]
            for a2 in range(STALK):
                for h in range(2):
                    at = pl.ds(pl.multiple_of(a2 * COLS + i * 16 + h * 8, 8), 8)
                    out_ref[at, :] = combine(acc[a2][h], at)
            return carry

        lax.fori_loop(0, 4, columns, 0)

    half = COLS // 2

    def remote_part(step):
        if step == 0:
            per_tile, stride = 2, COLS
            pairs = [vrecv_ref[0, :, t * 128 : (t + 1) * 128] for t in range(4)]
            pairs = [(block, pltpu.roll(block, 128 - half, 1)) for block in pairs]
        else:
            per_tile, stride = 4, half
            pairs = [
                (
                    vrecv_ref[1, :, t * 128 : (t + 1) * 128],
                    vrecv_ref[1, :, 256 + t * 128 : 256 + (t + 1) * 128],
                )
                for t in range(2)
            ]
        turned = [jnp.concatenate(pair, axis=0).T for pair in pairs]
        for cg in range(half // 8):
            acc = [jnp.zeros((8, 128), F32) for _ in range(STALK)]
            for b in range(STALK):
                row = (b % per_tile) * stride + cg * 8
                val = turned[b // per_tile][row : row + 8, :]
                for a2 in range(STALK):
                    coef = row_bcast(ms_ref[a2 * 8 + b : a2 * 8 + b + 1, :])
                    acc[a2] = acc[a2] + coef * val
            for a2 in range(STALK):
                at = slice(a2 * half + cg * 8, a2 * half + cg * 8 + 8)
                hi = acc[a2].astype(BF16).astype(F32)
                cpack_ref[at, 0:128] = hi
                cpack_ref[at, 128:256] = acc[a2] - hi
        return cpack_ref[...].astype(BF16)

    def add_remote(out_ref, packed_slots, scale):
        sums = dot_nn(packed_slots, hot_tall)
        for a2 in range(STALK):
            for h in range(2):
                at = slice(a2 * COLS + h * half, a2 * COLS + (h + 1) * half)
                part = sums[a2 * half : (a2 + 1) * half, h * 128 : (h + 1) * 128]
                out_ref[at, :] = out_ref[at, :] + scale * part

    spread(vt_ref)
    local_part(vt_ref, t_ref, lambda acc, at: acc)
    hi, lo = split_two(t_ref[...])
    both = jnp.concatenate([hi, lo], axis=1)
    by_half = jnp.concatenate(
        [
            both[a * COLS + h * half : a * COLS + (h + 1) * half, :]
            for h in range(2)
            for a in range(STALK)
        ],
        axis=0,
    )
    vsend_ref[1] = dot_nt(hot_wide, by_half)

    recv_waits(map_copies)
    far_maps = jnp.concatenate([rrecv_ref[...], rrecv_ref[...]], axis=0).T
    own_maps = jnp.concatenate([rs, rs], axis=0).T
    for a2 in range(STALK):
        acc = jnp.zeros((8, 128), F32)
        for a in range(STALK):
            acc = acc + row_bcast(own_maps[a * 8 + a2 : a * 8 + a2 + 1, :]) * (
                far_maps[a * 8 : (a + 1) * 8, :]
            )
        ms_ref[a2 * 8 : (a2 + 1) * 8, :] = acc * (-1.0 / RADIUS)
    recv_waits(first_copies)
    packed_far = remote_part(0)
    far_rows = dot_nt(same_wide, packed_far)
    vsend_ref[1, :, 0:256] = vsend_ref[1, :, 0:256] + far_rows[0:64, :]
    vsend_ref[1, :, 256:512] = vsend_ref[1, :, 256:512] + far_rows[64:128, :]
    second_copies = value_copies(1)
    for copy in second_copies:
        copy.start()

    add_remote(t_ref, packed_far, 1.0)
    spread(t_ref)
    pl.semaphore_wait(zsem.at[0], 2)
    for by in (4, -4):
        pl.semaphore_signal(zsem.at[1], inc=1, device_id=z_shift(by), device_id_type=MESH)
    local_part(t_ref, vt_ref, lambda acc, at: 2.0 * acc - vt_ref[at, :])
    recv_waits(second_copies)
    add_remote(vt_ref, remote_part(1), 2.0)

    spread(vt_ref)
    tall = jnp.concatenate(
        [
            jnp.concatenate(
                [vhl_ref[a * COLS : (a + 1) * COLS, h * 128 : (h + 1) * 128] for a in range(STALK)],
                axis=1,
            )
            for h in range(2)
        ],
        axis=0,
    )
    prod = dot_nt(tall, tall)
    halves = prod[0:64, :] + prod[64:128, :]
    both = halves + pltpu.roll(halves, 64, 1)
    lane32 = lax.broadcasted_iota(jnp.int32, (32, 128), 1)
    packed = jnp.where(lane32 < 64, both[0:32, :], both[32:64, :])
    share = 32 // PLANE_DOM
    for i in range(PLANE_DOM):
        gsl_ref[i] = packed[i * share : (i + 1) * share, :]

    pl.semaphore_wait(xsem, len(x_peers))
    chips_x = PLANE_DOM // 2
    x, c = mine // 2, lax.rem(mine, 2)

    def ring(step, count):
        return min(step, count - step)

    offsets = [
        (dx, dy, dc) for dx in range(chips_x) for dy in range(n_rep) for dc in range(2)
    ][1:]
    offsets.sort(key=lambda o: -(ring(o[0], chips_x) + ring(o[1], n_rep)))

    def slice_of(at_x, at_y, at_c):
        return lax.rem(at_x + 2 * at_y, chips_x) * 2 + at_c

    my_slice = slice_of(x, r, c)

    def plane_peer(dx, dy, dc):
        at_x, at_y, at_c = lax.rem(x + dx, chips_x), lax.rem(r + dy, n_rep), lax.rem(c + dc, 2)
        return slice_of(at_x, at_y, at_c), (base + at_x * 2 + at_c, at_y)

    for offset in offsets:
        to, peer = plane_peer(*offset)
        pltpu.make_async_remote_copy(
            src_ref=gsl_ref.at[to],
            dst_ref=rsbuf_ref.at[q],
            send_sem=arsem.at[0],
            recv_sem=arsem.at[1],
            device_id=peer,
            device_id_type=MESH,
        ).start()
    rsbuf_ref[q] = gsl_ref[my_slice]
    for t in range(4):
        f_ref[:, t * 128 : (t + 1) * 128] = vt_ref[t * 128 : (t + 1) * 128, :].T
    pl.semaphore_wait(zsem.at[1], 2)
    drain(rsbuf_ref, plane - 1, arsem.at[1])

    def total(ref, count):
        rows = [ref[i] for i in range(count)]
        while len(rows) > 1:
            rows = [rows[i] + rows[i + 1] for i in range(0, len(rows) - 1, 2)] + (
                [rows[-1]] if len(rows) % 2 else []
            )
        return rows[0]

    part_sum = total(rsbuf_ref, plane)
    zsend_ref[0] = part_sum
    for by in sorted(range(1, z_count), key=lambda step: -ring(step, z_count)):
        pltpu.make_async_remote_copy(
            src_ref=zsend_ref.at[0],
            dst_ref=zbuf_ref.at[z],
            send_sem=arsem.at[2],
            recv_sem=arsem.at[3],
            device_id=z_shift(by),
            device_id_type=MESH,
        ).start()
    zbuf_ref[z] = part_sum
    drain(zbuf_ref, z_count - 1, arsem.at[3])
    slice_sum = total(zbuf_ref, z_count)
    zsend_ref[1] = slice_sum
    beside = [(dx, dy, dc) for dx, dy in ((1, 0), (-1, 0), (0, -1)) for dc in range(2)]
    for dx, dy, dc in beside + [(0, 0, 1)]:
        pltpu.make_async_remote_copy(
            src_ref=zsend_ref.at[1],
            dst_ref=agbuf_ref.at[my_slice],
            send_sem=arsem.at[4],
            recv_sem=arsem.at[5],
            device_id=plane_peer(dx % chips_x, dy % n_rep, dc)[1],
            device_id_type=MESH,
        ).start()
    agbuf_ref[my_slice] = slice_sum
    drain(agbuf_ref, PLANE_DOM - 1, arsem.at[5])
    for i in range(PLANE_DOM):
        g_ref[i * share : (i + 1) * share, :] = agbuf_ref[i]

    for copies in (map_copies, first_copies, second_copies):
        for copy in copies:
            copy.wait_send()
    drain(rsbuf_ref, plane - 1, arsem.at[0])
    drain(zbuf_ref, z_count - 1, arsem.at[2])
    drain(agbuf_ref, PLANE_DOM - 1, arsem.at[4])


def full8(value):
    return jnp.broadcast_to(value, (8, 128))


def eliminate(work):
    sub = lax.broadcasted_iota(jnp.int32, (8, 128), 0)
    for g in range(8):
        cols = [[full8(work[i][:, g * 8 + j : g * 8 + j + 1]) for i in range(g, 8)] for j in range(8)]
        rows = [full8(work[g][j : j + 1, :]) for j in range(8)]
        block = [[full8(cols[b][0][a : a + 1, :]) for b in range(a + 1)] for a in range(8)]
        mult = [[None] * 8 for _ in range(8)]
        inverse = []
        for j in range(8):
            inverse.append(1.0 / block[j][j])
            for a in range(j + 1, 8):
                mult[a][j] = block[a][j] * inverse[j]
            for a in range(j + 1, 8):
                for b in range(j + 1, a + 1):
                    block[a][b] = block[a][b] - mult[a][j] * block[b][j]
                rows[a] = rows[a] - mult[a][j] * rows[j]
        scaled = [rows[j] * inverse[j] for j in range(8)]
        done = rows[0]
        for j in range(1, 8):
            done = jnp.where(sub == j, rows[j], done)
        work[g] = done
        for i in range(g + 1, 8):
            col = [cols[j][i - g] for j in range(8)]
            for j in range(8):
                for t in range(j):
                    col[j] = col[j] - col[t] * mult[j][t]
            terms = [col[j] * scaled[j] for j in range(8)]
            while len(terms) > 1:
                terms = [terms[t] + terms[t + 1] for t in range(0, len(terms), 2)]
            work[i] = work[i] - terms[0]


def solve_kernel(
    scaling, f_ref, g_ref, basis_hbm, triangle_hbm, basis_ref, triangle_ref, left_ref, sem
):
    g = g_ref[...]
    turned = pltpu.roll(g, 64, 1)
    lane32 = lax.broadcasted_iota(jnp.int32, (32, 128), 1)
    row32 = lax.broadcasted_iota(jnp.int32, (32, 128), 0)
    top = jnp.where(lane32 < 64, g, jnp.where(lane32 - 64 == row32, 1.0, 0.0))
    bottom = jnp.where(lane32 < 64, turned, jnp.where(lane32 - 96 == row32, 1.0, 0.0))
    work = [top[i * 8 : (i + 1) * 8, :] for i in range(4)] + [
        bottom[i * 8 : (i + 1) * 8, :] for i in range(4)
    ]
    for t in range(4):
        fhi, flo = split_two(f_ref[:, t * 128 : (t + 1) * 128])
        left_ref[t * 128 : (t + 1) * 128, 0:128] = fhi
        left_ref[t * 128 : (t + 1) * 128, 128:256] = flo
    eliminate(work)
    sub = lax.broadcasted_iota(jnp.int32, (8, 128), 0)
    lane = lax.broadcasted_iota(jnp.int32, (8, 128), 1)
    rows_out = []
    for i in range(8):
        diag = jnp.sum(jnp.where(lane == sub + 8 * i, work[i], 0.0), axis=1, keepdims=True)
        rows_out.append(work[i] * lax.rsqrt(diag))
    full = jnp.concatenate(rows_out, axis=0)
    lane64 = lax.broadcasted_iota(jnp.int32, (COLS, 128), 1)
    row64 = lax.broadcasted_iota(jnp.int32, (COLS, 128), 0)
    triangle_ref[...] = jnp.where(lane64 >= row64, full * (1.0 / scaling), 0.0)[:, 0:COLS]
    copies = [pltpu.make_async_copy(triangle_ref, triangle_hbm, sem.at[4])]
    copies[0].start()
    full = full * scaling
    block = jnp.concatenate(
        [
            jnp.where(lane64 < 64, pltpu.roll(full, 64, 1), 0.0),
            jnp.where(lane64 < 64, 0.0, full),
        ],
        axis=0,
    )
    bhi, blo = split_two(block)
    right = jnp.concatenate(
        [
            jnp.concatenate([bhi, bhi], axis=1),
            jnp.concatenate([blo, jnp.zeros_like(blo)], axis=1),
        ],
        axis=0,
    )
    for t in range(4):
        both = dot_nt(left_ref[t * 128 : (t + 1) * 128, :], right)
        basis_ref[t] = both[:, 0:128] + both[:, 128:256]
        copy = pltpu.make_async_copy(
            basis_ref.at[t], basis_hbm.at[:, pl.ds(t * 128, 128)], sem.at[t]
        )
        copy.start()
        copies.append(copy)
    for copy in copies:
        copy.wait()


def local(n_dom, n_rep, start_block, restriction_maps, send_rows, partner):
    z_count = n_dom // PLANE_DOM
    plane = PLANE_DOM * n_rep
    share = 32 // PLANE_DOM
    vmem = pl.BlockSpec(memory_space=pltpu.VMEM)
    hbm = pl.BlockSpec(memory_space=pltpu.HBM)
    inputs = [
        pltpu.with_memory_space_constraint(value, pltpu.HBM)
        for value in (start_block, restriction_maps, send_rows, partner)
    ]
    f_rows, gram = pl.pallas_call(
        functools.partial(filter_kernel, n_dom, n_rep),
        out_shape=[
            pltpu.VMEM((NODE_DEV, WIDE), F32),
            pltpu.VMEM((32, 128), F32),
        ],
        in_specs=[hbm, hbm, hbm, hbm],
        out_specs=[vmem, vmem],
        scratch_shapes=[
            pltpu.VMEM((NODE_DEV, WIDE), F32),
            pltpu.VMEM((STALK, STALK, ENDS), F32),
            pltpu.SMEM((1, SLOTS), jnp.int32),
            pltpu.VMEM((ENDS,), jnp.int32),
            pltpu.VMEM((ENDS, 128), F32),
            pltpu.VMEM((DEG, 64, 128), F32),
            pltpu.VMEM((DEG + 1, 64, 128), F32),
            pltpu.VMEM((256, ENDS), BF16),
            pltpu.VMEM((WIDE, 128), F32),
            pltpu.VMEM((WIDE, 256), BF16),
            pltpu.VMEM((WIDE, ENDS), F32),
            pltpu.VMEM((WIDE, 128), F32),
            pltpu.VMEM((SLOTS, 128), F32),
            pltpu.VMEM((64, 128), F32),
            pltpu.VMEM((2, SLOTS, WIDE), F32),
            pltpu.VMEM((SLOTS, 128), F32),
            pltpu.VMEM((2, SLOTS, WIDE), F32),
            pltpu.VMEM((WIDE // 2, 256), F32),
            pltpu.VMEM((PLANE_DOM, share, 128), F32),
            pltpu.VMEM((plane, share, 128), F32),
            pltpu.VMEM((2, share, 128), F32),
            pltpu.VMEM((z_count, share, 128), F32),
            pltpu.VMEM((PLANE_DOM, share, 128), F32),
            pltpu.SemaphoreType.DMA((2, 4)),
            pltpu.SemaphoreType.DMA((2, 2, 4)),
            pltpu.SemaphoreType.DMA((6,)),
            pltpu.SemaphoreType.DMA((4,)),
            pltpu.SemaphoreType.REGULAR,
            pltpu.SemaphoreType.REGULAR((2,)),
        ],
        compiler_params=pltpu.CompilerParams(
            collective_id=0, has_side_effects=True, vmem_limit_bytes=40 * 1024 * 1024
        ),
        name="filter_and_gram",
    )(*inputs)
    scaling = math.sqrt(NODE_DEV * STALK * n_dom * n_rep)
    return pl.pallas_call(
        functools.partial(solve_kernel, scaling),
        out_shape=[
            jax.ShapeDtypeStruct((NODE_DEV, WIDE), F32),
            jax.ShapeDtypeStruct((COLS, COLS), F32),
        ],
        in_specs=[vmem, vmem],
        out_specs=[hbm, hbm],
        scratch_shapes=[
            pltpu.VMEM((4, NODE_DEV, 128), F32),
            pltpu.VMEM((COLS, COLS), F32),
            pltpu.VMEM((4 * NODE_DEV, 256), BF16),
            pltpu.SemaphoreType.DMA((5,)),
        ],
        compiler_params=pltpu.CompilerParams(vmem_limit_bytes=16 * 1024 * 1024),
        name="factor_and_solve",
    )(f_rows, gram)


def solution(mesh):
    n_dom, n_rep = mesh.shape["dom"], mesh.shape["rep"]
    in_specs = (
        P(("dom", "rep"), None),
        P(None, None, ("dom", "rep")),
        P(("dom", "rep"), None),
        P(("dom", "rep")),
    )
    out_specs = (P(("dom", "rep"), None), P())
    return jax.shard_map(
        functools.partial(local, n_dom, n_rep),
        mesh=mesh,
        in_specs=in_specs,
        out_specs=out_specs,
        check_vma=False,
    )
```

```python
import functools
import math

import jax
import jax.numpy as jnp
from jax import lax
from jax.experimental import pallas as pl
from jax.experimental.pallas import tpu as pltpu
from jax.sharding import PartitionSpec as P

MESH = pl.DeviceIdType.MESH
F32 = jnp.float32
BF16 = jnp.bfloat16

STALK = 8
COLS = 64
DEG = 6
NODE_DEV = 128
ENDS = NODE_DEV * DEG
BND = 16
SLOTS = 4 * BND
WIDE = STALK * COLS
PLANE_DOM = 8
CENTER = 21.0
RADIUS = 15.0


def split_two(x):
    hi = x.astype(BF16)
    lo = (x - hi.astype(F32)).astype(BF16)
    return hi, lo


def dot_nn(a, b):
    return lax.dot_general(a, b, (((1,), (0,)), ((), ())), preferred_element_type=F32)


def dot_nt(a, b):
    return lax.dot_general(a, b, (((1,), (1,)), ((), ())), preferred_element_type=F32)


def row_bcast(row):
    return jnp.broadcast_to(row, (8, row.shape[1]))


def drain(ref, count, sem):
    pltpu.make_async_copy(ref.at[pl.ds(0, count)], ref.at[pl.ds(0, count)], sem).wait()


def filter_kernel(
    n_dom,
    n_rep,
    start_hbm,
    maps_hbm,
    send_hbm,
    partner_hbm,
    f_ref,
    g_ref,
    start_ref,
    maps_ref,
    send_ref,
    partner_ref,
    rt_ref,
    rk_ref,
    coef_ref,
    ss_ref,
    vt_ref,
    vhl_ref,
    vx_ref,
    t_ref,
    rs_ref,
    ms_ref,
    vsend_ref,
    rrecv_ref,
    vrecv_ref,
    cpack_ref,
    tall_ref,
    gsl_ref,
    rsbuf_ref,
    zsend_ref,
    zbuf_ref,
    agbuf_ref,
    rsem,
    vsem,
    arsem,
    insem,
    xsem,
    zsem,
):
    d = lax.axis_index("dom")
    r = lax.axis_index("rep")
    z_count = n_dom // PLANE_DOM
    plane = PLANE_DOM * n_rep
    z = d // PLANE_DOM
    base = z * PLANE_DOM
    q = (d - base) * n_rep + r

    up = lax.rem(d + 1, n_dom)
    down = lax.rem(d + n_dom - 1, n_dom)
    nxt = lax.rem(r + 1, n_rep)
    prv = lax.rem(r + n_rep - 1, n_rep)
    neighbours = ((up, r), (down, r), (d, nxt), (d, prv))

    loads = [
        pltpu.make_async_copy(src, dst, insem.at[i])
        for i, (src, dst) in enumerate(
            (
                (send_hbm, send_ref),
                (start_hbm, start_ref),
                (maps_hbm, maps_ref),
                (partner_hbm, partner_ref),
            )
        )
    ]
    mine = d - base
    other_core = d + 1 - 2 * lax.rem(d, 2)
    x_peers = [(base + lax.rem(mine + 2 * i, PLANE_DOM), r) for i in range(1, PLANE_DOM // 2)]
    near = [(up, r), (down, r)]

    def z_shift(by):
        return (lax.rem(z + z_count + by, z_count) * PLANE_DOM + mine, r)

    near += [z_shift(by) for by in (2, -2)]
    for i in sorted(range(1, n_rep), key=lambda i: -min(i, n_rep - i)):
        turn = lax.rem(r + i, n_rep)
        near += [(d, turn), (other_core, turn)]
    near += [
        (base + lax.rem(mine + i, PLANE_DOM), r)
        for i in sorted(range(1, PLANE_DOM), key=lambda i: -min(i, PLANE_DOM - i))
    ]
    near += [z_shift(by) for by in (1, -1)]
    barrier = pltpu.get_barrier_semaphore()
    for peer in near:
        pl.semaphore_signal(barrier, inc=1, device_id=peer, device_id_type=MESH)

    for load in loads:
        load.start()

    loads[0].wait()
    loads[1].wait()
    for s in range(SLOTS):
        node = lax.div(send_ref[0, s], DEG)
        vsend_ref[0, s : s + 1, :] = start_ref[pl.ds(node, 1), :]
    loads[2].wait()
    loads[3].wait()

    part = jnp.broadcast_to(partner_ref[...].reshape(1, ENDS).astype(F32), (8, ENDS))
    end_id = lax.broadcasted_iota(jnp.int32, (8, ENDS), 1).astype(F32)
    node_id = jnp.floor((end_id + 0.5) * (1.0 / DEG))
    sub8 = lax.broadcasted_iota(jnp.int32, (8, ENDS), 0)
    extra = jnp.where(sub8 == 0, part, node_id)
    for t in range(DEG):
        cols = slice(t * 128, (t + 1) * 128)
        block = jnp.concatenate(
            [maps_ref[:, :, cols].reshape(64, 128), extra[:, cols], jnp.zeros((56, 128), F32)], axis=0
        )
        rt_ref[cols, :] = block.T

    for t in range(4):
        vt_ref[t * 128 : (t + 1) * 128, :] = start_ref[:, t * 128 : (t + 1) * 128].T

    for s in range(SLOTS):
        rs_ref[s : s + 1, :] = rt_ref[pl.ds(send_ref[0, s], 1), :]
    rs = rs_ref[...]
    lane = lax.broadcasted_iota(jnp.int32, (SLOTS, 128), 1).astype(F32)
    slot = lax.broadcasted_iota(jnp.int32, (SLOTS, 1), 0)
    expect = (ENDS + jnp.bitwise_xor(slot, BND)).astype(F32)
    used = rs[:, 64:65] == expect
    hot = jnp.where(jnp.logical_and(rs[:, 65:66] == lane, used), 1.0, 0.0).astype(BF16)
    hot_wide = jnp.concatenate([hot, hot], axis=1)
    none = jnp.zeros_like(hot)
    hot_pair = jnp.concatenate(
        [jnp.concatenate([hot, none], axis=1), jnp.concatenate([none, hot], axis=1)], axis=0
    )
    hot_tall = jnp.concatenate([hot_pair, hot_pair], axis=0)
    same = dot_nt(hot_pair, hot_pair).astype(BF16)
    same_wide = jnp.concatenate([same, same], axis=1)

    sub = lax.broadcasted_iota(jnp.int32, (128, 128), 0).astype(F32)
    rhl = []
    kk_rows = []
    for k in range(DEG):
        rk = rt_ref[pl.ds(k, NODE_DEV, stride=DEG), :].T
        rk_ref[k] = rk[0:64, :]
        p = rk[64:65, :]
        node = jnp.floor((p + 0.5) * (1.0 / DEG))
        kk_rows.append(p - DEG * node)
        one = jnp.where(sub == node, 1.0, 0.0).astype(BF16)
        ss_ref[0:128, k * 128 : (k + 1) * 128] = one
        ss_ref[128:256, k * 128 : (k + 1) * 128] = one
        hi, lo = split_two(rk[0:64, :])
        rhl.append(jnp.concatenate([hi, lo], axis=1))
    rhl = jnp.concatenate(rhl, axis=0)

    def value_copies(step):
        return [
            pltpu.make_async_remote_copy(
                src_ref=vsend_ref.at[step, pl.ds(k * BND, BND), :],
                dst_ref=vrecv_ref.at[step, pl.ds((k ^ 1) * BND, BND), :],
                send_sem=vsem.at[0, step, k],
                recv_sem=vsem.at[1, step, k ^ 1],
                device_id=neighbours[k],
                device_id_type=MESH,
            )
            for k in range(4)
        ]

    map_copies = [
        pltpu.make_async_remote_copy(
            src_ref=rs_ref.at[pl.ds(k * BND, BND), :],
            dst_ref=rrecv_ref.at[pl.ds((k ^ 1) * BND, BND), :],
            send_sem=rsem.at[0, k],
            recv_sem=rsem.at[1, k ^ 1],
            device_id=neighbours[k],
            device_id_type=MESH,
        )
        for k in range(4)
    ]

    pl.semaphore_wait(barrier, len(near))
    first_copies = value_copies(0)
    for copy in map_copies + first_copies:
        copy.start()
    for peer in x_peers:
        pl.semaphore_signal(xsem, inc=1, device_id=peer, device_id_type=MESH)
    for by in (2, -2):
        pl.semaphore_signal(zsem.at[0], inc=1, device_id=z_shift(by), device_id_type=MESH)

    sub_b = lax.broadcasted_iota(jnp.int32, (8, 128), 0)
    own = [jnp.zeros((8, 128), F32) for _ in range(STALK)]
    for j in range(3):
        far = dot_nn(rhl, ss_ref[:, j * 256 : (j + 1) * 256])
        for h in range(2):
            k = 2 * j + h
            mate_map = far[0:64, h * 128 : (h + 1) * 128]
            for m in range(1, DEG):
                mate_map = jnp.where(
                    kk_rows[k] == float(m),
                    far[m * 64 : (m + 1) * 64, h * 128 : (h + 1) * 128],
                    mate_map,
                )
            for a2 in range(STALK):
                acc = jnp.zeros((8, 128), F32)
                for a in range(STALK):
                    coef = row_bcast(rk_ref[k, a * 8 + a2 : a * 8 + a2 + 1, :])
                    acc = acc + coef * mate_map[a * 8 : (a + 1) * 8, :]
                    own[a2] = own[a2] + coef * rk_ref[k, a * 8 : (a + 1) * 8, :]
                coef_ref[k, a2 * 8 : (a2 + 1) * 8, :] = acc * (-1.0 / RADIUS)
    for a2 in range(STALK):
        coef_ref[DEG, a2 * 8 : (a2 + 1) * 8, :] = (
            own[a2] - jnp.where(sub_b == a2, CENTER, 0.0)
        ) * (1.0 / RADIUS)

    def spread(values_ref):
        hi, lo = split_two(values_ref[...])
        vhl_ref[:, 0:128] = hi
        vhl_ref[:, 128:256] = lo

    def recv_waits(copies):
        for copy in copies:
            copy.wait_recv()

    def local_part(own_ref, out_ref, combine):
        for j in range(3):
            vx_ref[:, j * 256 : (j + 1) * 256] = dot_nn(
                vhl_ref[...], ss_ref[:, j * 256 : (j + 1) * 256]
            )

        def columns(i, carry):
            acc = [[jnp.zeros((8, 128), F32) for _ in range(2)] for _ in range(STALK)]
            for k in range(DEG + 1):
                for b in range(STALK):
                    vals = []
                    for h in range(2):
                        at = pl.ds(pl.multiple_of(b * COLS + i * 16 + h * 8, 8), 8)
                        if k == DEG:
                            vals.append(own_ref[at, :])
                        else:
                            vals.append(vx_ref[at, k * 128 : (k + 1) * 128])
                    for a2 in range(STALK):
                        coef = row_bcast(coef_ref[k, a2 * 8 + b : a2 * 8 + b + 1, :])
                        for h in range(2):
                            acc[a2][h] = acc[a2][h] + coef * vals[h]
            for a2 in range(STALK):
                for h in range(2):
                    at = pl.ds(pl.multiple_of(a2 * COLS + i * 16 + h * 8, 8), 8)
                    out_ref[at, :] = combine(acc[a2][h], at)
            return carry

        lax.fori_loop(0, 4, columns, 0)

    half = COLS // 2

    def remote_part(step):
        if step == 0:
            per_tile, stride = 2, COLS
            pairs = [vrecv_ref[0, :, t * 128 : (t + 1) * 128] for t in range(4)]
            pairs = [(block, pltpu.roll(block, 128 - half, 1)) for block in pairs]
        else:
            per_tile, stride = 4, half
            pairs = [
                (
                    vrecv_ref[1, :, t * 128 : (t + 1) * 128],
                    vrecv_ref[1, :, 256 + t * 128 : 256 + (t + 1) * 128],
                )
                for t in range(2)
            ]
        turned = [jnp.concatenate(pair, axis=0).T for pair in pairs]
        for cg in range(half // 8):
            acc = [jnp.zeros((8, 128), F32) for _ in range(STALK)]
            for b in range(STALK):
                row = (b % per_tile) * stride + cg * 8
                val = turned[b // per_tile][row : row + 8, :]
                for a2 in range(STALK):
                    coef = row_bcast(ms_ref[a2 * 8 + b : a2 * 8 + b + 1, :])
                    acc[a2] = acc[a2] + coef * val
            for a2 in range(STALK):
                at = slice(a2 * half + cg * 8, a2 * half + cg * 8 + 8)
                hi = acc[a2].astype(BF16).astype(F32)
                cpack_ref[at, 0:128] = hi
                cpack_ref[at, 128:256] = acc[a2] - hi
        return cpack_ref[...].astype(BF16)

    def add_remote(out_ref, packed_slots, scale):
        sums = dot_nn(packed_slots, hot_tall)
        for a2 in range(STALK):
            for h in range(2):
                at = slice(a2 * COLS + h * half, a2 * COLS + (h + 1) * half)
                part = sums[a2 * half : (a2 + 1) * half, h * 128 : (h + 1) * 128]
                out_ref[at, :] = out_ref[at, :] + scale * part

    spread(vt_ref)
    local_part(vt_ref, t_ref, lambda acc, at: acc)
    hi, lo = split_two(t_ref[...])
    both = jnp.concatenate([hi, lo], axis=1)
    by_half = jnp.concatenate(
        [
            both[a * COLS + h * half : a * COLS + (h + 1) * half, :]
            for h in range(2)
            for a in range(STALK)
        ],
        axis=0,
    )
    vsend_ref[1] = dot_nt(hot_wide, by_half)

    recv_waits(map_copies)
    far_maps = jnp.concatenate([rrecv_ref[...], rrecv_ref[...]], axis=0).T
    own_maps = jnp.concatenate([rs, rs], axis=0).T
    for a2 in range(STALK):
        acc = jnp.zeros((8, 128), F32)
        for a in range(STALK):
            acc = acc + row_bcast(own_maps[a * 8 + a2 : a * 8 + a2 + 1, :]) * (
                far_maps[a * 8 : (a + 1) * 8, :]
            )
        ms_ref[a2 * 8 : (a2 + 1) * 8, :] = acc * (-1.0 / RADIUS)
    recv_waits(first_copies)
    packed_far = remote_part(0)
    far_rows = dot_nt(same_wide, packed_far)
    vsend_ref[1, :, 0:256] = vsend_ref[1, :, 0:256] + far_rows[0:64, :]
    vsend_ref[1, :, 256:512] = vsend_ref[1, :, 256:512] + far_rows[64:128, :]
    second_copies = value_copies(1)
    for copy in second_copies:
        copy.start()

    add_remote(t_ref, packed_far, 1.0)
    spread(t_ref)
    pl.semaphore_wait(zsem.at[0], 2)
    for by in (4, -4):
        pl.semaphore_signal(zsem.at[1], inc=1, device_id=z_shift(by), device_id_type=MESH)
    local_part(t_ref, vt_ref, lambda acc, at: 2.0 * acc - vt_ref[at, :])
    recv_waits(second_copies)
    far_sums = dot_nn(remote_part(1), hot_tall)
    for a2 in range(STALK):
        for h in range(2):
            at = slice(a2 * COLS + h * half, a2 * COLS + (h + 1) * half)
            part = far_sums[a2 * half : (a2 + 1) * half, h * 128 : (h + 1) * 128]
            value = vt_ref[at, :] + 2.0 * part
            vt_ref[at, :] = value
            hi, lo = split_two(value)
            lanes = slice(a2 * 128, (a2 + 1) * 128)
            tall_ref[h * half : (h + 1) * half, lanes] = hi
            tall_ref[COLS + h * half : COLS + (h + 1) * half, lanes] = lo
    tall = tall_ref[...]
    prod = dot_nt(tall, tall)
    halves = prod[0:64, :] + prod[64:128, :]
    both = halves + pltpu.roll(halves, 64, 1)
    lane32 = lax.broadcasted_iota(jnp.int32, (32, 128), 1)
    packed = jnp.where(lane32 < 64, both[0:32, :], both[32:64, :])
    share = 32 // PLANE_DOM
    for i in range(PLANE_DOM):
        gsl_ref[i] = packed[i * share : (i + 1) * share, :]

    pl.semaphore_wait(xsem, len(x_peers))
    chips_x = PLANE_DOM // 2
    x, c = mine // 2, lax.rem(mine, 2)

    def ring(step, count):
        return min(step, count - step)

    offsets = [
        (dx, dy, dc) for dx in range(chips_x) for dy in range(n_rep) for dc in range(2)
    ][1:]
    offsets.sort(key=lambda o: -(ring(o[0], chips_x) + ring(o[1], n_rep)))

    def slice_of(at_x, at_y, at_c):
        return lax.rem(at_x + 2 * at_y, chips_x) * 2 + at_c

    my_slice = slice_of(x, r, c)

    def plane_peer(dx, dy, dc):
        at_x, at_y, at_c = lax.rem(x + dx, chips_x), lax.rem(r + dy, n_rep), lax.rem(c + dc, 2)
        return slice_of(at_x, at_y, at_c), (base + at_x * 2 + at_c, at_y)

    for offset in offsets:
        to, peer = plane_peer(*offset)
        pltpu.make_async_remote_copy(
            src_ref=gsl_ref.at[to],
            dst_ref=rsbuf_ref.at[q],
            send_sem=arsem.at[0],
            recv_sem=arsem.at[1],
            device_id=peer,
            device_id_type=MESH,
        ).start()
    rsbuf_ref[q] = gsl_ref[my_slice]
    for t in range(4):
        f_ref[:, t * 128 : (t + 1) * 128] = vt_ref[t * 128 : (t + 1) * 128, :].T
    pl.semaphore_wait(zsem.at[1], 2)
    drain(rsbuf_ref, plane - 1, arsem.at[1])

    def total(ref, count):
        rows = [ref[i] for i in range(count)]
        while len(rows) > 1:
            rows = [rows[i] + rows[i + 1] for i in range(0, len(rows) - 1, 2)] + (
                [rows[-1]] if len(rows) % 2 else []
            )
        return rows[0]

    part_sum = total(rsbuf_ref, plane)
    zsend_ref[0] = part_sum
    for by in sorted(range(1, z_count), key=lambda step: -ring(step, z_count)):
        pltpu.make_async_remote_copy(
            src_ref=zsend_ref.at[0],
            dst_ref=zbuf_ref.at[z],
            send_sem=arsem.at[2],
            recv_sem=arsem.at[3],
            device_id=z_shift(by),
            device_id_type=MESH,
        ).start()
    zbuf_ref[z] = part_sum
    drain(zbuf_ref, z_count - 1, arsem.at[3])
    slice_sum = total(zbuf_ref, z_count)
    zsend_ref[1] = slice_sum
    beside = [(dx, dy, dc) for dx, dy in ((1, 0), (-1, 0), (0, -1)) for dc in range(2)]
    for dx, dy, dc in beside + [(0, 0, 1)]:
        pltpu.make_async_remote_copy(
            src_ref=zsend_ref.at[1],
            dst_ref=agbuf_ref.at[my_slice],
            send_sem=arsem.at[4],
            recv_sem=arsem.at[5],
            device_id=plane_peer(dx % chips_x, dy % n_rep, dc)[1],
            device_id_type=MESH,
        ).start()
    agbuf_ref[my_slice] = slice_sum
    drain(agbuf_ref, PLANE_DOM - 1, arsem.at[5])
    for i in range(PLANE_DOM):
        g_ref[i * share : (i + 1) * share, :] = agbuf_ref[i]

    for copies in (map_copies, first_copies, second_copies):
        for copy in copies:
            copy.wait_send()
    drain(rsbuf_ref, plane - 1, arsem.at[0])
    drain(zbuf_ref, z_count - 1, arsem.at[2])
    drain(agbuf_ref, PLANE_DOM - 1, arsem.at[4])


def full8(value):
    return jnp.broadcast_to(value, (8, 128))


def eliminate(work):
    sub = lax.broadcasted_iota(jnp.int32, (8, 128), 0)
    scales = []
    for g in range(8):
        cols = [[full8(work[i][:, g * 8 + j : g * 8 + j + 1]) for i in range(g, 8)] for j in range(8)]
        rows = [full8(work[g][j : j + 1, :]) for j in range(8)]
        block = [[full8(cols[b][0][a : a + 1, :]) for b in range(a + 1)] for a in range(8)]
        mult = [[None] * 8 for _ in range(8)]
        inverse = []
        for j in range(8):
            inverse.append(1.0 / block[j][j])
            for a in range(j + 1, 8):
                mult[a][j] = block[a][j] * inverse[j]
            for a in range(j + 1, 8):
                for b in range(j + 1, a + 1):
                    block[a][b] = block[a][b] - mult[a][j] * block[b][j]
                rows[a] = rows[a] - mult[a][j] * rows[j]
        scaled = [rows[j] * inverse[j] for j in range(8)]
        done, pivots = rows[0], block[0][0]
        for j in range(1, 8):
            done = jnp.where(sub == j, rows[j], done)
            pivots = jnp.where(sub == j, block[j][j], pivots)
        work[g] = done
        scales.append(lax.rsqrt(pivots))
        for i in range(g + 1, 8):
            col = [cols[j][i - g] for j in range(8)]
            for j in range(8):
                for t in range(j):
                    col[j] = col[j] - col[t] * mult[j][t]
            terms = [col[j] * scaled[j] for j in range(8)]
            while len(terms) > 1:
                terms = [terms[t] + terms[t + 1] for t in range(0, len(terms), 2)]
            work[i] = work[i] - terms[0]
    return scales


def solve_kernel(
    scaling, f_ref, g_ref, basis_hbm, triangle_hbm, basis_ref, triangle_ref, left_ref, sem
):
    g = g_ref[...]
    turned = pltpu.roll(g, 64, 1)
    lane32 = lax.broadcasted_iota(jnp.int32, (32, 128), 1)
    row32 = lax.broadcasted_iota(jnp.int32, (32, 128), 0)
    top = jnp.where(lane32 < 64, g, jnp.where(lane32 - 64 == row32, 1.0, 0.0))
    bottom = jnp.where(lane32 < 64, turned, jnp.where(lane32 - 96 == row32, 1.0, 0.0))
    work = [top[i * 8 : (i + 1) * 8, :] for i in range(4)] + [
        bottom[i * 8 : (i + 1) * 8, :] for i in range(4)
    ]
    for t in range(4):
        fhi, flo = split_two(f_ref[:, t * 128 : (t + 1) * 128])
        left_ref[t * 128 : (t + 1) * 128, 0:128] = fhi
        left_ref[t * 128 : (t + 1) * 128, 128:256] = flo
    scales = eliminate(work)
    full = jnp.concatenate([work[i] * scales[i] for i in range(8)], axis=0)
    lane64 = lax.broadcasted_iota(jnp.int32, (COLS, 128), 1)
    row64 = lax.broadcasted_iota(jnp.int32, (COLS, 128), 0)
    triangle_ref[...] = jnp.where(lane64 >= row64, full * (1.0 / scaling), 0.0)[:, 0:COLS]
    copies = [pltpu.make_async_copy(triangle_ref, triangle_hbm, sem.at[4])]
    copies[0].start()
    full = full * scaling
    block = jnp.concatenate(
        [
            jnp.where(lane64 < 64, pltpu.roll(full, 64, 1), 0.0),
            jnp.where(lane64 < 64, 0.0, full),
        ],
        axis=0,
    )
    bhi, blo = split_two(block)
    right = jnp.concatenate(
        [
            jnp.concatenate([bhi, bhi], axis=1),
            jnp.concatenate([blo, jnp.zeros_like(blo)], axis=1),
        ],
        axis=0,
    )
    for t in range(4):
        both = dot_nt(left_ref[t * 128 : (t + 1) * 128, :], right)
        basis_ref[t] = both[:, 0:128] + both[:, 128:256]
        copy = pltpu.make_async_copy(
            basis_ref.at[t], basis_hbm.at[:, pl.ds(t * 128, 128)], sem.at[t]
        )
        copy.start()
        copies.append(copy)
    for copy in copies:
        copy.wait()


def local(n_dom, n_rep, start_block, restriction_maps, send_rows, partner):
    z_count = n_dom // PLANE_DOM
    plane = PLANE_DOM * n_rep
    share = 32 // PLANE_DOM
    vmem = pl.BlockSpec(memory_space=pltpu.VMEM)
    hbm = pl.BlockSpec(memory_space=pltpu.HBM)
    inputs = [
        pltpu.with_memory_space_constraint(value, pltpu.HBM)
        for value in (start_block, restriction_maps, send_rows, partner)
    ]
    f_rows, gram = pl.pallas_call(
        functools.partial(filter_kernel, n_dom, n_rep),
        out_shape=[
            pltpu.VMEM((NODE_DEV, WIDE), F32),
            pltpu.VMEM((32, 128), F32),
        ],
        in_specs=[hbm, hbm, hbm, hbm],
        out_specs=[vmem, vmem],
        scratch_shapes=[
            pltpu.VMEM((NODE_DEV, WIDE), F32),
            pltpu.VMEM((STALK, STALK, ENDS), F32),
            pltpu.SMEM((1, SLOTS), jnp.int32),
            pltpu.VMEM((ENDS,), jnp.int32),
            pltpu.VMEM((ENDS, 128), F32),
            pltpu.VMEM((DEG, 64, 128), F32),
            pltpu.VMEM((DEG + 1, 64, 128), F32),
            pltpu.VMEM((256, ENDS), BF16),
            pltpu.VMEM((WIDE, 128), F32),
            pltpu.VMEM((WIDE, 256), BF16),
            pltpu.VMEM((WIDE, ENDS), F32),
            pltpu.VMEM((WIDE, 128), F32),
            pltpu.VMEM((SLOTS, 128), F32),
            pltpu.VMEM((64, 128), F32),
            pltpu.VMEM((2, SLOTS, WIDE), F32),
            pltpu.VMEM((SLOTS, 128), F32),
            pltpu.VMEM((2, SLOTS, WIDE), F32),
            pltpu.VMEM((WIDE // 2, 256), F32),
            pltpu.VMEM((2 * COLS, STALK * 128), BF16),
            pltpu.VMEM((PLANE_DOM, share, 128), F32),
            pltpu.VMEM((plane, share, 128), F32),
            pltpu.VMEM((2, share, 128), F32),
            pltpu.VMEM((z_count, share, 128), F32),
            pltpu.VMEM((PLANE_DOM, share, 128), F32),
            pltpu.SemaphoreType.DMA((2, 4)),
            pltpu.SemaphoreType.DMA((2, 2, 4)),
            pltpu.SemaphoreType.DMA((6,)),
            pltpu.SemaphoreType.DMA((4,)),
            pltpu.SemaphoreType.REGULAR,
            pltpu.SemaphoreType.REGULAR((2,)),
        ],
        compiler_params=pltpu.CompilerParams(
            collective_id=0, has_side_effects=True, vmem_limit_bytes=40 * 1024 * 1024
        ),
        name="filter_and_gram",
    )(*inputs)
    scaling = math.sqrt(NODE_DEV * STALK * n_dom * n_rep)
    return pl.pallas_call(
        functools.partial(solve_kernel, scaling),
        out_shape=[
            jax.ShapeDtypeStruct((NODE_DEV, WIDE), F32),
            jax.ShapeDtypeStruct((COLS, COLS), F32),
        ],
        in_specs=[vmem, vmem],
        out_specs=[hbm, hbm],
        scratch_shapes=[
            pltpu.VMEM((4, NODE_DEV, 128), F32),
            pltpu.VMEM((COLS, COLS), F32),
            pltpu.VMEM((4 * NODE_DEV, 256), BF16),
            pltpu.SemaphoreType.DMA((5,)),
        ],
        compiler_params=pltpu.CompilerParams(vmem_limit_bytes=16 * 1024 * 1024),
        name="factor_and_solve",
    )(f_rows, gram)


def solution(mesh):
    n_dom, n_rep = mesh.shape["dom"], mesh.shape["rep"]
    in_specs = (
        P(("dom", "rep"), None),
        P(None, None, ("dom", "rep")),
        P(("dom", "rep"), None),
        P(("dom", "rep")),
    )
    out_specs = (P(("dom", "rep"), None), P())
    return jax.shard_map(
        functools.partial(local, n_dom, n_rep),
        mesh=mesh,
        in_specs=in_specs,
        out_specs=out_specs,
        check_vma=False,
    )
```
